512 devices in a mesh: bx: 32 (over z, x_lo), by: 16 (over x_hi, y, core).
Axes of the slice: x: 4 (x_hi: 2, x_lo: 2; x = x_hi * 2 + x_lo), y: 4, z: 16, core: 2. Of those that a mesh axis runs over, the one named last changes fastest.
Arguments:
- blocks: bfloat16 [32, 16, 32, 4096], P('bx', 'by'), as said below
- faces: bfloat16 [32, 16, 32, 4096], P('bx', 'by'), may hold values from -1.1953125 to 1.1953125
- tentative: bfloat16 [32, 16, 32, 4096], P('bx', 'by'), may hold values from -0.75 to 0.75
- aggregate: int32 [32, 16, 32], P('bx', 'by'), may hold values from 0 to 3
- ghost_labels: int32 [32, 16, 24], P('bx', 'by'), may hold values from 0 to 3, as said below
- rhs: float32 [32, 16, 6, 64, 32], P('bx', 'by'), may hold values from -6 to 6
- guess: float32 [32, 16, 6, 64, 32], P('bx', 'by'), may hold values from -6 to 6
- bounds: float32 [2], replicated, as said below
Outputs:
- smoothed: float32 [32, 16, 6, 64, 32], P('bx', 'by')
- coarse_local: float32 [32, 16, 256, 256], P('bx', 'by')
- coarse_ghost: float32 [32, 16, 4, 256, 256], P('bx', 'by')
The draws below stay inside these ranges and needn't reach their ends.
Inputs may be any that keep to these rules, and one draw needn't show every extreme that they name: `ghost_labels`: each entry equals the aggregate number of the neighbouring brick's element across that face, 0 where the brick has no neighbour on that side. `blocks`: every diagonal entry of every block is at least 2. 0 < bounds[0] < bounds[1].
All inputs are finite; a program needn't handle non-finite values.
Results may differ from the reference program's by a relative error of at most 0.0029.
Values may be sent and summed in bfloat16 or wider, within the bound.
No kernel may reach another device: no remote copies, remote signals or barrier semaphores. Data moves between devices by JAX's collectives and lax.ppermute only.
A program may use at most 64 MiB of HBM per device.

```python
import jax
import jax.numpy as jnp
from jax import lax

BLOCK = 64
CB = 64
NAGG = 4
EX = 4
EY = 8
NRHS = 6
BRICKS_X = 32
BRICKS_Y = 16


def label_grid(key):
    return jax.random.randint(key, (BRICKS_X, BRICKS_Y, EX, EY), 0, NAGG, dtype=jnp.int32)


def draw_aggregate(key, part):
    labels = label_grid(key)
    return labels.reshape(BRICKS_X, BRICKS_Y, EX * EY)


def draw_ghost_labels(key, part):
    labels = label_grid(key)
    empty_x = jnp.zeros((1, BRICKS_Y, EY), jnp.int32)
    empty_y = jnp.zeros((BRICKS_X, 1, EX), jnp.int32)
    low_x = jnp.concatenate([empty_x, labels[:-1, :, EX - 1, :]], 0)
    high_x = jnp.concatenate([labels[1:, :, 0, :], empty_x], 0)
    low_y = jnp.concatenate([empty_y, labels[:, :-1, :, EY - 1]], 1)
    high_y = jnp.concatenate([labels[:, 1:, :, 0], empty_y], 1)
    return jnp.concatenate([low_x, high_x, low_y, high_y], 2)


def draw_blocks(key, part):
    key = jax.random.fold_in(key, 11)
    first_key, second_key = jax.random.split(key)
    off_diagonal = 0.08 * jax.random.normal(first_key, (BRICKS_X, BRICKS_Y, EX * EY, BLOCK, BLOCK), jnp.float32)
    diagonal_values = jax.random.uniform(second_key, (BRICKS_X, BRICKS_Y, EX * EY, BLOCK, 1), jnp.float32, 2.0, 4.0)
    identity = jnp.eye(BLOCK, dtype=jnp.float32)
    combined = off_diagonal * (1.0 - identity) + diagonal_values * identity
    return combined.reshape(BRICKS_X, BRICKS_Y, EX * EY, BLOCK * BLOCK).astype(jnp.bfloat16)


def draw_bounds(key, part):
    key = jax.random.fold_in(key, 23)
    first_key, second_key = jax.random.split(key)
    upper_bound = jax.random.uniform(first_key, (), jnp.float32, 2.0, 3.0)
    lower_bound = upper_bound * jax.random.uniform(second_key, (), jnp.float32, 0.05, 0.15)
    return jnp.stack([lower_bound, upper_bound])


def level_of(rng, shape, cuts, smallest, largest):
    factor_of = 1.0
    for position, blocks in cuts:
        draws = jax.random.uniform(jax.random.fold_in(jax.random.fold_in(rng, 6), position), (blocks,), jnp.float32, smallest / len(cuts), largest / len(cuts))
        factor_of = factor_of * jnp.repeat(jnp.exp(draws), shape[position] // blocks).reshape((-1,) + (1,) * (len(shape) - 1 - position))
    return factor_of


def gaussian(own_key, extent, scale, most, shards=(), kind=jnp.bfloat16):
    values = scale * jax.random.normal(own_key, extent, jnp.float32)
    if shards:
        values = values * level_of(own_key, extent, shards, -0.22, 0.18)
    return jnp.clip(values, -most, most).astype(kind)


def setup_inputs(seed: int = 0) -> dict:
    key_of = jax.random.split(jax.random.key(seed), 9)
    return {
        "blocks": draw_blocks(jax.random.fold_in(key_of[8], 71), 0),
        "faces": gaussian(key_of[1], (BRICKS_X, BRICKS_Y, EX * EY, 4 * BLOCK * 16), 0.2, 1.1953125, ((0, 32), (1, 16))),
        "tentative": gaussian(key_of[2], (BRICKS_X, BRICKS_Y, EX * EY, BLOCK * CB), BLOCK ** -0.5, 0.75, ((0, 32), (1, 16))),
        "aggregate": draw_aggregate(jax.random.fold_in(key_of[8], 71), 0),
        "ghost_labels": draw_ghost_labels(jax.random.fold_in(key_of[8], 71), 0),
        "rhs": gaussian(key_of[5], (BRICKS_X, BRICKS_Y, NRHS, BLOCK, EX * EY), 1.0, 6.0, ((0, 32), (1, 16)), jnp.float32),
        "guess": gaussian(key_of[6], (BRICKS_X, BRICKS_Y, NRHS, BLOCK, EX * EY), 1.0, 6.0, ((0, 32), (1, 16)), jnp.float32),
        "bounds": draw_bounds(jax.random.fold_in(key_of[8], 71), 0),
    }


def trace_blocks(prolong):
    dof_cube = prolong.reshape(EX, EY, 4, 4, 4, prolong.shape[-1])
    width = prolong.shape[-1]
    minus_x = dof_cube[:, :, 0].reshape(EX, EY, 16, width)
    plus_x = dof_cube[:, :, 3].reshape(EX, EY, 16, width)
    minus_y = dof_cube[:, :, :, 0].reshape(EX, EY, 16, width)
    plus_y = dof_cube[:, :, :, 3].reshape(EX, EY, 16, width)
    return minus_x, plus_x, minus_y, plus_y


def field_traces(vector_field):
    vectors = vector_field.shape[0]
    dof_cube = vector_field.reshape(vectors, 4, 4, 4, EX, EY)
    minus_x = dof_cube[:, 0].reshape(vectors, 16, EX, EY)
    plus_x = dof_cube[:, 3].reshape(vectors, 16, EX, EY)
    minus_y = dof_cube[:, :, 0].reshape(vectors, 16, EX, EY)
    plus_y = dof_cube[:, :, 3].reshape(vectors, 16, EX, EY)
    return minus_x, plus_x, minus_y, plus_y


def neighbour_rows(traces, edge_rows, axis_x, axis_y):
    minus_x, plus_x, minus_y, plus_y = traces
    low_x, high_x, low_y, high_y = edge_rows
    rows_x = plus_x.shape[axis_x]
    rows_y = plus_y.shape[axis_y]
    from_low_x = jnp.concatenate([jnp.expand_dims(low_x, axis_x), lax.slice_in_dim(plus_x, 0, rows_x - 1, axis=axis_x)], axis_x)
    from_high_x = jnp.concatenate([lax.slice_in_dim(minus_x, 1, rows_x, axis=axis_x), jnp.expand_dims(high_x, axis_x)], axis_x)
    from_low_y = jnp.concatenate([jnp.expand_dims(low_y, axis_y), lax.slice_in_dim(plus_y, 0, rows_y - 1, axis=axis_y)], axis_y)
    from_high_y = jnp.concatenate([lax.slice_in_dim(minus_y, 1, rows_y, axis=axis_y), jnp.expand_dims(high_y, axis_y)], axis_y)
    return jnp.stack([from_low_x, from_high_x, from_low_y, from_high_y])


def galerkin(diag_blocks, couplings, prolong, labels, traces, row_ghosts, label_ghosts):
    elements = EX * EY
    near_rows = neighbour_rows(traces, row_ghosts, 0, 1).reshape(4, elements, 16, CB)
    grid_labels = labels.reshape(EX, EY)
    label_traces = (grid_labels, grid_labels, grid_labels, grid_labels)
    near_labels = neighbour_rows(label_traces, label_ghosts, 0, 1).reshape(4, elements)
    applied = jnp.einsum('epq,eqr->epr', diag_blocks, prolong, preferred_element_type=jnp.float32).astype(jnp.bfloat16)
    w_self = jnp.einsum('epa,epb->eab', prolong, applied, preferred_element_type=jnp.float32)
    coupled = jnp.einsum('efpt,fetr->fepr', couplings, near_rows, preferred_element_type=jnp.float32).astype(jnp.bfloat16)
    w_face = jnp.einsum('epa,fepb->feab', prolong, coupled, preferred_element_type=jnp.float32)
    numbers = jnp.arange(NAGG, dtype=jnp.int32)
    own_onehot = (labels[:, None] == numbers[None, :]).astype(jnp.float32)
    other_onehot = (near_labels[:, :, None] == numbers[None, None, :]).astype(jnp.float32)
    row_index = lax.broadcasted_iota(jnp.int32, (EX, EY), 0).reshape(elements)
    col_index = lax.broadcasted_iota(jnp.int32, (EX, EY), 1).reshape(elements)
    outside = jnp.stack([row_index == 0, row_index == EX - 1, col_index == 0, col_index == EY - 1]).astype(jnp.float32)
    pair_self = own_onehot[:, :, None] * own_onehot[:, None, :]
    pair_face = own_onehot[None, :, :, None] * other_onehot[:, :, None, :]
    local_part = jnp.einsum('eab,epr->apbr', pair_self, w_self, precision=lax.Precision.HIGHEST)
    local_part = local_part + jnp.einsum('feab,fepr->apbr', pair_face * (1.0 - outside)[:, :, None, None], w_face, precision=lax.Precision.HIGHEST)
    ghost_part = jnp.einsum('feab,fepr->fapbr', pair_face * outside[:, :, None, None], w_face, precision=lax.Precision.HIGHEST)
    coarse_width = NAGG * CB
    return local_part.reshape(coarse_width, coarse_width), ghost_part.reshape(4, coarse_width, coarse_width)


def operate_brick(diag_blocks, couplings, vector_field, traces, edge_rows):
    vectors = vector_field.shape[0]
    near_rows = neighbour_rows(traces, edge_rows, 2, 3).reshape(4, vectors, 16, EX * EY)
    own_term = jnp.einsum('epq,nqe->npe', diag_blocks.astype(jnp.float32), vector_field, precision=lax.Precision.HIGHEST)
    face_term = jnp.einsum('efpt,fnte->npe', couplings.astype(jnp.float32), near_rows, precision=lax.Precision.HIGHEST)
    return own_term + face_term


def chebyshev(operate, inverse, rhs_values, guess_values, bounds):
    lower_bound = bounds[0]
    upper_bound = bounds[1]
    centre = 0.5 * (upper_bound + lower_bound)
    half_width = 0.5 * (upper_bound - lower_bound)
    spread = centre / half_width
    factor = 1.0 / spread
    residue = rhs_values - operate(guess_values)
    update = inverse * residue / centre
    answer = guess_values + update
    for sweep_index in range(2):
        residue = residue - operate(update)
        next_factor = 1.0 / (2.0 * spread - factor)
        update = next_factor * factor * update + (2.0 * next_factor / half_width) * inverse * residue
        answer = answer + update
        factor = next_factor
    return answer


def shift_down(array_in, axis):
    empty_row = jnp.zeros_like(lax.slice_in_dim(array_in, 0, 1, axis=axis))
    return jnp.concatenate([empty_row, lax.slice_in_dim(array_in, 0, array_in.shape[axis] - 1, axis=axis)], axis)


def shift_up(array_in, axis):
    empty_row = jnp.zeros_like(lax.slice_in_dim(array_in, 0, 1, axis=axis))
    return jnp.concatenate([lax.slice_in_dim(array_in, 1, array_in.shape[axis], axis=axis), empty_row], axis)


def reference(blocks, faces, tentative, aggregate, ghost_labels, rhs, guess, bounds):
    bricks = BRICKS_X * BRICKS_Y
    elements = EX * EY
    diag_all = blocks.reshape(bricks, elements, BLOCK, BLOCK)
    couple_all = faces.reshape(bricks, elements, 4, BLOCK, 16)
    prolong_all = tentative.reshape(bricks, elements, BLOCK, CB)
    element_grid = tentative.reshape(BRICKS_X, BRICKS_Y, EX, EY, 4, 4, 4, CB)
    plus_x_last = element_grid[:, :, EX - 1, :, 3].reshape(BRICKS_X, BRICKS_Y, EY, 16, CB)
    minus_x_first = element_grid[:, :, 0, :, 0].reshape(BRICKS_X, BRICKS_Y, EY, 16, CB)
    plus_y_last = element_grid[:, :, :, EY - 1, :, 3].reshape(BRICKS_X, BRICKS_Y, EX, 16, CB)
    minus_y_first = element_grid[:, :, :, 0, :, 0].reshape(BRICKS_X, BRICKS_Y, EX, 16, CB)
    low_x = shift_down(plus_x_last, 0).reshape(bricks, EY, 16, CB)
    high_x = shift_up(minus_x_first, 0).reshape(bricks, EY, 16, CB)
    low_y = shift_down(plus_y_last, 1).reshape(bricks, EX, 16, CB)
    high_y = shift_up(minus_y_first, 1).reshape(bricks, EX, 16, CB)

    def one_brick(brick_items):
        diag_b, couple_b, prolong_b, labels_b, lx, hx, ly, hy, glabels = brick_items
        traces = trace_blocks(prolong_b)
        label_ghosts = (glabels[:EY], glabels[EY:2 * EY], glabels[2 * EY:2 * EY + EX], glabels[2 * EY + EX:])
        return galerkin(diag_b, couple_b, prolong_b, labels_b, traces, (lx, hx, ly, hy), label_ghosts)

    local_all, ghost_all = lax.map(one_brick, (diag_all, couple_all, prolong_all, aggregate.reshape(bricks, elements), low_x, high_x, low_y, high_y, ghost_labels.reshape(bricks, 2 * EY + 2 * EX)))
    coarse_local = local_all.reshape(BRICKS_X, BRICKS_Y, NAGG * CB, NAGG * CB)
    coarse_ghost = ghost_all.reshape(BRICKS_X, BRICKS_Y, 4, NAGG * CB, NAGG * CB)

    def operate(vector_field):
        dof_cube = vector_field.reshape(BRICKS_X, BRICKS_Y, NRHS, 4, 4, 4, EX, EY)
        field_plus_x = dof_cube[:, :, :, 3, :, :, EX - 1, :].reshape(BRICKS_X, BRICKS_Y, NRHS, 16, EY)
        field_minus_x = dof_cube[:, :, :, 0, :, :, 0, :].reshape(BRICKS_X, BRICKS_Y, NRHS, 16, EY)
        field_plus_y = dof_cube[:, :, :, :, 3, :, :, EY - 1].reshape(BRICKS_X, BRICKS_Y, NRHS, 16, EX)
        field_minus_y = dof_cube[:, :, :, :, 0, :, :, 0].reshape(BRICKS_X, BRICKS_Y, NRHS, 16, EX)
        edge_low_x = shift_down(field_plus_x, 0).reshape(bricks, NRHS, 16, EY)
        edge_high_x = shift_up(field_minus_x, 0).reshape(bricks, NRHS, 16, EY)
        edge_low_y = shift_down(field_plus_y, 1).reshape(bricks, NRHS, 16, EX)
        edge_high_y = shift_up(field_minus_y, 1).reshape(bricks, NRHS, 16, EX)

        def one_field(brick_items):
            diag_b, couple_b, field_b, lx, hx, ly, hy = brick_items
            return operate_brick(diag_b, couple_b, field_b, field_traces(field_b), (lx, hx, ly, hy))

        result = lax.map(one_field, (diag_all, couple_all, vector_field.reshape(bricks, NRHS, BLOCK, elements), edge_low_x, edge_high_x, edge_low_y, edge_high_y))
        return result.reshape(vector_field.shape)

    diagonal_values = jnp.swapaxes(jnp.diagonal(diag_all, axis1=2, axis2=3), 1, 2).astype(jnp.float32)
    inverse = (1.0 / diagonal_values).reshape(BRICKS_X, BRICKS_Y, 1, BLOCK, elements)
    smoothed = chebyshev(operate, inverse, rhs, guess, bounds)
    return smoothed, coarse_local, coarse_ghost
```

```python
import jax
import jax.numpy as jnp
from jax import lax
from jax.experimental import pallas as pl
from jax.experimental.pallas import tpu as pltpu
from jax.sharding import PartitionSpec as P

EX, EY, NE, NRHS = 4, 8, 32, 6
ROWS = NRHS * NE
F32, BF16 = jnp.float32, jnp.bfloat16
VMEM = pl.BlockSpec(memory_space=pltpu.VMEM)
SMEM = pl.BlockSpec(memory_space=pltpu.SMEM)
NT = (((1,), (1,)), ((), ()))
NN = (((1,), (0,)), ((), ()))


def dot(a, b, dims=NN):
    return lax.dot_general(a, b, dims, preferred_element_type=F32)


def iota(shape, dim):
    return lax.broadcasted_iota(jnp.int32, shape, dim)


def split(x):
    hi = x.astype(BF16)
    return hi, (x - hi.astype(F32)).astype(BF16)


def trace_matrix():
    q, lane = iota((64, 128), 0), iota((64, 128), 1)
    t = lane % 16
    f = lane // 16 - 4
    along_y = 16 * (t // 4) + t % 4
    source = jnp.where(f == 0, 48 + t, jnp.where(f == 1, t, jnp.where(f == 2, along_y + 12, along_y)))
    return (q == jnp.where(f < 0, lane, source)).astype(F32).astype(BF16)


def with_traces(v):
    hi, lo = split(v)
    pick = trace_matrix()
    return dot(hi, pick) + dot(lo, pick)


def pack_field(rows):
    hi, lo = split(rows)
    return jnp.where(
        iota(rows.shape, 1) >= 64, hi.astype(F32), pltpu.roll(lo.astype(F32), 64, 1)
    ).astype(BF16)


def unpack_field(message):
    wide = message.astype(F32)
    return wide + pltpu.roll(wide, 64, 1)


def edges_x(traces, low):
    start = 0 if low else NE - EY
    return jnp.concatenate([traces[n * NE + start : n * NE + start + EY] for n in range(NRHS)], 0)


def field_messages(traces, t_ref):
    t_ref[...] = traces
    pad = jnp.zeros((8, 128), F32)
    return (
        pack_field(edges_x(traces, True)),
        pack_field(edges_x(traces, False)),
        pack_field(jnp.concatenate([t_ref[pl.ds(0, 24, stride=8), :], pad], 0)),
        pack_field(jnp.concatenate([t_ref[pl.ds(7, 24, stride=8), :], pad], 0)),
    )


def parities():
    return lax.axis_index("bx") % 2, lax.axis_index("by") % 2


def swap(even, first, second):
    a, b = first.astype(F32), second.astype(F32)
    return (
        jnp.where(even, a, b).astype(first.dtype),
        jnp.where(even, b, a).astype(first.dtype),
    )


def store_messages(outs, first_row, messages):
    px, py = parities()
    x_low, x_high, y_low, y_high = messages
    x_even, x_odd = swap(px == 0, x_high, x_low)
    y_even, y_odd = swap(py == 0, y_high, y_low)
    for out, value in zip(outs, (x_even, x_odd, y_even, y_odd)):
        out[first_row : first_row + value.shape[0], :] = value


def received(refs, first_row, sizes):
    px, py = parities()
    x_even, x_odd, y_even, y_odd = [
        ref[first_row : first_row + size, :] for ref, size in zip(refs, sizes)
    ]
    x_high, x_low = swap(px == 0, x_even, x_odd)
    y_high, y_low = swap(py == 0, y_even, y_odd)
    return x_low, x_high, y_low, y_high


FIELD_SIZES = (48, 48, 32, 32)
TENT_SIZES = (64, 64, 64, 64)


def pack_kernel(guess, tent, t16, plus_y, minus_y, xe, xo, ye, yo, stage, t32, traces_ref):
    lane = iota((256, 128), 1)
    for k in range(4):
        for ph in range(8):
            chunk = tent[:, (ph * 4 + k) * 128 : (ph * 4 + k + 1) * 128].astype(F32)
            stage[k, pl.ds(ph, NE, stride=8), :] = chunk
    for k in range(4):
        both = stage[k]
        other = pltpu.roll(both, 64, 1)
        t32[pl.ds(2 * k, 256, stride=8), :] = jnp.where(lane < 64, both, other)
        t32[pl.ds(2 * k + 1, 256, stride=8), :] = jnp.where(lane < 64, other, both)
    t16[...] = t32[...].astype(BF16)
    sub = iota((8, 128), 0)
    for e in range(NE):
        plus, minus = [], []
        for h in range(2):
            base = e * 64 + 32 * h
            a, b = t32[base + 8 : base + 16, :], t32[base + 24 : base + 32, :]
            plus.append(jnp.where(sub < 4, pltpu.roll(a, 4, 0), b))
            a, b = t32[base : base + 8, :], t32[base + 16 : base + 24, :]
            minus.append(jnp.where(sub < 4, a, pltpu.roll(b, 4, 0)))
        plus_y[e * 16 : e * 16 + 16, :] = jnp.concatenate(plus, 0).astype(BF16)
        minus_y[e * 16 : e * 16 + 16, :] = jnp.concatenate(minus, 0).astype(BF16)

    lane16 = iota((16, 128), 1)

    def tent_x(first, row):
        parts = []
        for iy in range(4):
            a = (first + iy) * 64 + row
            b = (first + iy + 4) * 64 + row
            parts.append(jnp.where(lane16 < 64, t32[a : a + 16, :], t32[b : b + 16, :]))
        return jnp.concatenate(parts, 0).astype(BF16)

    def tent_y(ref, iy):
        return jnp.concatenate([ref[(8 * ix + iy) * 16 : (8 * ix + iy) * 16 + 16, :] for ix in range(4)], 0)

    fields = field_messages(with_traces(guess[...].reshape(ROWS, 64)), traces_ref)
    tents = (tent_x(0, 0), tent_x(24, 48), tent_y(minus_y, 0), tent_y(plus_y, 7))
    store_messages((xe, xo, ye, yo), 0, tents)
    store_messages((xe, xo, ye, yo), 64, fields)


def prep_kernel(blocks, faces, w, inverse, stage, fstage, w32):
    lane = iota((256, 128), 1)
    lane_e = iota((NE, 128), 1)
    diag = jnp.zeros((NE, 128), F32)
    for k in range(4):
        for ph in range(8):
            c = ph * 4 + k
            chunk = blocks[:, c * 128 : (c + 1) * 128].astype(F32)
            diag = diag + jnp.where((lane_e == 2 * c) | (lane_e == 65 + 2 * c), chunk, 0.0)
            stage[k, pl.ds(ph, NE, stride=8), :] = chunk
    diag = diag + pltpu.roll(diag, 64, 1)
    inverse[...] = 1.0 / diag[:, :64]
    for f in range(4):
        for ph in range(8):
            c = f * 8 + ph
            fstage[f, pl.ds(ph, NE, stride=8), :] = faces[:, c * 128 : (c + 1) * 128].astype(F32)
    folded = jnp.concatenate([fstage[f].astype(BF16) for f in range(4)], 1)
    row, col = iota((512, 128), 0), iota((512, 128), 1)
    face_of, lo_of, t_of = row // 128, (row // 16) % 8, row % 16
    target = 64 + face_of * 16 + t_of
    for k in range(4):
        both = stage[k]
        other = pltpu.roll(both, 64, 1)
        for s, part in enumerate((both, other)):
            p_lo = 2 * k + s
            pick = ((col == target) & (lo_of == p_lo)).astype(F32).astype(BF16)
            coupled = dot(folded, pick)
            w32[pl.ds(p_lo, 256, stride=8), :] = jnp.where(lane < 64, part, coupled)
    w[...] = w32[...].astype(BF16)


def apply(v, ghosts, w, traces, x_ref, ghost_low, ghost_high, a_ref):
    x_low, x_high, y_low, y_high = [unpack_field(g) for g in ghosts]
    ghost_low[pl.ds(0, 24, stride=8), :] = y_low[:24]
    ghost_high[pl.ds(7, 24, stride=8), :] = y_high[:24]
    lane, row = iota((NE, 128), 1), iota((NE, 128), 0)
    for n in range(NRHS):
        own = traces[n * NE : (n + 1) * NE]
        from_low_x = jnp.concatenate([x_low[n * 8 : n * 8 + 8], own[:24]], 0)
        from_high_x = jnp.concatenate([own[8:], x_high[n * 8 : n * 8 + 8]], 0)
        from_low_y = jnp.where(
            row % 8 == 0, ghost_low[n * NE : (n + 1) * NE, :], pltpu.roll(own, 1, 0)
        )
        from_high_y = jnp.where(
            row % 8 == 7, ghost_high[n * NE : (n + 1) * NE, :], pltpu.roll(own, NE - 1, 0)
        )
        x_ref[n * NE : (n + 1) * NE, :] = jnp.where(
            lane < 64,
            own,
            jnp.where(
                lane < 80,
                from_low_x,
                jnp.where(lane < 96, from_high_x, jnp.where(lane < 112, from_low_y, from_high_y)),
            ),
        )
    x_ref[ROWS:, :] = jnp.zeros((64, 128), F32)
    for e in range(NE):
        hi, lo = split(x_ref[pl.ds(e, 8, stride=NE), :])
        out = dot(jnp.concatenate([hi, lo], 0), w[e * 64 : e * 64 + 64, :], NT)
        a_ref[pl.ds(e, 8, stride=NE), 0:64] = out[:8] + out[8:]
    return a_ref[:ROWS, 0:64]


def factors(bounds):
    low, high = bounds[0:1, 0:1], bounds[0:1, 1:2]
    centre = 0.5 * (high + low)
    half_width = 0.5 * (high - low)
    spread = centre / half_width
    first = 1.0 / spread
    second = 1.0 / (2.0 * spread - first)
    third = 1.0 / (2.0 * spread - second)
    return centre, half_width, first, second, third


def expand(inverse):
    return jnp.concatenate([inverse] * NRHS, 0)


def first_kernel(guess, rhs, w, inverse, bounds, g0, g1, g2, g3, residue, update, answer,
                 xe, xo, ye, yo, x_ref, low_ref, high_ref, a_ref):
    centre = factors(bounds)[0]
    ghosts = received((g0, g1, g2, g3), 64, FIELD_SIZES)
    v = guess[...].reshape(ROWS, 64)
    applied = apply(v, ghosts, w, with_traces(v), x_ref, low_ref, high_ref, a_ref)
    r = rhs[...].reshape(ROWS, 64) - applied
    u = expand(inverse[...]) * r / centre
    residue[...] = r
    update[...] = u
    answer[...] = v + u
    store_messages((xe, xo, ye, yo), 0, field_messages(with_traces(u), low_ref))


def next_kernel(step, residue, update, answer, w, inverse, bounds, g0, g1, g2, g3, *refs):
    centre, half_width, first, second, third = factors(bounds)
    ghosts = received((g0, g1, g2, g3), 0, FIELD_SIZES)
    u = update[...]
    x_ref, low_ref, high_ref, a_ref = refs[-4:]
    applied = apply(u, ghosts, w, with_traces(u), x_ref, low_ref, high_ref, a_ref)
    r = residue[...] - applied
    factor, new = (first, second) if step == 0 else (second, third)
    u = new * factor * u + (2.0 * new / half_width) * expand(inverse[...]) * r
    x = answer[...] + u
    if step == 0:
        residue_out, update_out, answer_out, xe, xo, ye, yo = refs[:-4]
        residue_out[...] = r
        update_out[...] = u
        answer_out[...] = x
        store_messages((xe, xo, ye, yo), 0, field_messages(with_traces(u), low_ref))
    else:
        refs[0][...] = x.reshape(NRHS, NE, 64)


def galerkin_kernel(labels, side_labels, t16, plus_y, minus_y, w, g0, g1, g2, g3, local, ghost,
                    tt, xlow, xhigh, ylow, yhigh, masks, big, side):
    lane16 = iota((16, 128), 1)
    x_low, x_high, y_low, y_high = received((g0, g1, g2, g3), 0, TENT_SIZES)
    for ref, value in ((xlow, x_low), (xhigh, x_high)):
        wide = value.astype(F32)
        other = pltpu.roll(wide, 64, 1)
        lane64 = iota((64, 128), 1)
        ref[0:64, :] = jnp.where(lane64 < 64, wide, other).astype(BF16)
        ref[64:128, :] = jnp.where(lane64 < 64, other, wide).astype(BF16)
    ylow[...] = y_low
    yhigh[...] = y_high
    lane256 = iota((16, 256), 1)
    for b in range(4):
        masks[b * 16 : b * 16 + 16, :] = (lane256 // 64 == b).astype(F32).astype(BF16)
    lane128 = iota((64, 128), 1)
    for pair in range(NE // 2):
        turned = t16[pair * 128 : pair * 128 + 128, :].astype(F32).T[:64]
        first, second = labels[2 * pair], labels[2 * pair + 1]
        for a in range(4):
            keep = jnp.where(
                lane128 < 64,
                jnp.where(first == a, 1.0, 0.0),
                jnp.where(second == a, 1.0, 0.0),
            )
            tt[a * 64 : a * 64 + 64, pair * 128 : pair * 128 + 128] = (turned * keep).astype(BF16)
    side[...] = jnp.zeros_like(side)
    z = lambda count: jnp.zeros((count, 128), BF16)

    def masked(piece, label):
        mask = masks[pl.ds(pl.multiple_of(label * 16, 16), 16), :]
        return jnp.concatenate([piece, piece], 1) * jnp.concatenate([mask] * 4, 0)

    def row_of_elements(ix, carry):
        for iy in range(EY):
            e = ix * EY + iy
            own = pl.ds(pl.multiple_of(e * 64, 64), 64)
            before = pl.multiple_of(jnp.maximum(e - 8, 0) * 64, 64)
            after = pl.multiple_of(jnp.minimum(e + 8, 31) * 64, 64)
            rows0 = jnp.where(
                ix == 0,
                xlow[iy * 16 : iy * 16 + 16, :].astype(F32),
                t16[pl.ds(before + 48, 16), :].astype(F32),
            ).astype(BF16)
            rows1 = jnp.where(
                ix == 3,
                xhigh[iy * 16 : iy * 16 + 16, :].astype(F32),
                t16[pl.ds(after, 16), :].astype(F32),
            ).astype(BF16)
            edge = pl.ds(pl.multiple_of(ix * 16, 16), 16)
            rows2 = ylow[edge, :] if iy == 0 else plus_y[pl.ds(pl.multiple_of((e - 1) * 16, 16), 16), :]
            rows3 = yhigh[edge, :] if iy == 7 else minus_y[pl.ds(pl.multiple_of((e + 1) * 16, 16), 16), :]
            columns = [jnp.concatenate([t16[own, :], z(64)], 0)]
            for f, rows in enumerate((rows0, rows1, rows2, rows3)):
                parts = [z(64 + 16 * f), rows] + ([z(48 - 16 * f)] if f < 3 else [])
                columns.append(jnp.concatenate(parts, 0))
            pieces = dot(w[own, :], jnp.concatenate(columns, 1)).astype(BF16)
            piece = lambda s: pieces[:, s * 128 : s * 128 + 128]
            label0 = jnp.where(ix == 0, side_labels[iy], labels[jnp.maximum(e - 8, 0)])
            label1 = jnp.where(ix == 3, side_labels[8 + iy], labels[jnp.minimum(e + 8, 31)])
            big[0, own, :] = masked(piece(0), labels[e])
            big[1, own, :] = masked(piece(1), label0)
            big[2, own, :] = masked(piece(2), label1)
            if iy == 0:
                big[3, own, :] = jnp.zeros((64, 256), BF16)
                side[0, pl.ds(pl.multiple_of(ix * 128, 128), 64), :] = masked(piece(3), side_labels[16 + ix])
            else:
                big[3, own, :] = masked(piece(3), labels[e - 1])
            if iy == 7:
                big[4, own, :] = jnp.zeros((64, 256), BF16)
                side[1, pl.ds(pl.multiple_of(ix * 128, 128) + 64, 64), :] = masked(piece(4), side_labels[20 + ix])
            else:
                big[4, own, :] = masked(piece(4), labels[e + 1])
        return carry

    lax.fori_loop(0, EX, row_of_elements, 0)
    local[...] = (
        dot(tt[...], big[0])
        + dot(tt[:, 512:], big[1, 512:, :])
        + dot(tt[:, :1536], big[2, :1536, :])
        + dot(tt[...], big[3])
        + dot(tt[...], big[4])
    )
    ghost[0] = dot(tt[:, :512], big[1, :512, :])
    ghost[1] = dot(tt[:, 1536:], big[2, 1536:, :])
    for f in range(2):
        lhs = jnp.concatenate(
            [tt[:, (4 * ix + 3 * f) * 128 : (4 * ix + 3 * f + 1) * 128] for ix in range(4)], 1
        )
        ghost[2 + f] = dot(lhs, side[f])


def call(kernel, outs, scratch, operands, flops, moved, specs=None):
    return pl.pallas_call(
        kernel,
        out_shape=outs,
        in_specs=specs or [VMEM] * len(operands),
        out_specs=jax.tree.map(lambda _: VMEM, outs),
        scratch_shapes=scratch,
        cost_estimate=pl.CostEstimate(flops=flops, bytes_accessed=moved, transcendentals=0),
        compiler_params=pltpu.CompilerParams(vmem_limit_bytes=48 * 1024 * 1024),
    )(*operands)


def exchange(messages):
    out = []
    for message, axis, first in zip(messages, ("bx", "bx", "by", "by"), (0, 1, 0, 1)):
        pairs = []
        for i in range(first, lax.axis_size(axis) - 1, 2):
            pairs += [(i, i + 1), (i + 1, i)]
        out.append(lax.ppermute(message, axis, pairs))
    return out


def shaped(*shape, dtype=F32):
    return jax.ShapeDtypeStruct(shape, dtype)


FIELD_SCRATCH = [
    pltpu.VMEM((ROWS + 64, 128), F32),
    pltpu.VMEM((ROWS, 128), F32),
    pltpu.VMEM((ROWS, 128), F32),
    pltpu.VMEM((ROWS + 64, 128), F32),
]


def on_device(blocks, faces, tentative, aggregate, ghost_labels, rhs, guess, bounds):
    blocks, faces, tentative = [a.reshape(NE, 4096) for a in (blocks, faces, tentative)]
    rhs = jnp.swapaxes(rhs[0, 0], 1, 2)
    guess = jnp.swapaxes(guess[0, 0], 1, 2)
    bounds = bounds.reshape(1, 2)
    message = lambda rows: [shaped(r, 128, dtype=BF16) for r in rows]
    both = [f + t for f, t in zip(FIELD_SIZES, TENT_SIZES)]
    t16, plus_y, minus_y, *sends = call(
        pack_kernel,
        [shaped(2048, 128, dtype=BF16), shaped(512, 128, dtype=BF16), shaped(512, 128, dtype=BF16)] + message(both),
        [pltpu.VMEM((4, 256, 128), F32), pltpu.VMEM((2048, 128), F32), pltpu.VMEM((ROWS, 128), F32)],
        (guess, tentative), 10**6, 2**20,
    )
    first_ghosts = exchange(sends)
    w, inverse = call(
        prep_kernel,
        [shaped(2048, 128, dtype=BF16), shaped(NE, 64)],
        [pltpu.VMEM((4, 256, 128), F32), pltpu.VMEM((4, 256, 128), F32), pltpu.VMEM((2048, 128), F32)],
        (blocks, faces), 10**8, 2**20,
    )
    field = shaped(ROWS, 64)
    residue, update, answer, *sends = call(
        first_kernel, [field] * 3 + message(FIELD_SIZES), FIELD_SCRATCH,
        (guess, rhs, w, inverse, bounds, *first_ghosts), 10**8, 2**20,
    )
    ghosts = exchange(sends)
    local, ghost = call(
        galerkin_kernel,
        [shaped(256, 256), shaped(4, 256, 256)],
        [
            pltpu.VMEM((256, 2048), BF16),
            pltpu.VMEM((128, 128), BF16),
            pltpu.VMEM((128, 128), BF16),
            pltpu.VMEM((64, 128), BF16),
            pltpu.VMEM((64, 128), BF16),
            pltpu.VMEM((64, 256), BF16),
            pltpu.VMEM((5, 2048, 256), BF16),
            pltpu.VMEM((2, 512, 256), BF16),
        ],
        (aggregate.reshape(NE), ghost_labels.reshape(24), t16, plus_y, minus_y, w, *first_ghosts),
        4 * 10**9, 4 * 2**20,
        [SMEM, SMEM] + [VMEM] * 8,
    )
    residue, update, answer, *sends = call(
        lambda *refs: next_kernel(0, *refs), [field] * 3 + message(FIELD_SIZES), FIELD_SCRATCH,
        (residue, update, answer, w, inverse, bounds, *ghosts), 10**8, 2**20,
    )
    ghosts = exchange(sends)
    (smoothed,) = call(
        lambda *refs: next_kernel(1, *refs), [shaped(NRHS, NE, 64)], FIELD_SCRATCH,
        (residue, update, answer, w, inverse, bounds, *ghosts), 10**8, 2**20,
    )
    return jnp.swapaxes(smoothed, 1, 2)[None, None], local[None, None], ghost[None, None]


def solution(mesh):
    b = lambda extra: P("bx", "by", *([None] * extra))
    return jax.shard_map(
        on_device,
        mesh=mesh,
        in_specs=(b(2), b(2), b(2), b(1), b(1), b(3), b(3), P()),
        out_specs=(b(3), b(2), b(3)),
        check_vma=False,
    )
```

```python
import jax
import jax.numpy as jnp
from jax import lax
from jax.experimental import pallas as pl
from jax.experimental.pallas import tpu as pltpu
from jax.sharding import PartitionSpec as P

EX, EY, NE, NRHS = 4, 8, 32, 6
F32, BF16 = jnp.float32, jnp.bfloat16
VMEM = pl.BlockSpec(memory_space=pltpu.VMEM)
SMEM = pl.BlockSpec(memory_space=pltpu.SMEM)
ANY = pl.BlockSpec(memory_space=pl.ANY)
NT = (((1,), (1,)), ((), ()))
NN = (((1,), (0,)), ((), ()))

XA, XB = 0, 2048
XC = 4096
XD = 5120
XG = 5888
XR = 6656
XT = 7424
XLEN = 7936
YA, YB = 0, 2048
YF = 4096
YC = 5120
YD = 5632
YG = 6400
YR = 7168
YT = 7552
YLEN = 8064

EXT, SPAN = 160, 960


def dot(a, b, dims=NN):
    return lax.dot_general(a, b, dims, preferred_element_type=F32)


def iota(shape, dim):
    return lax.broadcasted_iota(jnp.int32, shape, dim)


def onehot(mask):
    return mask.astype(F32).astype(BF16)


def split(x):
    hi = x.astype(BF16)
    return hi, (x - hi.astype(F32)).astype(BF16)


def halves(x):
    lanes = x.shape[1] // 2
    return jnp.concatenate([x[:, :lanes], x[:, lanes:]], 0)


def over(a, b):
    return jnp.concatenate([a, b], 0)


def parity(axis):
    return lax.axis_index(axis) % 2


def with_traces(v):
    q, lane = iota((64, 128), 0), iota((64, 128), 1)
    t = lane % 16
    f = lane // 16 - 4
    along_y = 16 * (t // 4) + t % 4
    source = jnp.where(f == 0, 48 + t, jnp.where(f == 1, t, jnp.where(f == 2, along_y + 12, along_y)))
    pick = onehot(q == jnp.where(f < 0, lane, source))
    hi, lo = split(v)
    return dot(hi, pick) + dot(lo, pick)


def pack_lanes(v):
    hi, lo = split(v)
    q, lane = iota((64, 128), 0), iota((64, 128), 1)
    both = dot(hi, onehot(q == lane)) + dot(lo, onehot(q == lane - 64))
    return jnp.concatenate([both[n * NE : (n + 1) * NE] for n in range(NRHS)], 1)


def pack_x_kernel(blocks, faces, tent, guess, rhs, even, odd, guess_packed, rhs_packed):
    g = pack_lanes(guess[...].reshape(NRHS * NE, 64))
    r = pack_lanes(rhs[...].reshape(NRHS * NE, 64))
    guess_packed[...] = g.astype(BF16)
    rhs_packed[...] = r.astype(BF16)
    first = parity("bx") == 0

    def put(start, lanes, make):
        low, high = make(0), make(1)
        even[:, start : start + lanes] = jnp.where(first, high, low).astype(BF16)
        odd[:, start : start + lanes] = jnp.where(first, low, high).astype(BF16)

    def rows(k, side):
        return 8 * k if side == 0 else 24 - 8 * k

    def of(ref, k, side, start, lanes):
        row = rows(k, side)
        base = row // 16 * 16
        return ref[base : base + 16, start : start + lanes].astype(F32)[row - base : row - base + 8]

    def packed(value, k, side):
        return value[rows(k, side) : rows(k, side) + 8]

    def face_traces(side):
        return jnp.concatenate([of(faces, 1, side, f * 1024 + 768 * side, 256) for f in range(4)], 1)

    for h in range(2):
        put(XA + h * 1024, 1024, lambda s: over(of(blocks, 0, s, h * 1024, 1024), of(blocks, 0, s, h * 1024 + 2048, 1024)))
        put(XB + h * 1024, 1024, lambda s: over(of(faces, 0, s, h * 1024, 1024), of(faces, 0, s, h * 1024 + 2048, 1024)))
    put(XC, 1024, lambda s: over(of(blocks, 1, s, 3072 * s, 1024), face_traces(s)))
    put(XD, 768, lambda s: over(packed(g, 0, s), packed(g, 1, s)))
    put(XG, 768, lambda s: over(packed(g, 2, s), packed(r, 0, s)))
    put(XR, 768, lambda s: over(packed(r, 1, s), jnp.zeros((8, 768), F32)))
    put(XT, 512, lambda s: halves(of(tent, 0, s, 3072 * s, 1024)))


def pack_y_kernel(blocks, faces, tent, guess_packed, rhs_packed, x_even, x_odd, even, odd, low, high):
    first = parity("bx") == 0
    for start in range(0, XLEN, 256):
        a = x_even[:, start : start + 256].astype(F32)
        b = x_odd[:, start : start + 256].astype(F32)
        low[:, start : start + 256] = jnp.where(first, b, a).astype(BF16)
        high[:, start : start + 256] = jnp.where(first, a, b).astype(BF16)
    py = parity("by")
    is_first = py == 0

    def select(k, near=None, far=None, columns=64):
        r, j = iota((16, columns), 0), iota((16, columns), 1)
        high_side = jnp.where(r < 8, py, 1 - py) == 0
        iy = jnp.where(high_side, 7 - k, k)
        row = r % 8 - 2
        source = jnp.where((row >= 0) & (row < 4), row * 8 + iy, -1)
        if near is not None:
            source = jnp.where(row == -1, 32 + near + iy, jnp.where(row == 4, 48 + near + iy, source))
        if far is not None:
            source = jnp.where(row == -2, 32 + far + iy, jnp.where(row == 5, 48 + far + iy, source))
        return onehot(j == source)

    def put(start, value):
        even[:, start : start + value[0].shape[1]] = value[0].astype(BF16)
        odd[:, start : start + value[1].shape[1]] = value[1].astype(BF16)

    def both(make, picked):
        return make(picked[:8]), make(picked[8:])

    for ref, start, part in ((blocks, YA, XA), (faces, YB, XB)):
        cut = []
        for h in range(2):
            source = jnp.concatenate(
                [ref[:, h * 2048 : h * 2048 + 2048], low[:, part : part + 2048], high[:, part : part + 2048]], 0
            )
            cut.append(dot(select(0, 8 * h), source))
        put(start, (over(cut[0][:8], cut[1][:8]), over(cut[0][8:], cut[1][8:])))

    def by_side(minus, plus):
        up = jnp.where(is_first, plus[:8], minus[:8])
        down = jnp.where(is_first, minus[8:], plus[8:])
        return halves(up), halves(down)

    own1, own0 = select(1, columns=32), select(0, columns=32)

    def lanes(ref, pieces, width):
        return jnp.concatenate([ref[:, p : p + width] for p in pieces], 1)

    minus, plus = [i * 1024 for i in range(4)], [i * 1024 + 768 for i in range(4)]
    put(YC, by_side(dot(own1, lanes(blocks, minus, 256)), dot(own1, lanes(blocks, plus, 256))))
    put(YT, by_side(dot(own0, lanes(tent, minus, 256)), dot(own0, lanes(tent, plus, 256))))
    minus = [f * 1024 + i * 256 for f in range(4) for i in range(4)]
    plus = [p + 128 for p in minus]
    put(YF, by_side(dot(own1, lanes(faces, minus, 128)), dot(own1, lanes(faces, plus, 128))))
    own = guess_packed[...]
    rows = jnp.concatenate([own, low[:, XD : XD + 768], high[:, XD : XD + 768]], 0)
    g0, g1, g2 = dot(select(0, 0, 8), rows), dot(select(1, 0), rows), dot(select(2, columns=32), own)
    rows = jnp.concatenate([rhs_packed[...], low[:, XG : XG + 768], high[:, XG : XG + 768]], 0)
    r0, r1 = dot(select(0, 8), rows), dot(own1, rhs_packed[...])
    put(YD, (over(g0[:8], g1[:8]), over(g0[8:], g1[8:])))
    put(YG, (over(g2[:8], r0[:8]), over(g2[8:], r0[8:])))
    put(YR, both(halves, r1))


def prolong_kernel(tent, t16, plus_y, minus_y, stage, t32):
    lane = iota((256, 128), 1)
    for k in range(4):
        for ph in range(8):
            chunk = tent[:, (ph * 4 + k) * 128 : (ph * 4 + k + 1) * 128].astype(F32)
            stage[k, pl.ds(ph, NE, stride=8), :] = chunk
    for k in range(4):
        both = stage[k]
        other = pltpu.roll(both, 64, 1)
        t32[pl.ds(2 * k, 256, stride=8), :] = jnp.where(lane < 64, both, other)
        t32[pl.ds(2 * k + 1, 256, stride=8), :] = jnp.where(lane < 64, other, both)
    t16[...] = t32[...].astype(BF16)
    sub = iota((8, 128), 0)
    for e in range(NE):
        plus, minus = [], []
        for h in range(2):
            base = e * 64 + 32 * h
            a, b = t32[base + 8 : base + 16, :], t32[base + 24 : base + 32, :]
            plus.append(jnp.where(sub < 4, pltpu.roll(a, 4, 0), b))
            a, b = t32[base : base + 8, :], t32[base + 16 : base + 24, :]
            minus.append(jnp.where(sub < 4, a, pltpu.roll(b, 4, 0)))
        plus_y[e * 16 : e * 16 + 16, :] = jnp.concatenate(plus, 0).astype(BF16)
        minus_y[e * 16 : e * 16 + 16, :] = jnp.concatenate(minus, 0).astype(BF16)


def operators(block_chunk, face_chunk, w, inverse, stage, fstage, w32):
    lane = iota((256, 128), 1)
    lane_e = iota((NE, 128), 1)
    diag = jnp.zeros((NE, 128), F32)
    for k in range(4):
        for ph in range(8):
            c = ph * 4 + k
            chunk = block_chunk(c)
            diag = diag + jnp.where((lane_e == 2 * c) | (lane_e == 65 + 2 * c), chunk, 0.0)
            stage[k, pl.ds(ph, NE, stride=8), :] = chunk
    diag = (diag + pltpu.roll(diag, 64, 1))[:, :64]
    inverse[...] = 1.0 / jnp.where(diag == 0.0, 1.0, diag)
    for f in range(4):
        for ph in range(8):
            fstage[f, pl.ds(ph, NE, stride=8), :] = face_chunk(f * 8 + ph)
    folded = jnp.concatenate([fstage[f].astype(BF16) for f in range(4)], 1)
    row, col = iota((512, 128), 0), iota((512, 128), 1)
    lo_of = (row // 16) % 8
    target = 64 + row // 128 * 16 + row % 16
    for k in range(4):
        both = stage[k]
        other = pltpu.roll(both, 64, 1)
        for s, part in enumerate((both, other)):
            p_lo = 2 * k + s
            coupled = dot(folded, onehot((col == target) & (lo_of == p_lo)))
            w32[pl.ds(p_lo, 256, stride=8), :] = jnp.where(lane < 64, part, coupled)
    w[...] = w32[...].astype(BF16)


def own_kernel(blocks, faces, w, inverse, *scratch):
    chunk = lambda ref: lambda c: ref[:, c * 128 : (c + 1) * 128].astype(F32)
    operators(chunk(blocks), chunk(faces), w, inverse, *scratch)


NOTHING = (8, 128)


def part(ref, start, c, half):
    row = 8 * (c // half)
    lane = start + (c % half) * 128
    return ref[:, lane : lane + 128].astype(F32)[row : row + 8]


def halo_x_kernel(low, high, w, inverse, *scratch):
    zero = jnp.zeros(NOTHING, F32)

    def block(c):
        far_low = part(low, XC, c - 24, 8) if c >= 24 else zero
        far_high = part(high, XC, c, 8) if c < 8 else zero
        return jnp.concatenate([part(low, XA, c, 16), far_low, part(high, XA, c, 16), far_high], 0)

    def face(c):
        f, ph = c // 8, c % 8
        far_low = part(low, XC, 8 + f * 2 + ph - 6, 8) if ph >= 6 else zero
        far_high = part(high, XC, 8 + f * 2 + ph, 8) if ph < 2 else zero
        return jnp.concatenate([part(low, XB, c, 16), far_low, part(high, XB, c, 16), far_high], 0)

    operators(block, face, w, inverse, *scratch)


def halo_y_kernel(even, odd, w, inverse, low, high, *scratch):
    first = parity("by") == 0
    for start in range(0, YLEN, 128):
        a = even[:, start : start + 128].astype(F32)
        b = odd[:, start : start + 128].astype(F32)
        low[:, start : start + 128] = jnp.where(first, b, a).astype(BF16)
        high[:, start : start + 128] = jnp.where(first, a, b).astype(BF16)
    zero = jnp.zeros(NOTHING, F32)

    def block(c):
        i, d = c // 8, c % 8
        far_low = part(low, YC, i * 2 + d - 6, 4) if d >= 6 else zero
        far_high = part(high, YC, i * 2 + d, 4) if d < 2 else zero
        return jnp.concatenate([part(low, YA, c, 16), far_low, part(high, YA, c, 16), far_high], 0)

    def face(c):
        f, ph = c // 8, c % 8
        i = ph // 2
        far_low = part(low, YF, f * 4 + i, 8) if ph % 2 == 1 else zero
        far_high = part(high, YF, f * 4 + i, 8) if ph % 2 == 0 else zero
        return jnp.concatenate([part(low, YB, c, 16), far_low, part(high, YB, c, 16), far_high], 0)

    operators(block, face, w, inverse, *scratch)


def factors(bounds):
    low, high = bounds[0:1, 0:1], bounds[0:1, 1:2]
    centre = 0.5 * (high + low)
    half_width = 0.5 * (high - low)
    spread = centre / half_width
    first = 1.0 / spread
    second = 1.0 / (2.0 * spread - first)
    third = 1.0 / (2.0 * spread - second)
    return centre, half_width, first, second, third


OWN = [((ix + 3) * 16 + iy, 0, ix * 8 + iy) for ix in range(EX) for iy in range(EY)]


def beside_x(k):
    return [((7 + k if s else 2 - k) * 16 + iy, 1, s * 16 + k * 8 + iy) for s in range(2) for iy in range(EY)]


def beside_y(k, rows):
    return [((r + 1) * 16 + (8 + k if s else 15 - k), 2, s * 16 + k * 8 + r) for s in range(2) for r in rows]


LEVELS = (
    (1, 9, OWN + beside_x(0) + beside_x(1) + beside_y(0, range(1, 7)) + beside_y(1, range(2, 6))),
    (2, 8, OWN + beside_x(0) + beside_y(0, range(2, 6))),
    (3, 7, OWN),
)


def smooth_kernel(guess, rhs, w, wx, wy, inv, inv_x, inv_y, bounds, x_low, x_high, y_low, y_high, smoothed,
                  g_ref, r_ref, i_ref, t_ref, x_ref, a_ref):
    def joined(value):
        return value + pltpu.roll(value, 64, 1)

    def fill(ref, own, x_parts, y_parts):
        ref[...] = jnp.zeros((SPAN, 128), F32)
        for n in range(NRHS):
            for ix in range(EX):
                row = n * EXT + (ix + 3) * 16
                ref[row : row + 8, 0:64] = own[n, ix * 8 : ix * 8 + 8, :]
            for side, message in enumerate((x_low, x_high)):
                for k, (start, top) in enumerate(x_parts):
                    row = n * EXT + (7 + k if side else 2 - k) * 16
                    value = message[:, start + n * 128 : start + n * 128 + 128].astype(F32)
                    ref[row : row + 8, :] = joined(value[8 * top : 8 * top + 8])
            for side, message in enumerate((y_low, y_high)):
                for k, (start, top, half) in enumerate(y_parts):
                    value = part(message, start, n, half) if half else (
                        message[:, start + n * 128 : start + n * 128 + 128].astype(F32)[8 * top : 8 * top + 8]
                    )
                    ref[pl.ds(n * EXT + 16 + (8 + k if side else 15 - k), 8, stride=16), :] = joined(value)

    fill(g_ref, guess, ((XD, 0), (XD, 1), (XG, 0)), ((YD, 0, 0), (YD, 1, 0), (YG, 0, 0)))
    fill(r_ref, rhs, ((XG, 1), (XR, 0)), ((YG, 1, 0), (YR, 0, 3)))
    i_ref[...] = jnp.ones((EXT, 128), F32)
    wide = lambda value: jnp.concatenate([value, value], 1)
    for ix in range(EX):
        i_ref[(ix + 3) * 16 : (ix + 3) * 16 + 8, 0:64] = inv[ix * 8 : ix * 8 + 8, :]
    for s in range(2):
        for k in range(2):
            base = s * 16 + k * 8
            row = (7 + k if s else 2 - k) * 16
            i_ref[row : row + 8, 0:64] = inv_x[base : base + 8, :]
            i_ref[pl.ds(16 + (8 + k if s else 15 - k), 8, stride=16), :] = wide(inv_y[base : base + 8, :])
    x_ref[...] = jnp.zeros((8 * EXT, 128), F32)
    a_ref[...] = jnp.zeros((8 * EXT, 128), F32)
    lane = iota((16, 128), 1)
    tables = (w, wx, wy)

    def apply(level, v):
        first, last, elements = LEVELS[level]
        t_ref[...] = with_traces(v)
        for n in range(NRHS):
            for ri in range(first, last):
                row = n * EXT + ri * 16
                own = t_ref[row : row + 16, :]
                sides = jnp.where(
                    lane < 80,
                    t_ref[row - 16 : row, :],
                    jnp.where(
                        lane < 96,
                        t_ref[row + 16 : row + 32, :],
                        jnp.where(lane < 112, pltpu.roll(own, 1, 0), pltpu.roll(own, 15, 0)),
                    ),
                )
                x_ref[row : row + 16, :] = jnp.where(lane < 64, own, sides)
        for row, table, e in elements:
            hi, lo = split(x_ref[pl.ds(row, 8, stride=EXT), :])
            out = dot(over(hi, lo), tables[table][e * 64 : e * 64 + 64, :], NT)
            a_ref[pl.ds(row, 8, stride=EXT), 0:64] = out[:8] + out[8:]
        return a_ref[:SPAN, 0:64]

    centre, half_width, first, second, third = factors(bounds)
    inverse = jnp.concatenate([i_ref[:, 0:64]] * NRHS, 0)
    v = g_ref[:, 0:64]
    r = r_ref[:, 0:64] - apply(0, v)
    u = inverse * r / centre
    x = v + u
    for level, factor, new in ((1, first, second), (2, second, third)):
        r = r - apply(level, u)
        u = new * factor * u + (2.0 * new / half_width) * inverse * r
        x = x + u
    for n in range(NRHS):
        for ix in range(EX):
            row = n * EXT + (ix + 3) * 16
            smoothed[n, ix * 8 : ix * 8 + 8, :] = x[row : row + 8]


def ghost_rows(message, start, out):
    lane = iota((8, 128), 1)
    for j in range(8):
        both = part(message, start, j, 4)
        other = pltpu.roll(both, 64, 1)
        out[pl.ds(2 * j, 8, stride=16), :] = jnp.where(lane < 64, both, other)
        out[pl.ds(2 * j + 1, 8, stride=16), :] = jnp.where(lane < 64, other, both)


def label_masks(masks):
    lane = iota((16, 256), 1)
    for b in range(4):
        masks[b * 16 : b * 16 + 16, :] = onehot(lane // 64 == b)


def masked(masks, piece, label):
    mask = masks[pl.ds(pl.multiple_of(label * 16, 16), 16), :]
    return jnp.concatenate([piece, piece], 1) * jnp.concatenate([mask] * 4, 0)


def none(count):
    return jnp.zeros((count, 128), BF16)


def face_column(f, rows):
    return jnp.concatenate([none(64 + 16 * f), rows] + ([none(48 - 16 * f)] if f < 3 else []), 0)


def galerkin_kernel(labels, side_labels, t16, plus_y, minus_y, w, x_low, x_high, local, ghost, edge_columns,
                    tt, xlow, xhigh, masks, big):
    ghost_rows(x_low, XT, xlow)
    ghost_rows(x_high, XT, xhigh)
    label_masks(masks)
    lane128 = iota((64, 128), 1)
    for pair in range(NE // 2):
        turned = t16[pair * 128 : pair * 128 + 128, :].astype(F32).T[:64]
        first, second = labels[2 * pair], labels[2 * pair + 1]
        for a in range(4):
            keep = jnp.where(
                lane128 < 64,
                jnp.where(first == a, 1.0, 0.0),
                jnp.where(second == a, 1.0, 0.0),
            )
            tt[a * 64 : a * 64 + 64, pair * 128 : pair * 128 + 128] = (turned * keep).astype(BF16)
    for f in range(2):
        for ix in range(EX):
            start = (4 * ix + 3 * f) * 128
            edge_columns[f, :, ix * 128 : ix * 128 + 128] = tt[:, start : start + 128]

    def row_of_elements(ix, carry):
        for iy in range(EY):
            e = ix * EY + iy
            own = pl.ds(pl.multiple_of(e * 64, 64), 64)
            before = pl.multiple_of(jnp.maximum(e - 8, 0) * 64, 64)
            after = pl.multiple_of(jnp.minimum(e + 8, 31) * 64, 64)
            rows = [
                jnp.where(ix == 0, xlow[iy * 16 : iy * 16 + 16, :], t16[pl.ds(before + 48, 16), :].astype(F32)).astype(BF16),
                jnp.where(ix == 3, xhigh[iy * 16 : iy * 16 + 16, :], t16[pl.ds(after, 16), :].astype(F32)).astype(BF16),
            ]
            if iy > 0:
                rows.append(plus_y[pl.ds(pl.multiple_of((e - 1) * 16, 16), 16), :])
            else:
                rows.append(none(16))
            if iy < 7:
                rows.append(minus_y[pl.ds(pl.multiple_of((e + 1) * 16, 16), 16), :])
            columns = [jnp.concatenate([t16[own, :], none(64)], 0)]
            columns += [face_column(f, value) for f, value in enumerate(rows)]
            pieces = dot(w[own, :], jnp.concatenate(columns, 1)).astype(BF16)
            piece = lambda s: pieces[:, s * 128 : s * 128 + 128]
            label0 = jnp.where(ix == 0, side_labels[iy], labels[jnp.maximum(e - 8, 0)])
            label1 = jnp.where(ix == 3, side_labels[8 + iy], labels[jnp.minimum(e + 8, 31)])
            big[0, own, :] = masked(masks, piece(0), labels[e])
            big[1, own, :] = masked(masks, piece(1), label0)
            big[2, own, :] = masked(masks, piece(2), label1)
            nothing = jnp.zeros((64, 256), BF16)
            big[3, own, :] = masked(masks, piece(3), labels[e - 1]) if iy > 0 else nothing
            big[4, own, :] = masked(masks, piece(4), labels[e + 1]) if iy < 7 else nothing
        return carry

    lax.fori_loop(0, EX, row_of_elements, 0)
    local[...] = (
        dot(tt[...], big[0])
        + dot(tt[:, 512:], big[1, 512:, :])
        + dot(tt[:, :1536], big[2, :1536, :])
        + dot(tt[...], big[3])
        + dot(tt[...], big[4])
    )
    ghost[0] = dot(tt[:, :512], big[1, :512, :])
    ghost[1] = dot(tt[:, 1536:], big[2, 1536:, :])
    ghost[2] = jnp.zeros((256, 256), F32)
    ghost[3] = jnp.zeros((256, 256), F32)


def ghost_y_kernel(side_labels, w, edge_columns, y_low, y_high, ghost_in, ghost, rows, masks, side, result, sems):
    label_masks(masks)
    copies = []
    for f, message in enumerate((y_low, y_high)):
        ghost_rows(message, YT, rows)
        side[...] = jnp.zeros((512, 256), BF16)
        for ix in range(EX):
            e = ix * EY + 7 * f
            near = rows[(ix + 2) * 16 : (ix + 2) * 16 + 16, :].astype(BF16)
            piece = dot(w[e * 64 : e * 64 + 64, :], face_column(2 + f, near)).astype(BF16)
            start = ix * 128 + 64 * f
            side[start : start + 64, :] = masked(masks, piece, side_labels[16 + 4 * f + ix])
        result[f] = dot(edge_columns[f], side[...])
        copies.append(pltpu.make_async_copy(result.at[f], ghost.at[2 + f], sems.at[f]))
        copies[-1].start()
    for copy in copies:
        copy.wait()


def call(kernel, outs, scratch, operands, flops, moved, in_specs=None, out_specs=None, aliases=None):
    return pl.pallas_call(
        kernel,
        out_shape=outs,
        in_specs=in_specs or [VMEM] * len(operands),
        out_specs=out_specs or [VMEM] * len(outs),
        scratch_shapes=scratch,
        input_output_aliases=aliases or {},
        cost_estimate=pl.CostEstimate(flops=flops, bytes_accessed=moved, transcendentals=0),
        compiler_params=pltpu.CompilerParams(vmem_limit_bytes=48 * 1024 * 1024),
    )(*operands)


def exchange(messages, axis):
    out = []
    for first, message in enumerate(messages):
        pairs = []
        for i in range(first, lax.axis_size(axis) - 1, 2):
            pairs += [(i, i + 1), (i + 1, i)]
        out.append(lax.ppermute(message, axis, pairs))
    return out


def shaped(*shape, dtype=BF16):
    return jax.ShapeDtypeStruct(shape, dtype)


STAGES = [pltpu.VMEM((4, 256, 128), F32), pltpu.VMEM((4, 256, 128), F32), pltpu.VMEM((2048, 128), F32)]


def on_device(blocks, faces, tentative, aggregate, ghost_labels, rhs, guess, bounds):
    blocks, faces, tentative = [a.reshape(NE, 4096) for a in (blocks, faces, tentative)]
    rhs = jnp.swapaxes(rhs[0, 0], 1, 2)
    guess = jnp.swapaxes(guess[0, 0], 1, 2)
    labels, side_labels = aggregate.reshape(NE), ghost_labels.reshape(24)
    packed = shaped(NE, 768)
    even, odd, guess_packed, rhs_packed = call(
        pack_x_kernel, [shaped(16, XLEN)] * 2 + [packed] * 2, [],
        (blocks, faces, tentative, guess, rhs), 10**6, 2**20,
    )
    even, odd = exchange((even, odd), "bx")
    w, inverse = call(
        own_kernel, [shaped(2048, 128), shaped(NE, 64, dtype=F32)], STAGES, (blocks, faces), 10**9, 2**20
    )
    t16, plus_y, minus_y = call(
        prolong_kernel, [shaped(2048, 128), shaped(512, 128), shaped(512, 128)],
        [STAGES[0], STAGES[2]], (tentative,), 5 * 10**8, 2**20,
    )
    even, odd, x_low, x_high = call(
        pack_y_kernel, [shaped(16, YLEN)] * 2 + [shaped(16, XLEN)] * 2, [],
        (blocks, faces, tentative, guess_packed, rhs_packed, even, odd), 10**8, 2**20,
    )
    even, odd = exchange((even, odd), "by")
    wx, inverse_x = call(
        halo_x_kernel, [shaped(2048, 128), shaped(NE, 64, dtype=F32)], STAGES, (x_low, x_high), 10**9, 2**20
    )
    local, ghost, edge_columns = call(
        galerkin_kernel,
        [shaped(256, 256, dtype=F32), shaped(4, 256, 256, dtype=F32), shaped(2, 256, 512)],
        [
            pltpu.VMEM((256, 2048), BF16),
            pltpu.VMEM((128, 128), F32),
            pltpu.VMEM((128, 128), F32),
            pltpu.VMEM((64, 256), BF16),
            pltpu.VMEM((5, 2048, 256), BF16),
        ],
        (labels, side_labels, t16, plus_y, minus_y, w, x_low, x_high),
        4 * 10**9, 4 * 2**20,
        [SMEM, SMEM] + [VMEM] * 6,
    )
    wy, inverse_y, y_low, y_high = call(
        halo_y_kernel, [shaped(2048, 128), shaped(NE, 64, dtype=F32)] + [shaped(16, YLEN)] * 2, STAGES,
        (even, odd), 10**9, 2**20,
    )
    (smoothed,) = call(
        smooth_kernel, [shaped(NRHS, NE, 64, dtype=F32)],
        [pltpu.VMEM((SPAN, 128), F32)] * 2
        + [pltpu.VMEM((EXT, 128), F32), pltpu.VMEM((SPAN, 128), F32)]
        + [pltpu.VMEM((8 * EXT, 128), F32)] * 2,
        (guess, rhs, w, wx, wy, inverse, inverse_x, inverse_y, bounds.reshape(1, 2), x_low, x_high, y_low, y_high),
        10**9, 2**20,
    )
    (ghost,) = call(
        ghost_y_kernel, [shaped(4, 256, 256, dtype=F32)],
        [
            pltpu.VMEM((128, 128), F32),
            pltpu.VMEM((64, 256), BF16),
            pltpu.VMEM((512, 256), BF16),
            pltpu.VMEM((2, 256, 256), F32),
            pltpu.SemaphoreType.DMA((2,)),
        ],
        (side_labels, w, edge_columns, y_low, y_high, ghost), 10**9, 2**20,
        [SMEM] + [VMEM] * 4 + [ANY], [ANY], {5: 0},
    )
    return jnp.swapaxes(smoothed, 1, 2)[None, None], local[None, None], ghost[None, None]


def solution(mesh):
    b = lambda extra: P("bx", "by", *([None] * extra))
    return jax.shard_map(
        on_device,
        mesh=mesh,
        in_specs=(b(2), b(2), b(2), b(1), b(1), b(3), b(3), P()),
        out_specs=(b(3), b(2), b(3)),
        check_vma=False,
    )
```

```python
import jax
import jax.numpy as jnp
from jax import lax
from jax.experimental import pallas as pl
from jax.experimental.pallas import tpu as pltpu
from jax.sharding import PartitionSpec as P

EX, EY, NE, NRHS = 4, 8, 32, 6
F32, BF16 = jnp.float32, jnp.bfloat16
VMEM = pl.BlockSpec(memory_space=pltpu.VMEM)
SMEM = pl.BlockSpec(memory_space=pltpu.SMEM)
HBM = pl.BlockSpec(memory_space=pltpu.HBM)
NT = (((1,), (1,)), ((), ()))
NN = (((1,), (0,)), ((), ()))

XA, XB = 0, 2048
XC = 4096
XD = 5120
XH = 5888
XK = 6272
XT = 6528
XLEN = 7040
YA, YB = 0, 2048
YF = 4096
YC = 5120
YD = 5632
YG = 6400
YR = 7168
YT = 7552
YLEN = 8064

EXT, SPAN = 160, 960


def dot(a, b, dims=NN):
    return lax.dot_general(a, b, dims, preferred_element_type=F32)


def iota(shape, dim):
    return lax.broadcasted_iota(jnp.int32, shape, dim)


def onehot(mask):
    return mask.astype(F32).astype(BF16)


def split(x):
    hi = x.astype(BF16)
    return hi, (x - hi.astype(F32)).astype(BF16)


def halves(x):
    lanes = x.shape[1] // 2
    return jnp.concatenate([x[:, :lanes], x[:, lanes:]], 0)


def over(a, b):
    return jnp.concatenate([a, b], 0)


def parity(axis):
    return lax.axis_index(axis) % 2


def with_traces(v):
    q, lane = iota((64, 128), 0), iota((64, 128), 1)
    t = lane % 16
    f = lane // 16 - 4
    along_y = 16 * (t // 4) + t % 4
    source = jnp.where(f == 0, 48 + t, jnp.where(f == 1, t, jnp.where(f == 2, along_y + 12, along_y)))
    pick = onehot(q == jnp.where(f < 0, lane, source))
    hi, lo = split(v)
    return dot(hi, pick) + dot(lo, pick)


def pack_lanes(v):
    hi, lo = split(v)
    q, lane = iota((64, 128), 0), iota((64, 128), 1)
    both = dot(hi, onehot(q == lane)) + dot(lo, onehot(q == lane - 64))
    return jnp.concatenate([both[n * NE : (n + 1) * NE] for n in range(NRHS)], 1)


def trace_lanes(side):
    row, lane = iota((768, 256), 0), iota((768, 256), 1)
    source = lane // 32 * 128 + lane // 16 % 2 * 64 + lane % 16 + 48 * side
    return onehot((row == source) & (lane < 192))


def pack_x_kernel(blocks_in, faces_in, tent_in, guess_in, rhs_in, bounds_in, even, odd, guess_packed, rhs_packed,
                  blocks, faces, tent, guess, rhs, bounds, sems):
    copies = [
        pltpu.make_async_copy(source, target, sems.at[i])
        for i, (source, target) in enumerate((
            (guess_in, guess), (rhs_in, rhs), (blocks_in, blocks), (faces_in, faces), (tent_in, tent), (bounds_in, bounds),
        ))
    ]
    for copy in copies:
        copy.start()
    for copy in copies:
        copy.wait()
    g = pack_lanes(guess[...].reshape(NRHS * NE, 64))
    r = pack_lanes(rhs[...].reshape(NRHS * NE, 64))
    guess_packed[...] = g.astype(BF16)
    rhs_packed[...] = r.astype(BF16)
    first = parity("bx") == 0

    def put(start, lanes, make):
        low, high = make(0), make(1)
        even[:, start : start + lanes] = jnp.where(first, high, low).astype(BF16)
        odd[:, start : start + lanes] = jnp.where(first, low, high).astype(BF16)

    def rows(k, side):
        return 8 * k if side == 0 else 24 - 8 * k

    def of(ref, k, side, start, lanes):
        row = rows(k, side)
        base = row // 16 * 16
        return ref[base : base + 16, start : start + lanes].astype(F32)[row - base : row - base + 8]

    def packed(value, k, side):
        return value[rows(k, side) : rows(k, side) + 8]

    def face_traces(side):
        return jnp.concatenate([of(faces, 1, side, f * 1024 + 768 * side, 256) for f in range(4)], 1)

    for h in range(2):
        put(XA + h * 1024, 1024, lambda s: over(of(blocks, 0, s, h * 1024, 1024), of(blocks, 0, s, h * 1024 + 2048, 1024)))
        put(XB + h * 1024, 1024, lambda s: over(of(faces, 0, s, h * 1024, 1024), of(faces, 0, s, h * 1024 + 2048, 1024)))
    put(XC, 1024, lambda s: over(of(blocks, 1, s, 3072 * s, 1024), face_traces(s)))
    put(XD, 768, lambda s: over(packed(g, 0, s), packed(g, 1, s)))
    put(XH, 384, lambda s: halves(packed(r, 0, s)))
    put(XK, 256, lambda s: dot(over(packed(g, 2, s), packed(r, 1, s)).astype(BF16), trace_lanes(s)))
    put(XT, 512, lambda s: halves(of(tent, 0, s, 3072 * s, 1024)))


def pack_y_kernel(blocks, faces, tent, guess_packed, rhs_packed, x_even, x_odd, even, odd, low, high):
    first = parity("bx") == 0
    for start in range(0, XLEN, 128):
        a = x_even[:, start : start + 128].astype(F32)
        b = x_odd[:, start : start + 128].astype(F32)
        low[:, start : start + 128] = jnp.where(first, b, a).astype(BF16)
        high[:, start : start + 128] = jnp.where(first, a, b).astype(BF16)
    py = parity("by")
    is_first = py == 0

    def select(k, near=None, far=None, columns=64):
        r, j = iota((16, columns), 0), iota((16, columns), 1)
        high_side = jnp.where(r < 8, py, 1 - py) == 0
        iy = jnp.where(high_side, 7 - k, k)
        row = r % 8 - 2
        source = jnp.where((row >= 0) & (row < 4), row * 8 + iy, -1)
        if near is not None:
            source = jnp.where(row == -1, 32 + near + iy, jnp.where(row == 4, 48 + near + iy, source))
        if far is not None:
            source = jnp.where(row == -2, 32 + far + iy, jnp.where(row == 5, 48 + far + iy, source))
        return onehot(j == source)

    def put(start, value):
        even[:, start : start + value[0].shape[1]] = value[0].astype(BF16)
        odd[:, start : start + value[1].shape[1]] = value[1].astype(BF16)

    def both(make, picked):
        return make(picked[:8]), make(picked[8:])

    for ref, start, part in ((blocks, YA, XA), (faces, YB, XB)):
        cut = []
        for h in range(2):
            source = jnp.concatenate(
                [ref[:, h * 2048 : h * 2048 + 2048], low[:, part : part + 2048], high[:, part : part + 2048]], 0
            )
            cut.append(dot(select(0, 8 * h), source))
        put(start, (over(cut[0][:8], cut[1][:8]), over(cut[0][8:], cut[1][8:])))

    def by_side(minus, plus):
        up = jnp.where(is_first, plus[:8], minus[:8])
        down = jnp.where(is_first, minus[8:], plus[8:])
        return halves(up), halves(down)

    own1, own0 = select(1, columns=32), select(0, columns=32)

    def lanes(ref, pieces, width):
        return jnp.concatenate([ref[:, p : p + width] for p in pieces], 1)

    minus, plus = [i * 1024 for i in range(4)], [i * 1024 + 768 for i in range(4)]
    put(YC, by_side(dot(own1, lanes(blocks, minus, 256)), dot(own1, lanes(blocks, plus, 256))))
    put(YT, by_side(dot(own0, lanes(tent, minus, 256)), dot(own0, lanes(tent, plus, 256))))
    minus = [f * 1024 + i * 256 for f in range(4) for i in range(4)]
    plus = [p + 128 for p in minus]
    put(YF, by_side(dot(own1, lanes(faces, minus, 128)), dot(own1, lanes(faces, plus, 128))))
    own = guess_packed[...]
    rows = jnp.concatenate([own, low[:, XD : XD + 768], high[:, XD : XD + 768]], 0)
    g0, g1, g2 = dot(select(0, 0, 8), rows), dot(select(1, 0), rows), dot(select(2, columns=32), own)
    cut = []
    for h in range(2):
        rows = [rhs_packed[:, h * 384 : h * 384 + 384], low[:, XH : XH + 384], high[:, XH : XH + 384]]
        cut.append(dot(select(0, 8 * h), jnp.concatenate(rows, 0)))
    r0, r1 = jnp.concatenate(cut, 1), dot(own1, rhs_packed[...])
    put(YD, (over(g0[:8], g1[:8]), over(g0[8:], g1[8:])))
    put(YG, (over(g2[:8], r0[:8]), over(g2[8:], r0[8:])))
    put(YR, both(halves, r1))


def prolong_kernel(tent, t16, plus_y, minus_y, stage, t32):
    lane = iota((256, 128), 1)
    for k in range(4):
        for ph in range(8):
            chunk = tent[:, (ph * 4 + k) * 128 : (ph * 4 + k + 1) * 128].astype(F32)
            stage[k, pl.ds(ph, NE, stride=8), :] = chunk
    for k in range(4):
        both = stage[k]
        other = pltpu.roll(both, 64, 1)
        t32[pl.ds(2 * k, 256, stride=8), :] = jnp.where(lane < 64, both, other)
        t32[pl.ds(2 * k + 1, 256, stride=8), :] = jnp.where(lane < 64, other, both)
    t16[...] = t32[...].astype(BF16)
    sub = iota((8, 128), 0)
    for e in range(NE):
        plus, minus = [], []
        for h in range(2):
            base = e * 64 + 32 * h
            a, b = t32[base + 8 : base + 16, :], t32[base + 24 : base + 32, :]
            plus.append(jnp.where(sub < 4, pltpu.roll(a, 4, 0), b))
            a, b = t32[base : base + 8, :], t32[base + 16 : base + 24, :]
            minus.append(jnp.where(sub < 4, a, pltpu.roll(b, 4, 0)))
        plus_y[e * 16 : e * 16 + 16, :] = jnp.concatenate(plus, 0).astype(BF16)
        minus_y[e * 16 : e * 16 + 16, :] = jnp.concatenate(minus, 0).astype(BF16)


def operators(block_chunk, face_chunk, w, inverse, stage, fstage, w32):
    lane = iota((256, 128), 1)
    lane_e = iota((NE, 128), 1)
    diag = jnp.zeros((NE, 128), F32)
    for k in range(4):
        for ph in range(8):
            c = ph * 4 + k
            chunk = block_chunk(c)
            diag = diag + jnp.where((lane_e == 2 * c) | (lane_e == 65 + 2 * c), chunk, 0.0)
            stage[k, pl.ds(ph, NE, stride=8), :] = chunk
    diag = (diag + pltpu.roll(diag, 64, 1))[:, :64]
    inverse[...] = 1.0 / jnp.where(diag == 0.0, 1.0, diag)
    for f in range(4):
        for ph in range(8):
            fstage[f, pl.ds(ph, NE, stride=8), :] = face_chunk(f * 8 + ph)
    folded = jnp.concatenate([fstage[f].astype(BF16) for f in range(4)], 1)
    row, col = iota((512, 128), 0), iota((512, 128), 1)
    lo_of = (row // 16) % 8
    target = 64 + row // 128 * 16 + row % 16
    for k in range(4):
        both = stage[k]
        other = pltpu.roll(both, 64, 1)
        for s, part in enumerate((both, other)):
            p_lo = 2 * k + s
            coupled = dot(folded, onehot((col == target) & (lo_of == p_lo)))
            w32[pl.ds(p_lo, 256, stride=8), :] = jnp.where(lane < 64, part, coupled)
    w[...] = w32[...].astype(BF16)


def own_kernel(blocks, faces, w, inverse, *scratch):
    chunk = lambda ref: lambda c: ref[:, c * 128 : (c + 1) * 128].astype(F32)
    operators(chunk(blocks), chunk(faces), w, inverse, *scratch)


NOTHING = (8, 128)


def part(ref, start, c, half):
    row = 8 * (c // half)
    lane = start + (c % half) * 128
    return ref[:, lane : lane + 128].astype(F32)[row : row + 8]


def halo_x(low, high, w, inverse, *scratch):
    zero = jnp.zeros(NOTHING, F32)

    def block(c):
        far_low = part(low, XC, c - 24, 8) if c >= 24 else zero
        far_high = part(high, XC, c, 8) if c < 8 else zero
        return jnp.concatenate([part(low, XA, c, 16), far_low, part(high, XA, c, 16), far_high], 0)

    def face(c):
        f, ph = c // 8, c % 8
        far_low = part(low, XC, 8 + f * 2 + ph - 6, 8) if ph >= 6 else zero
        far_high = part(high, XC, 8 + f * 2 + ph, 8) if ph < 2 else zero
        return jnp.concatenate([part(low, XB, c, 16), far_low, part(high, XB, c, 16), far_high], 0)

    operators(block, face, w, inverse, *scratch)


def halo_y(even, odd, w, inverse, low, high, *scratch):
    first = parity("by") == 0
    for start in range(0, YLEN, 128):
        a = even[:, start : start + 128].astype(F32)
        b = odd[:, start : start + 128].astype(F32)
        low[:, start : start + 128] = jnp.where(first, b, a).astype(BF16)
        high[:, start : start + 128] = jnp.where(first, a, b).astype(BF16)
    zero = jnp.zeros(NOTHING, F32)

    def block(c):
        i, d = c // 8, c % 8
        far_low = part(low, YC, i * 2 + d - 6, 4) if d >= 6 else zero
        far_high = part(high, YC, i * 2 + d, 4) if d < 2 else zero
        return jnp.concatenate([part(low, YA, c, 16), far_low, part(high, YA, c, 16), far_high], 0)

    def face(c):
        f, ph = c // 8, c % 8
        i = ph // 2
        far_low = part(low, YF, f * 4 + i, 8) if ph % 2 == 1 else zero
        far_high = part(high, YF, f * 4 + i, 8) if ph % 2 == 0 else zero
        return jnp.concatenate([part(low, YB, c, 16), far_low, part(high, YB, c, 16), far_high], 0)

    operators(block, face, w, inverse, *scratch)


def factors(bounds):
    low, high = bounds[0:1, 0:1], bounds[0:1, 1:2]
    centre = 0.5 * (high + low)
    half_width = 0.5 * (high - low)
    spread = centre / half_width
    first = 1.0 / spread
    second = 1.0 / (2.0 * spread - first)
    third = 1.0 / (2.0 * spread - second)
    return centre, half_width, first, second, third


OWN = [((ix + 3) * 16 + iy, 0, ix * 8 + iy) for ix in range(EX) for iy in range(EY)]


def beside_x(k):
    return [((7 + k if s else 2 - k) * 16 + iy, 1, s * 16 + k * 8 + iy) for s in range(2) for iy in range(EY)]


def beside_y(k, rows):
    return [((r + 1) * 16 + (8 + k if s else 15 - k), 2, s * 16 + k * 8 + r) for s in range(2) for r in rows]


LEVELS = (
    (1, 9, OWN + beside_x(0) + beside_x(1) + beside_y(0, range(1, 7)) + beside_y(1, range(2, 6))),
    (2, 8, OWN + beside_x(0) + beside_y(0, range(2, 6))),
    (3, 7, OWN),
)


def smooth(guess, rhs, w, wx, wy, inv, inv_x, inv_y, bounds, x_low, x_high, y_low, y_high, smoothed,
           g_ref, r_ref, i_ref, t_ref, x_ref, a_ref):
    def joined(value):
        return value + pltpu.roll(value, 64, 1)

    def fill(ref, own, x_value, x_count, y_parts):
        ref[...] = jnp.zeros((SPAN, 128), F32)
        for n in range(NRHS):
            for ix in range(EX):
                row = n * EXT + (ix + 3) * 16
                ref[row : row + 8, 0:64] = own[n, ix * 8 : ix * 8 + 8, :]
            for side in range(2):
                for k in range(x_count):
                    row = n * EXT + (7 + k if side else 2 - k) * 16
                    ref[row : row + 8, :] = joined(x_value(side, k, n))
            for side, message in enumerate((y_low, y_high)):
                for k, (start, top, half) in enumerate(y_parts):
                    value = part(message, start, n, half) if half else (
                        message[:, start + n * 128 : start + n * 128 + 128].astype(F32)[8 * top : 8 * top + 8]
                    )
                    ref[pl.ds(n * EXT + 16 + (8 + k if side else 15 - k), 8, stride=16), :] = joined(value)

    x_messages = (x_low, x_high)
    spread = [lax.dot_general(m[:, XK : XK + 256], trace_lanes(1 - s), NT, preferred_element_type=F32)
              for s, m in enumerate(x_messages)]

    def whole(side, start, n):
        return x_messages[side][:, start + n * 128 : start + n * 128 + 128].astype(F32)

    def x_guess(side, k, n):
        if k == 2:
            return spread[side][0:8, n * 128 : n * 128 + 128]
        return whole(side, XD, n)[8 * k : 8 * k + 8]

    def x_rhs(side, k, n):
        return spread[side][8:16, n * 128 : n * 128 + 128] if k else part(x_messages[side], XH, n, 3)

    fill(g_ref, guess, x_guess, 3, ((YD, 0, 0), (YD, 1, 0), (YG, 0, 0)))
    fill(r_ref, rhs, x_rhs, 2, ((YG, 1, 0), (YR, 0, 3)))
    i_ref[...] = jnp.ones((EXT, 128), F32)
    wide = lambda value: jnp.concatenate([value, value], 1)
    for ix in range(EX):
        i_ref[(ix + 3) * 16 : (ix + 3) * 16 + 8, 0:64] = inv[ix * 8 : ix * 8 + 8, :]
    for s in range(2):
        for k in range(2):
            base = s * 16 + k * 8
            row = (7 + k if s else 2 - k) * 16
            i_ref[row : row + 8, 0:64] = inv_x[base : base + 8, :]
            i_ref[pl.ds(16 + (8 + k if s else 15 - k), 8, stride=16), :] = wide(inv_y[base : base + 8, :])
    x_ref[...] = jnp.zeros((8 * EXT, 128), F32)
    a_ref[...] = jnp.zeros((8 * EXT, 128), F32)
    lane = iota((16, 128), 1)
    tables = (w, wx, wy)

    def apply(level, v):
        first, last, elements = LEVELS[level]
        t_ref[...] = with_traces(v)
        for n in range(NRHS):
            for ri in range(first, last):
                row = n * EXT + ri * 16
                own = t_ref[row : row + 16, :]
                sides = jnp.where(
                    lane < 80,
                    t_ref[row - 16 : row, :],
                    jnp.where(
                        lane < 96,
                        t_ref[row + 16 : row + 32, :],
                        jnp.where(lane < 112, pltpu.roll(own, 1, 0), pltpu.roll(own, 15, 0)),
                    ),
                )
                x_ref[row : row + 16, :] = jnp.where(lane < 64, own, sides)
        for row, table, e in elements:
            hi, lo = split(x_ref[pl.ds(row, 8, stride=EXT), :])
            out = dot(over(hi, lo), tables[table][e * 64 : e * 64 + 64, :], NT)
            a_ref[pl.ds(row, 8, stride=EXT), 0:64] = out[:8] + out[8:]
        return a_ref[:SPAN, 0:64]

    centre, half_width, first, second, third = factors(bounds)
    inverse = jnp.concatenate([i_ref[:, 0:64]] * NRHS, 0)
    v = g_ref[:, 0:64]
    r = r_ref[:, 0:64] - apply(0, v)
    u = inverse * r / centre
    x = v + u
    for level, factor, new in ((1, first, second), (2, second, third)):
        r = r - apply(level, u)
        u = new * factor * u + (2.0 * new / half_width) * inverse * r
        x = x + u
    for n in range(NRHS):
        for ix in range(EX):
            row = n * EXT + (ix + 3) * 16
            smoothed[n, ix * 8 : ix * 8 + 8, :] = x[row : row + 8]


def ghost_rows(message, start, out):
    lane = iota((8, 128), 1)
    for j in range(8):
        both = part(message, start, j, 4)
        other = pltpu.roll(both, 64, 1)
        out[pl.ds(2 * j, 8, stride=16), :] = jnp.where(lane < 64, both, other)
        out[pl.ds(2 * j + 1, 8, stride=16), :] = jnp.where(lane < 64, other, both)


def label_masks(masks):
    lane = iota((16, 256), 1)
    for b in range(4):
        masks[b * 16 : b * 16 + 16, :] = onehot(lane // 64 == b)


def masked(masks, piece, label):
    mask = masks[pl.ds(pl.multiple_of(label * 16, 16), 16), :]
    return jnp.concatenate([piece, piece], 1) * jnp.concatenate([mask] * 4, 0)


def none(count):
    return jnp.zeros((count, 128), BF16)


def face_column(f, rows):
    return jnp.concatenate([none(64 + 16 * f), rows] + ([none(48 - 16 * f)] if f < 3 else []), 0)


def galerkin_kernel(labels, t16, plus_y, minus_y, w, local, edge_columns, tt, masks, big):
    label_masks(masks)
    lane128 = iota((64, 128), 1)
    for pair in range(NE // 2):
        turned = t16[pair * 128 : pair * 128 + 128, :].astype(F32).T[:64]
        first, second = labels[2 * pair], labels[2 * pair + 1]
        for a in range(4):
            keep = jnp.where(
                lane128 < 64,
                jnp.where(first == a, 1.0, 0.0),
                jnp.where(second == a, 1.0, 0.0),
            )
            tt[a * 64 : a * 64 + 64, pair * 128 : pair * 128 + 128] = (turned * keep).astype(BF16)
    edge_columns[0] = tt[:, :512]
    edge_columns[1] = tt[:, 1536:]
    for f in range(2):
        for ix in range(EX):
            start = (4 * ix + 3 * f) * 128
            edge_columns[2 + f, :, ix * 128 : ix * 128 + 128] = tt[:, start : start + 128]

    def row_of_elements(ix, carry):
        for iy in range(EY):
            e = ix * EY + iy
            own = pl.ds(pl.multiple_of(e * 64, 64), 64)
            before = pl.multiple_of(jnp.maximum(e - 8, 0) * 64, 64)
            after = pl.multiple_of(jnp.minimum(e + 8, 31) * 64, 64)
            rows = [
                t16[pl.ds(before + 48, 16), :],
                t16[pl.ds(after, 16), :],
            ]
            if iy > 0:
                rows.append(plus_y[pl.ds(pl.multiple_of((e - 1) * 16, 16), 16), :])
            else:
                rows.append(none(16))
            if iy < 7:
                rows.append(minus_y[pl.ds(pl.multiple_of((e + 1) * 16, 16), 16), :])
            columns = [jnp.concatenate([t16[own, :], none(64)], 0)]
            columns += [face_column(f, value) for f, value in enumerate(rows)]
            pieces = dot(w[own, :], jnp.concatenate(columns, 1)).astype(BF16)
            piece = lambda s: pieces[:, s * 128 : s * 128 + 128]
            big[0, own, :] = masked(masks, piece(0), labels[e])
            big[1, own, :] = masked(masks, piece(1), labels[jnp.maximum(e - 8, 0)])
            big[2, own, :] = masked(masks, piece(2), labels[jnp.minimum(e + 8, 31)])
            nothing = jnp.zeros((64, 256), BF16)
            big[3, own, :] = masked(masks, piece(3), labels[e - 1]) if iy > 0 else nothing
            big[4, own, :] = masked(masks, piece(4), labels[e + 1]) if iy < 7 else nothing
        return carry

    lax.fori_loop(0, EX, row_of_elements, 0)
    local[...] = (
        dot(tt[...], big[0])
        + dot(tt[:, 512:], big[1, 512:, :])
        + dot(tt[:, :1536], big[2, :1536, :])
        + dot(tt[...], big[3])
        + dot(tt[...], big[4])
    )


def ghost_block(face, message, start, first_row, elements, side_labels, label_start, w, columns, rows, masks, side, result):
    ghost_rows(message, start, rows)
    for i, (e, place) in enumerate(elements):
        near = rows[(i + first_row) * 16 : (i + first_row) * 16 + 16, :].astype(BF16)
        piece = dot(w[e * 64 : e * 64 + 64, :], face_column(face, near)).astype(BF16)
        side[place : place + 64, :] = masked(masks, piece, side_labels[label_start + i])
    result[...] = dot(columns, side[...])


def middle_kernel(side_labels, w, edge_columns, x_low, x_high, wx, inverse_x, ghost,
                  stage, fstage, w32, rows, masks, side, result, sems):
    label_masks(masks)
    copies = []
    for f, message in enumerate((x_low, x_high)):
        elements = [(24 * f + iy, iy * 64) for iy in range(EY)]
        ghost_block(f, message, XT, 0, elements, side_labels, 8 * f, w, edge_columns[f], rows, masks, side, result.at[f])
        copies.append(pltpu.make_async_copy(result.at[f], ghost.at[f], sems.at[f]))
        copies[-1].start()
    halo_x(x_low, x_high, wx, inverse_x, stage, fstage, w32)
    for copy in copies:
        copy.wait()


def finish_kernel(side_labels, guess, rhs, w, wx, inv, inv_x, bounds, x_low, x_high, y_even, y_odd, edge_columns, ghost_in,
                  smoothed, ghost, wy, inv_y, y_low, y_high, stage, fstage, w32, g_ref, r_ref, i_ref, t_ref, x_ref, a_ref,
                  rows, masks, side, result, sems):
    halo_y(y_even, y_odd, wy, inv_y, y_low, y_high, stage, fstage, w32)
    label_masks(masks)
    copies = []
    for f, message in enumerate((y_low, y_high)):
        side[...] = jnp.zeros((512, 256), BF16)
        elements = [(8 * ix + 7 * f, ix * 128 + 64 * f) for ix in range(EX)]
        ghost_block(2 + f, message, YT, 2, elements, side_labels, 16 + 4 * f, w, edge_columns[2 + f], rows, masks, side,
                    result.at[f])
        copies.append(pltpu.make_async_copy(result.at[f], ghost.at[2 + f], sems.at[f]))
        copies[-1].start()
    smooth(guess, rhs, w, wx, wy, inv, inv_x, inv_y, bounds, x_low, x_high, y_low, y_high, smoothed,
           g_ref, r_ref, i_ref, t_ref, x_ref, a_ref)
    for copy in copies:
        copy.wait()


def call(kernel, outs, scratch, operands, flops, moved, in_specs=None, out_specs=None, aliases=None):
    return pl.pallas_call(
        kernel,
        out_shape=outs,
        in_specs=in_specs or [VMEM] * len(operands),
        out_specs=out_specs or [VMEM] * len(outs),
        scratch_shapes=scratch,
        input_output_aliases=aliases or {},
        cost_estimate=pl.CostEstimate(flops=flops, bytes_accessed=moved, transcendentals=0),
        compiler_params=pltpu.CompilerParams(vmem_limit_bytes=48 * 1024 * 1024),
    )(*operands)


def exchange(messages, axis):
    out = []
    for first, message in enumerate(messages):
        pairs = []
        for i in range(first, lax.axis_size(axis) - 1, 2):
            pairs += [(i, i + 1), (i + 1, i)]
        out.append(lax.ppermute(message, axis, pairs))
    return out


def shaped(*shape, dtype=BF16):
    return jax.ShapeDtypeStruct(shape, dtype)


STAGES = [pltpu.VMEM((4, 256, 128), F32), pltpu.VMEM((4, 256, 128), F32), pltpu.VMEM((2048, 128), F32)]


GHOST = [
    pltpu.VMEM((128, 128), F32),
    pltpu.VMEM((64, 256), BF16),
    pltpu.VMEM((512, 256), BF16),
    pltpu.VMEM((2, 256, 256), F32),
    pltpu.SemaphoreType.DMA((2,)),
]


def on_device(blocks, faces, tentative, aggregate, ghost_labels, rhs, guess, bounds):
    wide = lambda *shape: shaped(*shape, dtype=F32)
    rhs = jnp.swapaxes(rhs[0, 0], 1, 2)
    guess = jnp.swapaxes(guess[0, 0], 1, 2)
    labels, side_labels = aggregate.reshape(NE), ghost_labels.reshape(24)
    even, odd, guess_packed, rhs_packed, blocks, faces, tentative, guess, rhs, bounds = call(
        pack_x_kernel,
        [shaped(16, XLEN)] * 2 + [shaped(NE, 768)] * 2 + [shaped(NE, 4096)] * 3
        + [wide(NRHS, NE, 64)] * 2 + [wide(1, 2)],
        [pltpu.SemaphoreType.DMA((6,))],
        [a.reshape(NE, 4096) for a in (blocks, faces, tentative)] + [guess, rhs, bounds.reshape(1, 2)],
        10**6, 2**20, [HBM] * 6,
    )
    even, odd = exchange((even, odd), "bx")
    w, inverse = call(own_kernel, [shaped(2048, 128), wide(NE, 64)], STAGES, (blocks, faces), 10**9, 2**20)
    t16, plus_y, minus_y = call(
        prolong_kernel, [shaped(2048, 128), shaped(512, 128), shaped(512, 128)],
        [STAGES[0], STAGES[2]], (tentative,), 5 * 10**8, 2**20,
    )
    local, edge_columns = call(
        galerkin_kernel,
        [wide(256, 256), shaped(4, 256, 512)],
        [pltpu.VMEM((256, 2048), BF16), GHOST[1], pltpu.VMEM((5, 2048, 256), BF16)],
        (labels, t16, plus_y, minus_y, w),
        4 * 10**9, 4 * 2**20, [SMEM] + [VMEM] * 4,
    )
    even, odd, x_low, x_high = call(
        pack_y_kernel, [shaped(16, YLEN)] * 2 + [shaped(16, XLEN)] * 2, [],
        (blocks, faces, tentative, guess_packed, rhs_packed, even, odd), 10**8, 2**20,
    )
    even, odd = exchange((even, odd), "by")
    wx, inverse_x, ghost = call(
        middle_kernel, [shaped(2048, 128), wide(NE, 64), wide(4, 256, 256)], STAGES + GHOST,
        (side_labels, w, edge_columns, x_low, x_high), 10**9, 2**20,
        [SMEM] + [VMEM] * 4, [VMEM, VMEM, HBM],
    )
    smoothed, ghost = call(
        finish_kernel, [wide(NRHS, NE, 64), wide(4, 256, 256)],
        [pltpu.VMEM((2048, 128), BF16), pltpu.VMEM((NE, 64), F32)] + [pltpu.VMEM((16, YLEN), BF16)] * 2
        + STAGES
        + [pltpu.VMEM((SPAN, 128), F32)] * 2
        + [pltpu.VMEM((EXT, 128), F32), pltpu.VMEM((SPAN, 128), F32)]
        + [pltpu.VMEM((8 * EXT, 128), F32)] * 2
        + GHOST,
        (side_labels, guess, rhs, w, wx, inverse, inverse_x, bounds, x_low, x_high, even, odd, edge_columns, ghost),
        10**9, 2**20, [SMEM] + [VMEM] * 12 + [HBM], [VMEM, HBM], {13: 1},
    )
    return jnp.swapaxes(smoothed, 1, 2)[None, None], local[None, None], ghost[None, None]


def solution(mesh):
    b = lambda extra: P("bx", "by", *([None] * extra))
    return jax.shard_map(
        on_device,
        mesh=mesh,
        in_specs=(b(2), b(2), b(2), b(1), b(1), b(3), b(3), P()),
        out_specs=(b(3), b(2), b(3)),
        check_vma=False,
    )
```

```python
import jax
import jax.numpy as jnp
from jax import lax
from jax.experimental import pallas as pl
from jax.experimental.pallas import tpu as pltpu
from jax.sharding import PartitionSpec as P

EX, EY, NE, NRHS = 4, 8, 32, 6
F32, BF16 = jnp.float32, jnp.bfloat16
VMEM = pl.BlockSpec(memory_space=pltpu.VMEM)
SMEM = pl.BlockSpec(memory_space=pltpu.SMEM)
HBM = pl.BlockSpec(memory_space=pltpu.HBM)
NT = (((1,), (1,)), ((), ()))
NN = (((1,), (0,)), ((), ()))

XA, XB = 0, 2048
XC = 4096
XD = 5120
XH = 5888
XK = 6272
XT = 6528
XLEN = 7040
YA, YB = 0, 2048
YF = 4096
YC = 5120
YD = 5632
YG = 6400
YR = 7168
YT = 7552
YLEN = 8064

EXT, SPAN = 160, 960


def dot(a, b, dims=NN):
    return lax.dot_general(a, b, dims, preferred_element_type=F32)


def iota(shape, dim):
    return lax.broadcasted_iota(jnp.int32, shape, dim)


def onehot(mask):
    return mask.astype(F32).astype(BF16)


def split(x):
    hi = x.astype(BF16)
    return hi, (x - hi.astype(F32)).astype(BF16)


def halves(x):
    lanes = x.shape[1] // 2
    return jnp.concatenate([x[:, :lanes], x[:, lanes:]], 0)


def over(a, b):
    return jnp.concatenate([a, b], 0)


def parity(axis):
    return lax.axis_index(axis) % 2


def with_traces(v):
    q, lane = iota((64, 128), 0), iota((64, 128), 1)
    t = lane % 16
    f = lane // 16 - 4
    along_y = 16 * (t // 4) + t % 4
    source = jnp.where(f == 0, 48 + t, jnp.where(f == 1, t, jnp.where(f == 2, along_y + 12, along_y)))
    pick = onehot(q == jnp.where(f < 0, lane, source))
    hi, lo = split(v)
    return dot(hi, pick) + dot(lo, pick)


def pack_lanes(v):
    hi, lo = split(v)
    q, lane = iota((64, 128), 0), iota((64, 128), 1)
    both = dot(hi, onehot(q == lane)) + dot(lo, onehot(q == lane - 64))
    return jnp.concatenate([both[n * NE : (n + 1) * NE] for n in range(NRHS)], 1)


def trace_lanes(side):
    row, lane = iota((768, 256), 0), iota((768, 256), 1)
    source = lane // 32 * 128 + lane // 16 % 2 * 64 + lane % 16 + 48 * side
    return onehot((row == source) & (lane < 192))


def pack_x_kernel(blocks_in, faces_in, tent_in, guess_in, rhs_in, even, odd, guess_packed, rhs_packed,
                  blocks, faces, tent, guess, rhs, sems):
    copies = [
        pltpu.make_async_copy(source, target, sems.at[i])
        for i, (source, target) in enumerate(
            ((guess_in, guess), (rhs_in, rhs), (blocks_in, blocks), (faces_in, faces), (tent_in, tent))
        )
    ]
    for copy in copies:
        copy.start()
    for copy in copies:
        copy.wait()
    g = pack_lanes(guess[...].reshape(NRHS * NE, 64))
    r = pack_lanes(rhs[...].reshape(NRHS * NE, 64))
    guess_packed[...] = g.astype(BF16)
    rhs_packed[...] = r.astype(BF16)
    first = parity("bx") == 0

    def put(start, lanes, make):
        low, high = make(0), make(1)
        even[:, start : start + lanes] = jnp.where(first, high, low).astype(BF16)
        odd[:, start : start + lanes] = jnp.where(first, low, high).astype(BF16)

    def rows(k, side):
        return 8 * k if side == 0 else 24 - 8 * k

    def of(ref, k, side, start, lanes):
        row = rows(k, side)
        base = row // 16 * 16
        return ref[base : base + 16, start : start + lanes].astype(F32)[row - base : row - base + 8]

    def packed(value, k, side):
        return value[rows(k, side) : rows(k, side) + 8]

    def face_traces(side):
        return jnp.concatenate([of(faces, 1, side, f * 1024 + 768 * side, 256) for f in range(4)], 1)

    for h in range(2):
        put(XA + h * 1024, 1024, lambda s: over(of(blocks, 0, s, h * 1024, 1024), of(blocks, 0, s, h * 1024 + 2048, 1024)))
        put(XB + h * 1024, 1024, lambda s: over(of(faces, 0, s, h * 1024, 1024), of(faces, 0, s, h * 1024 + 2048, 1024)))
    put(XC, 1024, lambda s: over(of(blocks, 1, s, 3072 * s, 1024), face_traces(s)))
    put(XD, 768, lambda s: over(packed(g, 0, s), packed(g, 1, s)))
    put(XH, 384, lambda s: halves(packed(r, 0, s)))
    put(XK, 256, lambda s: dot(over(packed(g, 2, s), packed(r, 1, s)).astype(BF16), trace_lanes(s)))
    put(XT, 512, lambda s: halves(of(tent, 0, s, 3072 * s, 1024)))


def pack_y_kernel(blocks, faces, tent, guess_packed, rhs_packed, x_even, x_odd, _, even, odd, low, high):
    first = parity("bx") == 0
    for start in range(0, XLEN, 128):
        a = x_even[:, start : start + 128].astype(F32)
        b = x_odd[:, start : start + 128].astype(F32)
        low[:, start : start + 128] = jnp.where(first, b, a).astype(BF16)
        high[:, start : start + 128] = jnp.where(first, a, b).astype(BF16)
    py = parity("by")
    is_first = py == 0

    def select(k, near=None, far=None, columns=64):
        r, j = iota((16, columns), 0), iota((16, columns), 1)
        high_side = jnp.where(r < 8, py, 1 - py) == 0
        iy = jnp.where(high_side, 7 - k, k)
        row = r % 8 - 2
        source = jnp.where((row >= 0) & (row < 4), row * 8 + iy, -1)
        if near is not None:
            source = jnp.where(row == -1, 32 + near + iy, jnp.where(row == 4, 48 + near + iy, source))
        if far is not None:
            source = jnp.where(row == -2, 32 + far + iy, jnp.where(row == 5, 48 + far + iy, source))
        return onehot(j == source)

    def put(start, value):
        even[:, start : start + value[0].shape[1]] = value[0].astype(BF16)
        odd[:, start : start + value[1].shape[1]] = value[1].astype(BF16)

    def both(make, picked):
        return make(picked[:8]), make(picked[8:])

    for ref, start, part in ((blocks, YA, XA), (faces, YB, XB)):
        cut = []
        for h in range(2):
            source = jnp.concatenate(
                [ref[:, h * 2048 : h * 2048 + 2048], low[:, part : part + 2048], high[:, part : part + 2048]], 0
            )
            cut.append(dot(select(0, 8 * h), source))
        put(start, (over(cut[0][:8], cut[1][:8]), over(cut[0][8:], cut[1][8:])))

    def by_side(minus, plus):
        up = jnp.where(is_first, plus[:8], minus[:8])
        down = jnp.where(is_first, minus[8:], plus[8:])
        return halves(up), halves(down)

    own1, own0 = select(1, columns=32), select(0, columns=32)

    def lanes(ref, pieces, width):
        return jnp.concatenate([ref[:, p : p + width] for p in pieces], 1)

    minus, plus = [i * 1024 for i in range(4)], [i * 1024 + 768 for i in range(4)]
    put(YC, by_side(dot(own1, lanes(blocks, minus, 256)), dot(own1, lanes(blocks, plus, 256))))
    put(YT, by_side(dot(own0, lanes(tent, minus, 256)), dot(own0, lanes(tent, plus, 256))))
    minus = [f * 1024 + i * 256 for f in range(4) for i in range(4)]
    plus = [p + 128 for p in minus]
    put(YF, by_side(dot(own1, lanes(faces, minus, 128)), dot(own1, lanes(faces, plus, 128))))
    own = guess_packed[...]
    rows = jnp.concatenate([own, low[:, XD : XD + 768], high[:, XD : XD + 768]], 0)
    g0, g1, g2 = dot(select(0, 0, 8), rows), dot(select(1, 0), rows), dot(select(2, columns=32), own)
    cut = []
    for h in range(2):
        rows = [rhs_packed[:, h * 384 : h * 384 + 384], low[:, XH : XH + 384], high[:, XH : XH + 384]]
        cut.append(dot(select(0, 8 * h), jnp.concatenate(rows, 0)))
    r0, r1 = jnp.concatenate(cut, 1), dot(own1, rhs_packed[...])
    put(YD, (over(g0[:8], g1[:8]), over(g0[8:], g1[8:])))
    put(YG, (over(g2[:8], r0[:8]), over(g2[8:], r0[8:])))
    put(YR, both(halves, r1))


def prolong_kernel(tent, t16, plus_y, minus_y, stage, t32):
    lane = iota((256, 128), 1)
    for k in range(4):
        for ph in range(8):
            chunk = tent[:, (ph * 4 + k) * 128 : (ph * 4 + k + 1) * 128].astype(F32)
            stage[k, pl.ds(ph, NE, stride=8), :] = chunk
    for k in range(4):
        both = stage[k]
        other = pltpu.roll(both, 64, 1)
        t32[pl.ds(2 * k, 256, stride=8), :] = jnp.where(lane < 64, both, other)
        t32[pl.ds(2 * k + 1, 256, stride=8), :] = jnp.where(lane < 64, other, both)
    t16[...] = t32[...].astype(BF16)
    sub = iota((8, 128), 0)
    for e in range(NE):
        plus, minus = [], []
        for h in range(2):
            base = e * 64 + 32 * h
            a, b = t32[base + 8 : base + 16, :], t32[base + 24 : base + 32, :]
            plus.append(jnp.where(sub < 4, pltpu.roll(a, 4, 0), b))
            a, b = t32[base : base + 8, :], t32[base + 16 : base + 24, :]
            minus.append(jnp.where(sub < 4, a, pltpu.roll(b, 4, 0)))
        plus_y[e * 16 : e * 16 + 16, :] = jnp.concatenate(plus, 0).astype(BF16)
        minus_y[e * 16 : e * 16 + 16, :] = jnp.concatenate(minus, 0).astype(BF16)


def operators(block_chunk, face_chunk, w, inverse, stage, fstage, w32):
    lane = iota((256, 128), 1)
    lane_e = iota((NE, 128), 1)
    diag = jnp.zeros((NE, 128), F32)
    for k in range(4):
        for ph in range(8):
            c = ph * 4 + k
            chunk = block_chunk(c)
            diag = diag + jnp.where((lane_e == 2 * c) | (lane_e == 65 + 2 * c), chunk, 0.0)
            stage[k, pl.ds(ph, NE, stride=8), :] = chunk
    diag = (diag + pltpu.roll(diag, 64, 1))[:, :64]
    inverse[...] = 1.0 / jnp.where(diag == 0.0, 1.0, diag)
    for f in range(4):
        for ph in range(8):
            fstage[f, pl.ds(ph, NE, stride=8), :] = face_chunk(f * 8 + ph)
    folded = jnp.concatenate([fstage[f].astype(BF16) for f in range(4)], 1)
    row, col = iota((512, 128), 0), iota((512, 128), 1)
    lo_of = (row // 16) % 8
    target = 64 + row // 128 * 16 + row % 16
    for k in range(4):
        both = stage[k]
        other = pltpu.roll(both, 64, 1)
        for s, part in enumerate((both, other)):
            p_lo = 2 * k + s
            coupled = dot(folded, onehot((col == target) & (lo_of == p_lo)))
            w32[pl.ds(p_lo, 256, stride=8), :] = jnp.where(lane < 64, part, coupled)
    w[...] = w32[...].astype(BF16)


def own_kernel(blocks, faces, bounds, w, inverse, coefficients, *scratch):
    coefficients[...] = jnp.concatenate([jnp.broadcast_to(c, (1, 128)) for c in factors(bounds)] + [jnp.zeros((3, 128), F32)], 0)
    chunk = lambda ref: lambda c: ref[:, c * 128 : (c + 1) * 128].astype(F32)
    operators(chunk(blocks), chunk(faces), w, inverse, *scratch)


NOTHING = (8, 128)


def part(ref, start, c, half):
    row = 8 * (c // half)
    lane = start + (c % half) * 128
    return ref[:, lane : lane + 128].astype(F32)[row : row + 8]


def halo_x(low, high, w, inverse, *scratch):
    zero = jnp.zeros(NOTHING, F32)

    def block(c):
        far_low = part(low, XC, c - 24, 8) if c >= 24 else zero
        far_high = part(high, XC, c, 8) if c < 8 else zero
        return jnp.concatenate([part(low, XA, c, 16), far_low, part(high, XA, c, 16), far_high], 0)

    def face(c):
        f, ph = c // 8, c % 8
        far_low = part(low, XC, 8 + f * 2 + ph - 6, 8) if ph >= 6 else zero
        far_high = part(high, XC, 8 + f * 2 + ph, 8) if ph < 2 else zero
        return jnp.concatenate([part(low, XB, c, 16), far_low, part(high, XB, c, 16), far_high], 0)

    operators(block, face, w, inverse, *scratch)


def halo_y(even, odd, w, inverse, low, high, *scratch):
    first = parity("by") == 0
    for start in range(0, YLEN, 128):
        a = even[:, start : start + 128].astype(F32)
        b = odd[:, start : start + 128].astype(F32)
        low[:, start : start + 128] = jnp.where(first, b, a).astype(BF16)
        high[:, start : start + 128] = jnp.where(first, a, b).astype(BF16)
    zero = jnp.zeros(NOTHING, F32)

    def block(c):
        i, d = c // 8, c % 8
        far_low = part(low, YC, i * 2 + d - 6, 4) if d >= 6 else zero
        far_high = part(high, YC, i * 2 + d, 4) if d < 2 else zero
        return jnp.concatenate([part(low, YA, c, 16), far_low, part(high, YA, c, 16), far_high], 0)

    def face(c):
        f, ph = c // 8, c % 8
        i = ph // 2
        far_low = part(low, YF, f * 4 + i, 8) if ph % 2 == 1 else zero
        far_high = part(high, YF, f * 4 + i, 8) if ph % 2 == 0 else zero
        return jnp.concatenate([part(low, YB, c, 16), far_low, part(high, YB, c, 16), far_high], 0)

    operators(block, face, w, inverse, *scratch)


def factors(bounds):
    low, high = bounds[0:1, 0:1], bounds[0:1, 1:2]
    centre = 0.5 * (high + low)
    half_width = 0.5 * (high - low)
    spread = centre / half_width
    first = 1.0 / spread
    second = 1.0 / (2.0 * spread - first)
    third = 1.0 / (2.0 * spread - second)
    return centre, half_width, first, second, third


OWN = [((ix + 3) * 16 + iy, 0, ix * 8 + iy) for ix in range(EX) for iy in range(EY)]


def beside_x(k):
    return [((7 + k if s else 2 - k) * 16 + iy, 1, s * 16 + k * 8 + iy) for s in range(2) for iy in range(EY)]


def beside_y(k, rows):
    return [((r + 1) * 16 + (8 + k if s else 15 - k), 2, s * 16 + k * 8 + r) for s in range(2) for r in rows]


LEVELS = (
    (1, 9, OWN + beside_x(0) + beside_x(1) + beside_y(0, range(1, 7)) + beside_y(1, range(2, 6))),
    (2, 8, OWN + beside_x(0) + beside_y(0, range(2, 6))),
    (3, 7, OWN),
)


def smooth(guess, rhs, w, wx, wy, inv, inv_x, inv_y, coefficients, x_low, x_high, y_low, y_high, smoothed,
           g_ref, r_ref, i_ref, t_ref, x_ref, a_ref):
    def joined(value):
        return value + pltpu.roll(value, 64, 1)

    def fill(ref, own, x_value, x_count, y_parts):
        ref[...] = jnp.zeros((SPAN, 128), F32)
        for n in range(NRHS):
            for ix in range(EX):
                row = n * EXT + (ix + 3) * 16
                ref[row : row + 8, 0:64] = own[n, ix * 8 : ix * 8 + 8, :]
            for side in range(2):
                for k in range(x_count):
                    row = n * EXT + (7 + k if side else 2 - k) * 16
                    ref[row : row + 8, :] = joined(x_value(side, k, n))
            for side, message in enumerate((y_low, y_high)):
                for k, (start, top, half) in enumerate(y_parts):
                    value = part(message, start, n, half) if half else (
                        message[:, start + n * 128 : start + n * 128 + 128].astype(F32)[8 * top : 8 * top + 8]
                    )
                    ref[pl.ds(n * EXT + 16 + (8 + k if side else 15 - k), 8, stride=16), :] = joined(value)

    x_messages = (x_low, x_high)
    spread = [lax.dot_general(m[:, XK : XK + 256], trace_lanes(1 - s), NT, preferred_element_type=F32)
              for s, m in enumerate(x_messages)]

    def whole(side, start, n):
        return x_messages[side][:, start + n * 128 : start + n * 128 + 128].astype(F32)

    def x_guess(side, k, n):
        if k == 2:
            return spread[side][0:8, n * 128 : n * 128 + 128]
        return whole(side, XD, n)[8 * k : 8 * k + 8]

    def x_rhs(side, k, n):
        return spread[side][8:16, n * 128 : n * 128 + 128] if k else part(x_messages[side], XH, n, 3)

    fill(g_ref, guess, x_guess, 3, ((YD, 0, 0), (YD, 1, 0), (YG, 0, 0)))
    fill(r_ref, rhs, x_rhs, 2, ((YG, 1, 0), (YR, 0, 3)))
    i_ref[...] = jnp.ones((EXT, 128), F32)
    wide = lambda value: jnp.concatenate([value, value], 1)
    for ix in range(EX):
        i_ref[(ix + 3) * 16 : (ix + 3) * 16 + 8, 0:64] = inv[ix * 8 : ix * 8 + 8, :]
    for s in range(2):
        for k in range(2):
            base = s * 16 + k * 8
            row = (7 + k if s else 2 - k) * 16
            i_ref[row : row + 8, 0:64] = inv_x[base : base + 8, :]
            i_ref[pl.ds(16 + (8 + k if s else 15 - k), 8, stride=16), :] = wide(inv_y[base : base + 8, :])
    x_ref[...] = jnp.zeros((8 * EXT, 128), F32)
    a_ref[...] = jnp.zeros((8 * EXT, 128), F32)
    lane = iota((16, 128), 1)
    tables = (w, wx, wy)

    def apply(level, v):
        first, last, elements = LEVELS[level]
        t_ref[...] = with_traces(v)
        for n in range(NRHS):
            for ri in range(first, last):
                row = n * EXT + ri * 16
                own = t_ref[row : row + 16, :]
                sides = jnp.where(
                    lane < 80,
                    t_ref[row - 16 : row, :],
                    jnp.where(
                        lane < 96,
                        t_ref[row + 16 : row + 32, :],
                        jnp.where(lane < 112, pltpu.roll(own, 1, 0), pltpu.roll(own, 15, 0)),
                    ),
                )
                x_ref[row : row + 16, :] = jnp.where(lane < 64, own, sides)
        for row, table, e in elements:
            hi, lo = split(x_ref[pl.ds(row, 8, stride=EXT), :])
            out = dot(over(hi, lo), tables[table][e * 64 : e * 64 + 64, :], NT)
            a_ref[pl.ds(row, 8, stride=EXT), 0:64] = out[:8] + out[8:]
        return a_ref[:SPAN, 0:64]

    centre, half_width, first, second, third = [coefficients[i : i + 1, 0:64] for i in range(5)]
    inverse = jnp.concatenate([i_ref[:, 0:64]] * NRHS, 0)
    v = g_ref[:, 0:64]
    r = r_ref[:, 0:64] - apply(0, v)
    u = inverse * r / centre
    x = v + u
    for level, factor, new in ((1, first, second), (2, second, third)):
        r = r - apply(level, u)
        u = new * factor * u + (2.0 * new / half_width) * inverse * r
        x = x + u
    for n in range(NRHS):
        for ix in range(EX):
            row = n * EXT + (ix + 3) * 16
            smoothed[n, ix * 8 : ix * 8 + 8, :] = x[row : row + 8]


def ghost_rows(message, start, out):
    lane = iota((8, 128), 1)
    for j in range(8):
        both = part(message, start, j, 4)
        other = pltpu.roll(both, 64, 1)
        out[pl.ds(2 * j, 8, stride=16), :] = jnp.where(lane < 64, both, other)
        out[pl.ds(2 * j + 1, 8, stride=16), :] = jnp.where(lane < 64, other, both)


def label_masks(masks):
    lane = iota((16, 256), 1)
    for b in range(4):
        masks[b * 16 : b * 16 + 16, :] = onehot(lane // 64 == b)


def masked(masks, piece, label):
    mask = masks[pl.ds(pl.multiple_of(label * 16, 16), 16), :]
    return jnp.concatenate([piece, piece], 1) * jnp.concatenate([mask] * 4, 0)


def none(count):
    return jnp.zeros((count, 128), BF16)


def face_column(f, rows):
    return jnp.concatenate([none(64 + 16 * f), rows] + ([none(48 - 16 * f)] if f < 3 else []), 0)


def galerkin_kernel(labels, t16, plus_y, minus_y, w, local, edge_columns, tt, masks, big):
    label_masks(masks)
    lane128 = iota((64, 128), 1)
    for pair in range(NE // 2):
        turned = t16[pair * 128 : pair * 128 + 128, :].astype(F32).T[:64]
        first, second = labels[2 * pair], labels[2 * pair + 1]
        for a in range(4):
            keep = jnp.where(
                lane128 < 64,
                jnp.where(first == a, 1.0, 0.0),
                jnp.where(second == a, 1.0, 0.0),
            )
            tt[a * 64 : a * 64 + 64, pair * 128 : pair * 128 + 128] = (turned * keep).astype(BF16)
    edge_columns[0] = tt[:, :512]
    edge_columns[1] = tt[:, 1536:]
    for f in range(2):
        for ix in range(EX):
            start = (4 * ix + 3 * f) * 128
            edge_columns[2 + f, :, ix * 128 : ix * 128 + 128] = tt[:, start : start + 128]

    def row_of_elements(ix, carry):
        for iy in range(EY):
            e = ix * EY + iy
            own = pl.ds(pl.multiple_of(e * 64, 64), 64)
            before = pl.multiple_of(jnp.maximum(e - 8, 0) * 64, 64)
            after = pl.multiple_of(jnp.minimum(e + 8, 31) * 64, 64)
            rows = [
                t16[pl.ds(before + 48, 16), :],
                t16[pl.ds(after, 16), :],
            ]
            if iy > 0:
                rows.append(plus_y[pl.ds(pl.multiple_of((e - 1) * 16, 16), 16), :])
            else:
                rows.append(none(16))
            if iy < 7:
                rows.append(minus_y[pl.ds(pl.multiple_of((e + 1) * 16, 16), 16), :])
            columns = [jnp.concatenate([t16[own, :], none(64)], 0)]
            columns += [face_column(f, value) for f, value in enumerate(rows)]
            pieces = dot(w[own, :], jnp.concatenate(columns, 1)).astype(BF16)
            piece = lambda s: pieces[:, s * 128 : s * 128 + 128]
            big[0, own, :] = masked(masks, piece(0), labels[e])
            big[1, own, :] = masked(masks, piece(1), labels[jnp.maximum(e - 8, 0)])
            big[2, own, :] = masked(masks, piece(2), labels[jnp.minimum(e + 8, 31)])
            nothing = jnp.zeros((64, 256), BF16)
            big[3, own, :] = masked(masks, piece(3), labels[e - 1]) if iy > 0 else nothing
            big[4, own, :] = masked(masks, piece(4), labels[e + 1]) if iy < 7 else nothing
        return carry

    lax.fori_loop(0, EX, row_of_elements, 0)
    local[...] = (
        dot(tt[...], big[0])
        + dot(tt[:, 512:], big[1, 512:, :])
        + dot(tt[:, :1536], big[2, :1536, :])
        + dot(tt[...], big[3])
        + dot(tt[...], big[4])
    )


def ghost_block(face, message, start, first_row, elements, side_labels, label_start, w, columns, rows, masks, side, result):
    ghost_rows(message, start, rows)
    for i, (e, place) in enumerate(elements):
        near = rows[(i + first_row) * 16 : (i + first_row) * 16 + 16, :].astype(BF16)
        piece = dot(w[e * 64 : e * 64 + 64, :], face_column(face, near)).astype(BF16)
        side[place : place + 64, :] = masked(masks, piece, side_labels[label_start + i])
    result[...] = dot(columns, side[...])


def middle_kernel(side_labels, w, edge_columns, x_low, x_high, wx, inverse_x, ghost,
                  stage, fstage, w32, rows, masks, side, result, sems):
    label_masks(masks)
    copies = []
    for f, message in enumerate((x_low, x_high)):
        elements = [(24 * f + iy, iy * 64) for iy in range(EY)]
        ghost_block(f, message, XT, 0, elements, side_labels, 8 * f, w, edge_columns[f], rows, masks, side, result.at[f])
        copies.append(pltpu.make_async_copy(result.at[f], ghost.at[f], sems.at[f]))
        copies[-1].start()
    halo_x(x_low, x_high, wx, inverse_x, stage, fstage, w32)
    for copy in copies:
        copy.wait()


def finish_kernel(side_labels, guess, rhs, w, wx, inv, inv_x, coefficients, x_low, x_high, y_even, y_odd, edge_columns, ghost_in,
                  smoothed, ghost, wy, inv_y, y_low, y_high, stage, fstage, w32, g_ref, r_ref, i_ref, t_ref, x_ref, a_ref,
                  rows, masks, side, result, sems):
    halo_y(y_even, y_odd, wy, inv_y, y_low, y_high, stage, fstage, w32)
    label_masks(masks)
    copies = []
    for f, message in enumerate((y_low, y_high)):
        side[...] = jnp.zeros((512, 256), BF16)
        elements = [(8 * ix + 7 * f, ix * 128 + 64 * f) for ix in range(EX)]
        ghost_block(2 + f, message, YT, 2, elements, side_labels, 16 + 4 * f, w, edge_columns[2 + f], rows, masks, side,
                    result.at[f])
        copies.append(pltpu.make_async_copy(result.at[f], ghost.at[2 + f], sems.at[f]))
        copies[-1].start()
    smooth(guess, rhs, w, wx, wy, inv, inv_x, inv_y, coefficients, x_low, x_high, y_low, y_high, smoothed,
           g_ref, r_ref, i_ref, t_ref, x_ref, a_ref)
    for copy in copies:
        copy.wait()


def call(kernel, outs, scratch, operands, flops, moved, in_specs=None, out_specs=None, aliases=None, room=48):
    return pl.pallas_call(
        kernel,
        out_shape=outs,
        in_specs=in_specs or [VMEM] * len(operands),
        out_specs=out_specs or [VMEM] * len(outs),
        scratch_shapes=scratch,
        input_output_aliases=aliases or {},
        cost_estimate=pl.CostEstimate(flops=flops, bytes_accessed=moved, transcendentals=0),
        compiler_params=pltpu.CompilerParams(vmem_limit_bytes=room * 1024 * 1024),
    )(*operands)


def exchange(messages, axis):
    out = []
    for first, message in enumerate(messages):
        pairs = []
        for i in range(first, lax.axis_size(axis) - 1, 2):
            pairs += [(i, i + 1), (i + 1, i)]
        out.append(lax.ppermute(message, axis, pairs))
    return out


def shaped(*shape, dtype=BF16):
    return jax.ShapeDtypeStruct(shape, dtype)


STAGES = [pltpu.VMEM((4, 256, 128), F32), pltpu.VMEM((4, 256, 128), F32), pltpu.VMEM((2048, 128), F32)]


GHOST = [
    pltpu.VMEM((128, 128), F32),
    pltpu.VMEM((64, 256), BF16),
    pltpu.VMEM((512, 256), BF16),
    pltpu.VMEM((2, 256, 256), F32),
    pltpu.SemaphoreType.DMA((2,)),
]


def on_device(blocks, faces, tentative, aggregate, ghost_labels, rhs, guess, bounds):
    wide = lambda *shape: shaped(*shape, dtype=F32)
    rhs = jnp.swapaxes(rhs[0, 0], 1, 2)
    guess = jnp.swapaxes(guess[0, 0], 1, 2)
    labels, side_labels = aggregate.reshape(NE), ghost_labels.reshape(24)
    blocks, faces, tentative = [a.reshape(NE, 4096) for a in (blocks, faces, tentative)]
    even, odd, guess_packed, rhs_packed = call(
        pack_x_kernel, [shaped(16, XLEN)] * 2 + [shaped(NE, 768)] * 2,
        [pltpu.VMEM((NE, 4096), BF16)] * 3 + [pltpu.VMEM((NRHS, NE, 64), F32)] * 2 + [pltpu.SemaphoreType.DMA((5,))],
        (blocks, faces, tentative, guess, rhs), 10**6, 2**20, [HBM] * 5, room=62,
    )
    even, odd = exchange((even, odd), "bx")
    w, inverse, coefficients = call(
        own_kernel, [shaped(2048, 128), wide(NE, 64), wide(8, 128)], STAGES,
        (blocks, faces, bounds.reshape(1, 2)), 10**9, 2**20,
    )
    t16, plus_y, minus_y = call(
        prolong_kernel, [shaped(2048, 128), shaped(512, 128), shaped(512, 128)],
        [STAGES[0], STAGES[2]], (tentative,), 5 * 10**8, 2**20,
    )
    local, edge_columns = call(
        galerkin_kernel,
        [wide(256, 256), shaped(4, 256, 512)],
        [pltpu.VMEM((256, 2048), BF16), GHOST[1], pltpu.VMEM((5, 2048, 256), BF16)],
        (labels, t16, plus_y, minus_y, w),
        4 * 10**9, 4 * 2**20, [SMEM] + [VMEM] * 4,
    )
    even, odd, x_low, x_high = call(
        pack_y_kernel, [shaped(16, YLEN)] * 2 + [shaped(16, XLEN)] * 2, [],
        (blocks, faces, tentative, guess_packed, rhs_packed, even, odd, edge_columns), 10**8, 2**20,
        [VMEM] * 7 + [pl.BlockSpec(memory_space=pl.ANY)],
    )
    even, odd = exchange((even, odd), "by")
    wx, inverse_x, ghost = call(
        middle_kernel, [shaped(2048, 128), wide(NE, 64), wide(4, 256, 256)], STAGES + GHOST,
        (side_labels, w, edge_columns, x_low, x_high), 10**9, 2**20,
        [SMEM] + [VMEM] * 4, [VMEM, VMEM, HBM],
    )
    smoothed, ghost = call(
        finish_kernel, [wide(NRHS, NE, 64), wide(4, 256, 256)],
        [pltpu.VMEM((2048, 128), BF16), pltpu.VMEM((NE, 64), F32)] + [pltpu.VMEM((16, YLEN), BF16)] * 2
        + STAGES
        + [pltpu.VMEM((SPAN, 128), F32)] * 2
        + [pltpu.VMEM((EXT, 128), F32), pltpu.VMEM((SPAN, 128), F32)]
        + [pltpu.VMEM((8 * EXT, 128), F32)] * 2
        + GHOST,
        (side_labels, guess, rhs, w, wx, inverse, inverse_x, coefficients, x_low, x_high, even, odd, edge_columns, ghost),
        10**9, 2**20, [SMEM] + [VMEM] * 12 + [HBM], [VMEM, HBM], {13: 1},
    )
    return jnp.swapaxes(smoothed, 1, 2)[None, None], local[None, None], ghost[None, None]


def solution(mesh):
    b = lambda extra: P("bx", "by", *([None] * extra))
    return jax.shard_map(
        on_device,
        mesh=mesh,
        in_specs=(b(2), b(2), b(2), b(1), b(1), b(3), b(3), P()),
        out_specs=(b(3), b(2), b(3)),
        check_vma=False,
    )
```

```python
import jax
import jax.numpy as jnp
from jax import lax
from jax.experimental import pallas as pl
from jax.experimental.pallas import tpu as pltpu
from jax.sharding import PartitionSpec as P

EX, EY, NE, NRHS = 4, 8, 32, 6
F32, BF16 = jnp.float32, jnp.bfloat16
VMEM = pl.BlockSpec(memory_space=pltpu.VMEM)
SMEM = pl.BlockSpec(memory_space=pltpu.SMEM)
HBM = pl.BlockSpec(memory_space=pltpu.HBM)
ANY = pl.BlockSpec(memory_space=pl.ANY)
NT = (((1,), (1,)), ((), ()))
NN = (((1,), (0,)), ((), ()))

XA = 0
XB = 512
XC = 2560
XD = 3072
XH = 3840
XK = 4224
XT = 4480
XE = 4992
XLEN = 5120
YA, YB = 0, 512
YF = 2560
YD = 3584
YG = 4352
YR = 5120
YT = 5504
YE = 6016
YLEN = 6144

EXT, SPAN = 160, 960


def dot(a, b, dims=NN):
    return lax.dot_general(a, b, dims, preferred_element_type=F32)


def iota(shape, dim):
    return lax.broadcasted_iota(jnp.int32, shape, dim)


def onehot(mask):
    return mask.astype(F32).astype(BF16)


def split(x):
    hi = x.astype(BF16)
    return hi, (x - hi.astype(F32)).astype(BF16)


def halves(x):
    lanes = x.shape[1] // 2
    return jnp.concatenate([x[:, :lanes], x[:, lanes:]], 0)


def over(a, b):
    return jnp.concatenate([a, b], 0)


def parity(axis):
    return lax.axis_index(axis) % 2


def with_traces(v):
    q, lane = iota((64, 128), 0), iota((64, 128), 1)
    t = lane % 16
    f = lane // 16 - 4
    along_y = 16 * (t // 4) + t % 4
    source = jnp.where(f == 0, 48 + t, jnp.where(f == 1, t, jnp.where(f == 2, along_y + 12, along_y)))
    pick = onehot(q == jnp.where(f < 0, lane, source))
    hi, lo = split(v)
    return dot(hi, pick) + dot(lo, pick)


def by_element(rows):
    return jnp.concatenate([rows[n * NE : (n + 1) * NE] for n in range(NRHS)], 1)


def pack_lanes(v):
    hi, lo = split(v)
    q, lane = iota((64, 128), 0), iota((64, 128), 1)
    return by_element(dot(hi, onehot(q == lane)) + dot(lo, onehot(q == lane - 64)))


def pack_traces(traces):
    hi, lo = split(traces)
    lane = iota(traces.shape, 1)
    return by_element(jnp.where(lane >= 64, hi.astype(F32), pltpu.roll(lo.astype(F32), 64, 1)))


def squeeze(value, offset):
    lane = iota((8, 128), 1) % 64
    keep = (lane >= offset) & (lane < offset + 16)
    tiles = []
    for first in (0, 4):
        total = jnp.zeros((8, 128), F32)
        for j, n in enumerate(range(first, min(first + 4, NRHS))):
            one = jnp.where(keep, value[:, n * 128 : n * 128 + 128], 0.0)
            total = total + pltpu.roll(one, (16 * j - offset) % 128, 1)
        tiles.append(total)
    return jnp.concatenate(tiles, 1)


def unsqueeze(tiles, n, offset):
    lane = iota((8, 128), 1) % 64
    tile = tiles[:, n // 4 * 128 : n // 4 * 128 + 128]
    moved = pltpu.roll(tile, (offset - 16 * (n % 4)) % 128, 1)
    return jnp.where((lane >= offset) & (lane < offset + 16), moved, 0.0)


TRACE_OFFSET, VALUE_OFFSET = (16, 0), (0, 48)


def pack_x_kernel(blocks_in, faces_in, tent_in, guess_in, rhs_in, even, odd, traces_packed, b_packed, b_out, diagonal,
                  blocks, faces, tent, guess, rhs, stage, w32, w16, x_ref, a_ref, sems):
    copies = [
        pltpu.make_async_copy(source, target, sems.at[i])
        for i, (source, target) in enumerate(
            ((guess_in, guess), (blocks_in, blocks), (rhs_in, rhs), (faces_in, faces), (tent_in, tent))
        )
    ]
    for copy in copies:
        copy.start()
    copies[0].wait()
    v = guess[...].reshape(NRHS * NE, 64)
    traces = with_traces(v)
    t = pack_traces(traces)
    traces_packed[...] = t.astype(BF16)
    x_ref[0:192, :] = traces
    x_ref[192:256, :] = jnp.zeros((64, 128), F32)
    copies[1].wait()
    diag = stage_blocks(lambda c: blocks[:, c * 128 : (c + 1) * 128].astype(F32), stage)
    diag = diag + pltpu.roll(diag, 64, 1)
    diagonal[...] = diag.astype(BF16)
    for k in range(4):
        both = stage[k]
        w32[pl.ds(2 * k, 256, stride=8), :] = both
        w32[pl.ds(2 * k + 1, 256, stride=8), :] = pltpu.roll(both, 64, 1)
    w16[...] = w32[...].astype(BF16)
    lane8 = iota((8, 128), 1)
    for e in range(NE):
        hi, lo = split(jnp.where(lane8 < 64, x_ref[pl.ds(e, 8, stride=NE), :], 0.0))
        out = dot(over(hi, lo), w16[e * 64 : e * 64 + 64, :], NT)
        a_ref[pl.ds(e, 8, stride=NE), 0:64] = out[:8] + out[8:]
    for copy in copies[2:]:
        copy.wait()
    b = rhs[...].reshape(NRHS * NE, 64) - a_ref[0:192, 0:64]
    b_out[...] = b
    r = pack_lanes(b)
    b_packed[...] = r.astype(BF16)
    first = parity("bx") == 0

    def put(start, lanes, make):
        low, high = make(0), make(1)
        even[:, start : start + lanes] = jnp.where(first, high, low).astype(BF16)
        odd[:, start : start + lanes] = jnp.where(first, low, high).astype(BF16)

    def rows(k, side):
        return 8 * k if side == 0 else 24 - 8 * k

    def of(ref, k, side, start, lanes):
        row = rows(k, side)
        base = row // 16 * 16
        return ref[base : base + 16, start : start + lanes].astype(F32)[row - base : row - base + 8]

    def packed(value, k, side):
        return value[rows(k, side) : rows(k, side) + 8]

    def face_traces(side):
        return jnp.concatenate([of(faces, 1, side, f * 1024 + 768 * side, 256) for f in range(4)], 1)

    put(XA, 512, lambda s: halves(of(blocks, 0, s, 3072 * s, 1024)))
    for h in range(2):
        put(XB + h * 1024, 1024, lambda s: over(of(faces, 0, s, h * 1024, 1024), of(faces, 0, s, h * 1024 + 2048, 1024)))
    put(XC, 512, lambda s: halves(face_traces(s)))
    put(XD, 768, lambda s: over(packed(t, 0, s), packed(t, 1, s)))
    put(XH, 384, lambda s: halves(packed(r, 0, s)))
    put(XK, 256, lambda s: over(squeeze(packed(t, 2, s), TRACE_OFFSET[s]), squeeze(packed(r, 1, s), VALUE_OFFSET[s])))
    put(XT, 512, lambda s: halves(of(tent, 0, s, 3072 * s, 1024)))
    put(XE, 128, lambda s: over(packed(diag, 0, s), packed(diag, 1, s)))


def pack_y_kernel(blocks, faces, tent, traces_packed, b_packed, diagonal, x_even, x_odd, _, even, odd, low, high):
    first = parity("bx") == 0
    for start in range(0, XLEN, 128):
        a = x_even[:, start : start + 128].astype(F32)
        b = x_odd[:, start : start + 128].astype(F32)
        low[:, start : start + 128] = jnp.where(first, b, a).astype(BF16)
        high[:, start : start + 128] = jnp.where(first, a, b).astype(BF16)
    py = parity("by")
    is_first = py == 0

    def select(k, near=None, far=None, columns=64):
        r, j = iota((16, columns), 0), iota((16, columns), 1)
        high_side = jnp.where(r < 8, py, 1 - py) == 0
        iy = jnp.where(high_side, 7 - k, k)
        row = r % 8 - 2
        source = jnp.where((row >= 0) & (row < 4), row * 8 + iy, -1)
        if near is not None:
            source = jnp.where(row == -1, 32 + near + iy, jnp.where(row == 4, 48 + near + iy, source))
        if far is not None:
            source = jnp.where(row == -2, 32 + far + iy, jnp.where(row == 5, 48 + far + iy, source))
        return onehot(j == source)

    def put(start, value):
        even[:, start : start + value[0].shape[1]] = value[0].astype(BF16)
        odd[:, start : start + value[1].shape[1]] = value[1].astype(BF16)

    def both(make, picked):
        return make(picked[:8]), make(picked[8:])

    cut = []
    for h in range(2):
        source = [faces[:, h * 2048 : h * 2048 + 2048], low[:, XB : XB + 2048], high[:, XB : XB + 2048]]
        cut.append(dot(select(0, 8 * h), jnp.concatenate(source, 0)))
    put(YB, (over(cut[0][:8], cut[1][:8]), over(cut[0][8:], cut[1][8:])))

    def by_side(minus, plus):
        up = jnp.where(is_first, plus[:8], minus[:8])
        down = jnp.where(is_first, minus[8:], plus[8:])
        return halves(up), halves(down)

    own1, own0 = select(1, columns=32), select(0, columns=32)

    def lanes(ref, pieces, width):
        return jnp.concatenate([ref[:, p : p + width] for p in pieces], 1)

    minus, plus = [i * 1024 for i in range(4)], [i * 1024 + 768 for i in range(4)]
    put(YA, by_side(dot(own0, lanes(blocks, minus, 256)), dot(own0, lanes(blocks, plus, 256))))
    put(YT, by_side(dot(own0, lanes(tent, minus, 256)), dot(own0, lanes(tent, plus, 256))))
    minus = [f * 1024 + i * 256 for f in range(4) for i in range(4)]
    plus = [p + 128 for p in minus]
    put(YF, by_side(dot(own1, lanes(faces, minus, 128)), dot(own1, lanes(faces, plus, 128))))
    own = traces_packed[...]
    rows = jnp.concatenate([own, low[:, XD : XD + 768], high[:, XD : XD + 768]], 0)
    g0, g1, g2 = dot(select(0, 0, 8), rows), dot(select(1, 0), rows), dot(select(2, columns=32), own)
    cut = []
    for h in range(2):
        rows = [b_packed[:, h * 384 : h * 384 + 384], low[:, XH : XH + 384], high[:, XH : XH + 384]]
        cut.append(dot(select(0, 8 * h), jnp.concatenate(rows, 0)))
    r0, r1 = jnp.concatenate(cut, 1), dot(own1, b_packed[...])
    put(YD, (over(g0[:8], g1[:8]), over(g0[8:], g1[8:])))
    put(YG, (over(g2[:8], r0[:8]), over(g2[8:], r0[8:])))
    put(YR, both(halves, r1))
    own = diagonal[...]
    d0 = dot(select(0, 0), jnp.concatenate([own, low[:, XE : XE + 128], high[:, XE : XE + 128]], 0))
    d1 = dot(own1, own)
    put(YE, (over(d0[:8], d1[:8]), over(d0[8:], d1[8:])))


def prolong_kernel(tent, t16, plus_y, minus_y, stage, t32):
    lane = iota((256, 128), 1)
    for k in range(4):
        for ph in range(8):
            chunk = tent[:, (ph * 4 + k) * 128 : (ph * 4 + k + 1) * 128].astype(F32)
            stage[k, pl.ds(ph, NE, stride=8), :] = chunk
    for k in range(4):
        both = stage[k]
        other = pltpu.roll(both, 64, 1)
        t32[pl.ds(2 * k, 256, stride=8), :] = jnp.where(lane < 64, both, other)
        t32[pl.ds(2 * k + 1, 256, stride=8), :] = jnp.where(lane < 64, other, both)
    t16[...] = t32[...].astype(BF16)
    sub = iota((8, 128), 0)
    for e in range(NE):
        plus, minus = [], []
        for h in range(2):
            base = e * 64 + 32 * h
            a, b = t32[base + 8 : base + 16, :], t32[base + 24 : base + 32, :]
            plus.append(jnp.where(sub < 4, pltpu.roll(a, 4, 0), b))
            a, b = t32[base : base + 8, :], t32[base + 16 : base + 24, :]
            minus.append(jnp.where(sub < 4, a, pltpu.roll(b, 4, 0)))
        plus_y[e * 16 : e * 16 + 16, :] = jnp.concatenate(plus, 0).astype(BF16)
        minus_y[e * 16 : e * 16 + 16, :] = jnp.concatenate(minus, 0).astype(BF16)


def stage_blocks(block_chunk, stage):
    lane = iota((NE, 128), 1)
    diag = jnp.zeros((NE, 128), F32)
    for k in range(4):
        for ph in range(8):
            c = ph * 4 + k
            chunk = block_chunk(c)
            diag = diag + jnp.where((lane == 2 * c) | (lane == 65 + 2 * c), chunk, 0.0)
            stage[k, pl.ds(ph, NE, stride=8), :] = chunk
    return diag


def reciprocal(diagonal):
    return 1.0 / jnp.where(diagonal == 0.0, 1.0, diagonal)


def operators(block_chunk, face_chunk, w, stage, fstage, w32):
    lane = iota((256, 128), 1)
    diag = stage_blocks(block_chunk, stage)
    for f in range(4):
        for ph in range(8):
            fstage[f, pl.ds(ph, NE, stride=8), :] = face_chunk(f * 8 + ph)
    folded = jnp.concatenate([fstage[f].astype(BF16) for f in range(4)], 1)
    row, col = iota((512, 128), 0), iota((512, 128), 1)
    lo_of = (row // 16) % 8
    target = 64 + row // 128 * 16 + row % 16
    for k in range(4):
        both = stage[k]
        other = pltpu.roll(both, 64, 1)
        for s, part in enumerate((both, other)):
            p_lo = 2 * k + s
            coupled = dot(folded, onehot((col == target) & (lo_of == p_lo)))
            w32[pl.ds(p_lo, 256, stride=8), :] = jnp.where(lane < 64, part, coupled)
    w[...] = w32[...].astype(BF16)
    return (diag + pltpu.roll(diag, 64, 1))[:, :64]


def own_kernel(blocks, faces, bounds, w, inverse, coefficients, *scratch):
    coefficients[...] = jnp.concatenate([jnp.broadcast_to(c, (1, 128)) for c in factors(bounds)] + [jnp.zeros((3, 128), F32)], 0)
    chunk = lambda ref: lambda c: ref[:, c * 128 : (c + 1) * 128].astype(F32)
    inverse[...] = 1.0 / operators(chunk(blocks), chunk(faces), w, *scratch)


NOTHING = (8, 128)


def part(ref, start, c, half):
    row = 8 * (c // half)
    lane = start + (c % half) * 128
    return ref[:, lane : lane + 128].astype(F32)[row : row + 8]


def halo_x(low, high, w, *scratch):
    zero = jnp.zeros(NOTHING, F32)

    def block(c):
        near_low = part(low, XA, c - 24, 4) if c >= 24 else zero
        near_high = part(high, XA, c, 4) if c < 8 else zero
        return jnp.concatenate([near_low, zero, near_high, zero], 0)

    def face(c):
        f, ph = c // 8, c % 8
        far_low = part(low, XC, f * 2 + ph - 6, 4) if ph >= 6 else zero
        far_high = part(high, XC, f * 2 + ph, 4) if ph < 2 else zero
        return jnp.concatenate([part(low, XB, c, 16), far_low, part(high, XB, c, 16), far_high], 0)

    operators(block, face, w, *scratch)


def halo_y(even, odd, w, low, high, *scratch):
    first = parity("by") == 0
    for start in range(0, YLEN, 128):
        a = even[:, start : start + 128].astype(F32)
        b = odd[:, start : start + 128].astype(F32)
        low[:, start : start + 128] = jnp.where(first, b, a).astype(BF16)
        high[:, start : start + 128] = jnp.where(first, a, b).astype(BF16)
    zero = jnp.zeros(NOTHING, F32)

    def block(c):
        i, d = c // 8, c % 8
        near_low = part(low, YA, i * 2 + d - 6, 4) if d >= 6 else zero
        near_high = part(high, YA, i * 2 + d, 4) if d < 2 else zero
        return jnp.concatenate([near_low, zero, near_high, zero], 0)

    def face(c):
        f, ph = c // 8, c % 8
        i = ph // 2
        far_low = part(low, YF, f * 4 + i, 8) if ph % 2 == 1 else zero
        far_high = part(high, YF, f * 4 + i, 8) if ph % 2 == 0 else zero
        return jnp.concatenate([part(low, YB, c, 16), far_low, part(high, YB, c, 16), far_high], 0)

    operators(block, face, w, *scratch)


def factors(bounds):
    low, high = bounds[0:1, 0:1], bounds[0:1, 1:2]
    centre = 0.5 * (high + low)
    half_width = 0.5 * (high - low)
    spread = centre / half_width
    first = 1.0 / spread
    second = 1.0 / (2.0 * spread - first)
    third = 1.0 / (2.0 * spread - second)
    return centre, half_width, first, second, third


def beside_own(columns):
    return [((ix + 3) * 16 + iy, 0, ix * 8 + iy) for ix in range(EX) for iy in columns]


def beside_x(k, columns):
    return [((7 + k if s else 2 - k) * 16 + iy, 1, s * 16 + k * 8 + iy) for s in range(2) for iy in columns]


def beside_y(k, rows):
    return [((r + 1) * 16 + (8 + k if s else 15 - k), 2, s * 16 + k * 8 + r) for s in range(2) for r in rows]


INNER, OUTER = range(1, 7), (0, 7)
EARLY = (1, 9, beside_own(INNER) + beside_x(0, INNER) + beside_x(1, INNER))
LATE = (1, 9, beside_own(OUTER) + beside_x(0, OUTER) + beside_x(1, OUTER) + beside_y(0, range(1, 7)) + beside_y(1, range(2, 6)))
SECOND = (2, 8, beside_own(range(EY)) + beside_x(0, range(EY)) + beside_y(0, range(2, 6)))
THIRD = (3, 7, beside_own(range(EY)))


def joined(value):
    return value + pltpu.roll(value, 64, 1)


def apply(plan, values, tables, t_ref, x_ref, a_ref):
    first, last, elements = plan
    lane = iota((16, 128), 1)
    x_ref[SPAN:, :] = jnp.zeros((8 * EXT - SPAN, 128), F32)
    for n in range(NRHS):
        for ri in range(first, last):
            row = n * EXT + ri * 16
            own = t_ref[row : row + 16, :]
            sides = jnp.where(
                lane < 80,
                t_ref[row - 16 : row, :],
                jnp.where(
                    lane < 96,
                    t_ref[row + 16 : row + 32, :],
                    jnp.where(lane < 112, pltpu.roll(own, 1, 0), pltpu.roll(own, 15, 0)),
                ),
            )
            x_ref[row : row + 16, :] = jnp.where(lane < 64, own if values else 0.0, sides)
    for row, table, e in elements:
        hi, lo = split(x_ref[pl.ds(row, 8, stride=EXT), :])
        out = dot(over(hi, lo), tables[table][e * 64 : e * 64 + 64, :], NT)
        a_ref[pl.ds(row, 8, stride=EXT), 0:64] = out[:8] + out[8:]


def start_smoothing(guess, b, inverse, w, wx, x_low, x_high, t_ref, r_ref, i_ref, x_ref, a_ref):
    t_ref[...] = jnp.zeros((SPAN, 128), F32)
    r_ref[...] = jnp.zeros((SPAN, 128), F32)
    i_ref[...] = jnp.ones((EXT, 128), F32)
    a_ref[...] = jnp.zeros((8 * EXT, 128), F32)
    traces = with_traces(guess[...].reshape(NRHS * NE, 64))
    for ix in range(EX):
        row = (ix + 3) * 16
        i_ref[row : row + 8, 0:64] = inverse[ix * 8 : ix * 8 + 8, :]
        for n in range(NRHS):
            source = n * NE + ix * 8
            t_ref[n * EXT + row : n * EXT + row + 8, :] = traces[source : source + 8]
            r_ref[n * EXT + row : n * EXT + row + 8, 0:64] = b[source : source + 8, :]
    for side, message in enumerate((x_low, x_high)):
        at = [(7 + k if side else 2 - k) * 16 for k in range(3)]
        near = message[:, XD : XD + 768].astype(F32)
        far = message[:, XK : XK + 256].astype(F32)
        diagonal = reciprocal(message[:, XE : XE + 128].astype(F32))
        for k in range(2):
            i_ref[at[k] : at[k] + 8, :] = diagonal[8 * k : 8 * k + 8]
        for n in range(NRHS):
            base = n * EXT
            for k in range(2):
                t_ref[base + at[k] : base + at[k] + 8, :] = joined(near[8 * k : 8 * k + 8, n * 128 : n * 128 + 128])
            t_ref[base + at[2] : base + at[2] + 8, :] = joined(unsqueeze(far[:8], n, TRACE_OFFSET[1 - side]))
            r_ref[base + at[0] : base + at[0] + 8, :] = joined(part(message, XH, n, 3))
            r_ref[base + at[1] : base + at[1] + 8, :] = joined(unsqueeze(far[8:], n, VALUE_OFFSET[1 - side]))
    apply(EARLY, False, (w, wx), t_ref, x_ref, a_ref)
    r_ref[...] = r_ref[...] - a_ref[:SPAN, :]


def smooth(guess, w, wx, wy, coefficients, y_low, y_high, t_in, r_in, i_in, smoothed, t_ref, r_ref, i_ref, x_ref, a_ref):
    t_ref[...] = t_in[...]
    r_ref[...] = r_in[...]
    i_ref[...] = i_in[...]
    a_ref[...] = jnp.zeros((8 * EXT, 128), F32)
    for side, message in enumerate((y_low, y_high)):
        column = [16 + (8 + k if side else 15 - k) for k in range(3)]
        diagonal = reciprocal(message[:, YE : YE + 128].astype(F32))
        near = message[:, YD : YD + 768].astype(F32)
        far = message[:, YG : YG + 768].astype(F32)
        for k in range(2):
            i_ref[pl.ds(column[k], 8, stride=16), :] = diagonal[8 * k : 8 * k + 8]
        for n in range(NRHS):
            lanes = slice(n * 128, n * 128 + 128)
            for k, value in enumerate((near[:8, lanes], near[8:, lanes], far[:8, lanes])):
                t_ref[pl.ds(n * EXT + column[k], 8, stride=16), :] = joined(value)
            for k, value in enumerate((far[8:, lanes], part(message, YR, n, 3))):
                r_ref[pl.ds(n * EXT + column[k], 8, stride=16), :] = joined(value)
    tables = (w, wx, wy)
    centre, half_width, first, second, third = [coefficients[i : i + 1, 0:64] for i in range(5)]
    inverse = jnp.concatenate([i_ref[:, 0:64]] * NRHS, 0)
    apply(LATE, False, tables, t_ref, x_ref, a_ref)
    r = r_ref[:, 0:64] - a_ref[:SPAN, 0:64]
    u = inverse * r / centre
    x = u
    for plan, factor, new in ((SECOND, first, second), (THIRD, second, third)):
        t_ref[...] = with_traces(u)
        apply(plan, True, tables, t_ref, x_ref, a_ref)
        r = r - a_ref[:SPAN, 0:64]
        u = new * factor * u + (2.0 * new / half_width) * inverse * r
        x = x + u
    for n in range(NRHS):
        for ix in range(EX):
            row = n * EXT + (ix + 3) * 16
            smoothed[n, ix * 8 : ix * 8 + 8, :] = guess[n, ix * 8 : ix * 8 + 8, :] + x[row : row + 8]


def ghost_rows(message, start, out):
    lane = iota((8, 128), 1)
    for j in range(8):
        both = part(message, start, j, 4)
        other = pltpu.roll(both, 64, 1)
        out[pl.ds(2 * j, 8, stride=16), :] = jnp.where(lane < 64, both, other)
        out[pl.ds(2 * j + 1, 8, stride=16), :] = jnp.where(lane < 64, other, both)


def label_masks(masks):
    lane = iota((16, 256), 1)
    for b in range(4):
        masks[b * 16 : b * 16 + 16, :] = onehot(lane // 64 == b)


def masked(masks, piece, label):
    mask = masks[pl.ds(pl.multiple_of(label * 16, 16), 16), :]
    return jnp.concatenate([piece, piece], 1) * jnp.concatenate([mask] * 4, 0)


def none(count):
    return jnp.zeros((count, 128), BF16)


def face_column(f, rows):
    return jnp.concatenate([none(64 + 16 * f), rows] + ([none(48 - 16 * f)] if f < 3 else []), 0)


def galerkin_kernel(half, labels, t16, plus_y, minus_y, w, *refs):
    (before_local, _), refs = (refs[:2], refs[2:]) if half else ((None, None), refs)
    local, edge_column, edge_columns, tt, masks, big = refs
    label_masks(masks)
    lane128 = iota((64, 128), 1)
    for pair in range(8):
        e = 16 * half + 2 * pair
        turned = t16[e * 64 : e * 64 + 128, :].astype(F32).T[:64]
        first, second = labels[e], labels[e + 1]
        for a in range(4):
            keep = jnp.where(
                lane128 < 64,
                jnp.where(first == a, 1.0, 0.0),
                jnp.where(second == a, 1.0, 0.0),
            )
            tt[a * 64 : a * 64 + 64, pair * 128 : pair * 128 + 128] = (turned * keep).astype(BF16)
    edge_column[...] = tt[:, 512 * half : 512 * half + 512]
    for f in range(2):
        for i in range(2):
            start = (4 * i + 3 * f) * 128
            edge_columns[f, :, i * 128 : i * 128 + 128] = tt[:, start : start + 128]

    def row_of_elements(ix, carry):
        for iy in range(EY):
            e = ix * EY + iy
            own = pl.ds(pl.multiple_of(e * 64, 64), 64)
            here = pl.ds(pl.multiple_of((e - 16 * half) * 64, 64), 64)
            before = pl.multiple_of(jnp.maximum(e - 8, 0) * 64, 64)
            after = pl.multiple_of(jnp.minimum(e + 8, 31) * 64, 64)
            rows = [
                t16[pl.ds(before + 48, 16), :],
                t16[pl.ds(after, 16), :],
            ]
            if iy > 0:
                rows.append(plus_y[pl.ds(pl.multiple_of((e - 1) * 16, 16), 16), :])
            else:
                rows.append(none(16))
            if iy < 7:
                rows.append(minus_y[pl.ds(pl.multiple_of((e + 1) * 16, 16), 16), :])
            columns = [jnp.concatenate([t16[own, :], none(64)], 0)]
            columns += [face_column(f, value) for f, value in enumerate(rows)]
            pieces = dot(w[own, :], jnp.concatenate(columns, 1)).astype(BF16)
            piece = lambda s: pieces[:, s * 128 : s * 128 + 128]
            big[0, here, :] = masked(masks, piece(0), labels[e])
            big[1, here, :] = masked(masks, piece(1), labels[jnp.maximum(e - 8, 0)])
            big[2, here, :] = masked(masks, piece(2), labels[jnp.minimum(e + 8, 31)])
            nothing = jnp.zeros((64, 256), BF16)
            big[3, here, :] = masked(masks, piece(3), labels[e - 1]) if iy > 0 else nothing
            big[4, here, :] = masked(masks, piece(4), labels[e + 1]) if iy < 7 else nothing
        return carry

    lax.fori_loop(2 * half, 2 * half + 2, row_of_elements, 0)
    total = dot(tt[...], big[0]) + dot(tt[...], big[3]) + dot(tt[...], big[4])
    if half:
        total = before_local[...] + total + dot(tt[...], big[1]) + dot(tt[:, :512], big[2, :512, :])
    else:
        total = total + dot(tt[:, 512:], big[1, 512:, :]) + dot(tt[...], big[2])
    local[...] = total


def ghost_block(face, message, start, first_row, elements, side_labels, label_start, w, columns, rows, masks, side, result):
    ghost_rows(message, start, rows)
    for i, (e, place) in enumerate(elements):
        near = rows[(i + first_row) * 16 : (i + first_row) * 16 + 16, :].astype(BF16)
        piece = dot(w[e * 64 : e * 64 + 64, :], face_column(face, near)).astype(BF16)
        side[place : place + 64, :] = masked(masks, piece, side_labels[label_start + i])
    width = 512 // len(columns)
    result[...] = sum(dot(c[...], side[i * width : (i + 1) * width, :]) for i, c in enumerate(columns))


def middle_kernel(side_labels, w, column0, column1, x_low, x_high, guess, b, inverse, wx, t_ref, r_ref, i_ref, ghost,
                  stage, fstage, w32, x_ref, a_ref, rows, masks, side, result, sems):
    label_masks(masks)
    copies = []
    for f, (message, column) in enumerate(((x_low, column0), (x_high, column1))):
        elements = [(24 * f + iy, iy * 64) for iy in range(EY)]
        ghost_block(f, message, XT, 0, elements, side_labels, 8 * f, w, (column,), rows, masks, side, result.at[f])
        copies.append(pltpu.make_async_copy(result.at[f], ghost.at[f], sems.at[f]))
        copies[-1].start()
    halo_x(x_low, x_high, wx, stage, fstage, w32)
    start_smoothing(guess, b, inverse, w, wx, x_low, x_high, t_ref, r_ref, i_ref, x_ref, a_ref)
    for copy in copies:
        copy.wait()


def finish_kernel(side_labels, guess, w, wx, coefficients, y_even, y_odd, columns0, columns1, t_in, r_in, i_in, ghost_in,
                  smoothed, ghost, wy, y_low, y_high, stage, fstage, w32, t_ref, r_ref, i_ref, x_ref, a_ref,
                  rows, masks, side, result, sems):
    halo_y(y_even, y_odd, wy, y_low, y_high, stage, fstage, w32)
    label_masks(masks)
    copies = []
    for f, message in enumerate((y_low, y_high)):
        side[...] = jnp.zeros((512, 256), BF16)
        elements = [(8 * ix + 7 * f, ix * 128 + 64 * f) for ix in range(EX)]
        columns = (columns0.at[f], columns1.at[f])
        ghost_block(2 + f, message, YT, 2, elements, side_labels, 16 + 4 * f, w, columns, rows, masks, side, result.at[f])
        copies.append(pltpu.make_async_copy(result.at[f], ghost.at[2 + f], sems.at[f]))
        copies[-1].start()
    smooth(guess, w, wx, wy, coefficients, y_low, y_high, t_in, r_in, i_in, smoothed, t_ref, r_ref, i_ref, x_ref, a_ref)
    for copy in copies:
        copy.wait()


def call(kernel, outs, scratch, operands, flops, moved, in_specs=None, out_specs=None, aliases=None, room=48):
    return pl.pallas_call(
        kernel,
        out_shape=outs,
        in_specs=in_specs or [VMEM] * len(operands),
        out_specs=out_specs or [VMEM] * len(outs),
        scratch_shapes=scratch,
        input_output_aliases=aliases or {},
        cost_estimate=pl.CostEstimate(flops=flops, bytes_accessed=moved, transcendentals=0),
        compiler_params=pltpu.CompilerParams(vmem_limit_bytes=room * 1024 * 1024),
    )(*operands)


def exchange(messages, axis):
    out = []
    for first, message in enumerate(messages):
        pairs = []
        for i in range(first, lax.axis_size(axis) - 1, 2):
            pairs += [(i, i + 1), (i + 1, i)]
        out.append(lax.ppermute(message, axis, pairs))
    return out


def shaped(*shape, dtype=BF16):
    return jax.ShapeDtypeStruct(shape, dtype)


STAGES = [pltpu.VMEM((4, 256, 128), F32), pltpu.VMEM((4, 256, 128), F32), pltpu.VMEM((2048, 128), F32)]


GHOST = [
    pltpu.VMEM((128, 128), F32),
    pltpu.VMEM((64, 256), BF16),
    pltpu.VMEM((512, 256), BF16),
    pltpu.VMEM((2, 256, 256), F32),
    pltpu.SemaphoreType.DMA((2,)),
]


def on_device(blocks, faces, tentative, aggregate, ghost_labels, rhs, guess, bounds):
    wide = lambda *shape: shaped(*shape, dtype=F32)
    rhs = jnp.swapaxes(rhs[0, 0], 1, 2)
    guess = jnp.swapaxes(guess[0, 0], 1, 2)
    labels, side_labels = aggregate.reshape(NE), ghost_labels.reshape(24)
    blocks, faces, tentative = [a.reshape(NE, 4096) for a in (blocks, faces, tentative)]
    even, odd, traces_packed, b_packed, b, diagonal = call(
        pack_x_kernel,
        [shaped(16, XLEN)] * 2 + [shaped(NE, 768)] * 2 + [wide(NRHS * NE, 64), shaped(NE, 128)],
        [pltpu.VMEM((NE, 4096), BF16)] * 3 + [pltpu.VMEM((NRHS, NE, 64), F32)] * 2
        + [STAGES[0], STAGES[2], pltpu.VMEM((2048, 128), BF16)] + [pltpu.VMEM((256, 128), F32)] * 2
        + [pltpu.SemaphoreType.DMA((5,))],
        (blocks, faces, tentative, guess, rhs), 10**6, 2**20, [HBM] * 5, room=62,
    )
    even, odd = exchange((even, odd), "bx")
    w, inverse, coefficients = call(
        own_kernel, [shaped(2048, 128), wide(NE, 64), wide(8, 128)], STAGES,
        (blocks, faces, bounds.reshape(1, 2)), 10**9, 2**20,
    )
    t16, plus_y, minus_y = call(
        prolong_kernel, [shaped(2048, 128), shaped(512, 128), shaped(512, 128)],
        [STAGES[0], STAGES[2]], (tentative,), 5 * 10**8, 2**20,
    )

    def galerkin(half, *more):
        return call(
            lambda *refs: galerkin_kernel(half, *refs),
            [wide(256, 256), shaped(256, 512), shaped(2, 256, 256)],
            [pltpu.VMEM((256, 1024), BF16), GHOST[1], pltpu.VMEM((5, 1024, 256), BF16)],
            (labels, t16, plus_y, minus_y, w, *more),
            2 * 10**9, 2 * 2**20, [SMEM] + [VMEM] * 4 + [VMEM, ANY][: len(more)],
        )

    local, column0, columns0 = galerkin(0)
    even, odd, x_low, x_high = call(
        pack_y_kernel, [shaped(16, YLEN)] * 2 + [shaped(16, XLEN)] * 2, [],
        (blocks, faces, tentative, traces_packed, b_packed, diagonal, even, odd, column0), 10**8, 2**20,
        [VMEM] * 8 + [ANY],
    )
    even, odd = exchange((even, odd), "by")
    local, column1, columns1 = galerkin(1, local, x_low)
    extended = [wide(SPAN, 128)] * 2 + [wide(EXT, 128)]
    fields = [pltpu.VMEM(a.shape, F32) for a in extended]
    pads = [pltpu.VMEM((8 * EXT, 128), F32)] * 2
    wx, traces, residue, inverses, ghost = call(
        middle_kernel, [shaped(2048, 128)] + extended + [wide(4, 256, 256)], STAGES + pads + GHOST,
        (side_labels, w, column0, column1, x_low, x_high, guess, b, inverse), 10**9, 2**20,
        [SMEM] + [VMEM] * 8, [VMEM] * 4 + [HBM],
    )
    smoothed, ghost = call(
        finish_kernel, [wide(NRHS, NE, 64), wide(4, 256, 256)],
        [pltpu.VMEM((2048, 128), BF16)] + [pltpu.VMEM((16, YLEN), BF16)] * 2 + STAGES + fields + pads + GHOST,
        (side_labels, guess, w, wx, coefficients, even, odd, columns0, columns1, traces, residue, inverses, ghost),
        10**9, 2**20, [SMEM] + [VMEM] * 11 + [HBM], [VMEM, HBM], {12: 1},
    )
    return jnp.swapaxes(smoothed, 1, 2)[None, None], local[None, None], ghost[None, None]


def solution(mesh):
    b = lambda extra: P("bx", "by", *([None] * extra))
    return jax.shard_map(
        on_device,
        mesh=mesh,
        in_specs=(b(2), b(2), b(2), b(1), b(1), b(3), b(3), P()),
        out_specs=(b(3), b(2), b(3)),
        check_vma=False,
    )
```

```python
import jax
import jax.numpy as jnp
from jax import lax
from jax.experimental import pallas as pl
from jax.experimental.pallas import tpu as pltpu
from jax.sharding import PartitionSpec as P

EX, EY, NE, NRHS = 4, 8, 32, 6
F32, BF16 = jnp.float32, jnp.bfloat16
VMEM = pl.BlockSpec(memory_space=pltpu.VMEM)
SMEM = pl.BlockSpec(memory_space=pltpu.SMEM)
HBM = pl.BlockSpec(memory_space=pltpu.HBM)
ANY = pl.BlockSpec(memory_space=pl.ANY)
NT = (((1,), (1,)), ((), ()))
NN = (((1,), (0,)), ((), ()))

XA = 0
XB = 512
XC = 2560
XD = 3072
XH = 3840
XK = 4224
XT = 4480
XE = 4992
XLEN = 5120
YA, YB = 0, 512
YF = 2560
YD = 3584
YG = 4352
YR = 5120
YT = 5504
YE = 6016
YLEN = 6144

EXT, SPAN = 160, 960


def dot(a, b, dims=NN):
    return lax.dot_general(a, b, dims, preferred_element_type=F32)


def iota(shape, dim):
    return lax.broadcasted_iota(jnp.int32, shape, dim)


def onehot(mask):
    return mask.astype(F32).astype(BF16)


def none(count):
    return jnp.zeros((count, 128), BF16)


def split(x):
    hi = x.astype(BF16)
    return hi, (x - hi.astype(F32)).astype(BF16)


def halves(x):
    lanes = x.shape[1] // 2
    return jnp.concatenate([x[:, :lanes], x[:, lanes:]], 0)


def over(a, b):
    return jnp.concatenate([a, b], 0)


def parity(axis):
    return lax.axis_index(axis) % 2


def with_traces(v):
    q, lane = iota((64, 128), 0), iota((64, 128), 1)
    t = lane % 16
    f = lane // 16 - 4
    along_y = 16 * (t // 4) + t % 4
    source = jnp.where(f == 0, 48 + t, jnp.where(f == 1, t, jnp.where(f == 2, along_y + 12, along_y)))
    pick = onehot(q == jnp.where(f < 0, lane, source))
    hi, lo = split(v)
    return dot(hi, pick) + dot(lo, pick)


def by_element(rows):
    return jnp.concatenate([rows[n * NE : (n + 1) * NE] for n in range(NRHS)], 1)


def pack_lanes(v):
    hi, lo = split(v)
    q, lane = iota((64, 128), 0), iota((64, 128), 1)
    return by_element(dot(hi, onehot(q == lane)) + dot(lo, onehot(q == lane - 64)))


def pack_traces(traces):
    hi, lo = split(traces)
    lane = iota(traces.shape, 1)
    return by_element(jnp.where(lane >= 64, hi.astype(F32), pltpu.roll(lo.astype(F32), 64, 1)))


def squeeze(value, offset):
    lane = iota((8, 128), 1) % 64
    keep = (lane >= offset) & (lane < offset + 16)
    tiles = []
    for first in (0, 4):
        total = jnp.zeros((8, 128), F32)
        for j, n in enumerate(range(first, min(first + 4, NRHS))):
            one = jnp.where(keep, value[:, n * 128 : n * 128 + 128], 0.0)
            total = total + pltpu.roll(one, (16 * j - offset) % 128, 1)
        tiles.append(total)
    return jnp.concatenate(tiles, 1)


def unsqueeze(tiles, n, offset):
    lane = iota((8, 128), 1) % 64
    tile = tiles[:, n // 4 * 128 : n // 4 * 128 + 128]
    moved = pltpu.roll(tile, (offset - 16 * (n % 4)) % 128, 1)
    return jnp.where((lane >= offset) & (lane < offset + 16), moved, 0.0)


TRACE_OFFSET, VALUE_OFFSET = (16, 0), (0, 48)


def pack_x_kernel(blocks_in, faces_in, tent_in, guess_in, rhs_in, even, odd, traces_packed, b_packed, b_out, diagonal,
                  blocks, faces, tent, guess, rhs, stage, w32, w16, x_ref, a_ref, sems):
    copies = [
        pltpu.make_async_copy(source, target, sems.at[i])
        for i, (source, target) in enumerate(
            ((guess_in, guess), (blocks_in, blocks), (rhs_in, rhs), (faces_in, faces), (tent_in, tent))
        )
    ]
    for copy in copies:
        copy.start()
    copies[0].wait()
    v = guess[...].reshape(NRHS * NE, 64)
    traces = with_traces(v)
    t = pack_traces(traces)
    traces_packed[...] = t.astype(BF16)
    x_ref[0:192, :] = traces
    x_ref[192:256, :] = jnp.zeros((64, 128), F32)
    copies[1].wait()
    chunk = lambda c: blocks[:, c * 128 : (c + 1) * 128].astype(F32)
    stage_blocks(chunk, stage)
    diag = diagonals(chunk)
    diagonal[...] = diag.astype(BF16)
    for k in range(4):
        both = stage[k]
        w32[pl.ds(2 * k, 256, stride=8), :] = both
        w32[pl.ds(2 * k + 1, 256, stride=8), :] = pltpu.roll(both, 64, 1)
    w16[...] = w32[...].astype(BF16)
    lane8 = iota((8, 128), 1)
    for e in range(NE):
        hi, lo = split(jnp.where(lane8 < 64, x_ref[pl.ds(e, 8, stride=NE), :], 0.0))
        out = dot(over(hi, lo), w16[e * 64 : e * 64 + 64, :], NT)
        a_ref[pl.ds(e, 8, stride=NE), 0:64] = out[:8] + out[8:]
    for copy in copies[2:]:
        copy.wait()
    b = rhs[...].reshape(NRHS * NE, 64) - a_ref[0:192, 0:64]
    b_out[...] = b
    r = pack_lanes(b)
    b_packed[...] = r.astype(BF16)
    first = parity("bx") == 0

    def put(start, lanes, make):
        low, high = make(0), make(1)
        even[:, start : start + lanes] = jnp.where(first, high, low).astype(BF16)
        odd[:, start : start + lanes] = jnp.where(first, low, high).astype(BF16)

    def rows(k, side):
        return 8 * k if side == 0 else 24 - 8 * k

    def of(ref, k, side, start, lanes):
        row = rows(k, side)
        base = row // 16 * 16
        return ref[base : base + 16, start : start + lanes].astype(F32)[row - base : row - base + 8]

    def packed(value, k, side):
        return value[rows(k, side) : rows(k, side) + 8]

    def face_traces(side):
        return jnp.concatenate([of(faces, 1, side, f * 1024 + 768 * side, 256) for f in range(4)], 1)

    put(XA, 512, lambda s: halves(of(blocks, 0, s, 3072 * s, 1024)))
    for h in range(2):
        put(XB + h * 1024, 1024, lambda s: over(of(faces, 0, s, h * 1024, 1024), of(faces, 0, s, h * 1024 + 2048, 1024)))
    put(XC, 512, lambda s: halves(face_traces(s)))
    put(XD, 768, lambda s: over(packed(t, 0, s), packed(t, 1, s)))
    put(XH, 384, lambda s: halves(packed(r, 0, s)))
    put(XK, 256, lambda s: over(squeeze(packed(t, 2, s), TRACE_OFFSET[s]), squeeze(packed(r, 1, s), VALUE_OFFSET[s])))
    put(XT, 512, lambda s: halves(of(tent, 0, s, 3072 * s, 1024)))
    put(XE, 128, lambda s: over(packed(diag, 0, s), packed(diag, 1, s)))


def pack_y_kernel(blocks, faces, tent, traces_packed, b_packed, diagonal, x_even, x_odd, _, even, odd, low, high):
    first = parity("bx") == 0
    for start in range(0, XLEN, 128):
        a = x_even[:, start : start + 128].astype(F32)
        b = x_odd[:, start : start + 128].astype(F32)
        low[:, start : start + 128] = jnp.where(first, b, a).astype(BF16)
        high[:, start : start + 128] = jnp.where(first, a, b).astype(BF16)
    py = parity("by")
    is_first = py == 0

    def select(k, near=None, far=None, columns=64):
        r, j = iota((16, columns), 0), iota((16, columns), 1)
        high_side = jnp.where(r < 8, py, 1 - py) == 0
        iy = jnp.where(high_side, 7 - k, k)
        row = r % 8 - 2
        source = jnp.where((row >= 0) & (row < 4), row * 8 + iy, -1)
        if near is not None:
            source = jnp.where(row == -1, 32 + near + iy, jnp.where(row == 4, 48 + near + iy, source))
        if far is not None:
            source = jnp.where(row == -2, 32 + far + iy, jnp.where(row == 5, 48 + far + iy, source))
        return onehot(j == source)

    def put(start, value):
        even[:, start : start + value[0].shape[1]] = value[0].astype(BF16)
        odd[:, start : start + value[1].shape[1]] = value[1].astype(BF16)

    def both(make, picked):
        return make(picked[:8]), make(picked[8:])

    cut = []
    for h in range(2):
        source = [faces[:, h * 2048 : h * 2048 + 2048], low[:, XB : XB + 2048], high[:, XB : XB + 2048]]
        cut.append(dot(select(0, 8 * h), jnp.concatenate(source, 0)))
    put(YB, (over(cut[0][:8], cut[1][:8]), over(cut[0][8:], cut[1][8:])))

    def by_side(minus, plus):
        up = jnp.where(is_first, plus[:8], minus[:8])
        down = jnp.where(is_first, minus[8:], plus[8:])
        return halves(up), halves(down)

    own1, own0 = select(1, columns=32), select(0, columns=32)

    def lanes(ref, pieces, width):
        return jnp.concatenate([ref[:, p : p + width] for p in pieces], 1)

    minus, plus = [i * 1024 for i in range(4)], [i * 1024 + 768 for i in range(4)]
    put(YA, by_side(dot(own0, lanes(blocks, minus, 256)), dot(own0, lanes(blocks, plus, 256))))
    put(YT, by_side(dot(own0, lanes(tent, minus, 256)), dot(own0, lanes(tent, plus, 256))))
    minus = [f * 1024 + i * 256 for f in range(4) for i in range(4)]
    plus = [p + 128 for p in minus]
    put(YF, by_side(dot(own1, lanes(faces, minus, 128)), dot(own1, lanes(faces, plus, 128))))
    own = traces_packed[...]
    rows = jnp.concatenate([own, low[:, XD : XD + 768], high[:, XD : XD + 768]], 0)
    g0, g1, g2 = dot(select(0, 0, 8), rows), dot(select(1, 0), rows), dot(select(2, columns=32), own)
    cut = []
    for h in range(2):
        rows = [b_packed[:, h * 384 : h * 384 + 384], low[:, XH : XH + 384], high[:, XH : XH + 384]]
        cut.append(dot(select(0, 8 * h), jnp.concatenate(rows, 0)))
    r0, r1 = jnp.concatenate(cut, 1), dot(own1, b_packed[...])
    put(YD, (over(g0[:8], g1[:8]), over(g0[8:], g1[8:])))
    put(YG, (over(g2[:8], r0[:8]), over(g2[8:], r0[8:])))
    put(YR, both(halves, r1))
    own = diagonal[...]
    d0 = dot(select(0, 0), jnp.concatenate([own, low[:, XE : XE + 128], high[:, XE : XE + 128]], 0))
    d1 = dot(own1, own)
    put(YE, (over(d0[:8], d1[:8]), over(d0[8:], d1[8:])))


def prolongator(tent, t16, plus_y, minus_y, stage, t32):
    lane = iota((256, 128), 1)
    for k in range(4):
        for ph in range(8):
            chunk = tent[:, (ph * 4 + k) * 128 : (ph * 4 + k + 1) * 128].astype(F32)
            stage[k, pl.ds(ph, NE, stride=8), :] = chunk
    for k in range(4):
        both = stage[k]
        other = pltpu.roll(both, 64, 1)
        t32[pl.ds(2 * k, 256, stride=8), :] = jnp.where(lane < 64, both, other)
        t32[pl.ds(2 * k + 1, 256, stride=8), :] = jnp.where(lane < 64, other, both)
    t16[...] = t32[...].astype(BF16)
    sub = iota((8, 128), 0)
    for e in range(NE):
        plus, minus = [], []
        for h in range(2):
            base = e * 64 + 32 * h
            a, b = t32[base + 8 : base + 16, :], t32[base + 24 : base + 32, :]
            plus.append(jnp.where(sub < 4, pltpu.roll(a, 4, 0), b))
            a, b = t32[base : base + 8, :], t32[base + 16 : base + 24, :]
            minus.append(jnp.where(sub < 4, a, pltpu.roll(b, 4, 0)))
        plus_y[e * 16 : e * 16 + 16, :] = jnp.concatenate(plus, 0).astype(BF16)
        minus_y[e * 16 : e * 16 + 16, :] = jnp.concatenate(minus, 0).astype(BF16)


def stage_blocks(block_chunk, stage):
    for k in range(4):
        for ph in range(8):
            stage[k, pl.ds(ph, NE, stride=8), :] = block_chunk(ph * 4 + k)


def diagonals(block_chunk):
    lane = iota((NE, 128), 1)
    diag = jnp.zeros((NE, 128), F32)
    for c in range(32):
        diag = diag + jnp.where((lane == 2 * c) | (lane == 65 + 2 * c), block_chunk(c), 0.0)
    return diag + pltpu.roll(diag, 64, 1)


def reciprocal(diagonal):
    return 1.0 / jnp.where(diagonal == 0.0, 1.0, diagonal)


def operators(block_chunk, face_chunk, w, stage, fstage, w32):
    lane = iota((256, 128), 1)
    stage_blocks(block_chunk, stage)
    for f in range(4):
        for ph in range(8):
            fstage[f, pl.ds(ph, NE, stride=8), :] = face_chunk(f * 8 + ph)
    folded = jnp.concatenate([fstage[f].astype(BF16) for f in range(4)], 1)
    t, lane16 = iota((16, 128), 0), iota((16, 128), 1)
    moves = [onehot(lane16 == 64 + 16 * f + t) for f in range(4)]
    for k in range(4):
        both = stage[k]
        other = pltpu.roll(both, 64, 1)
        for s, part in enumerate((both, other)):
            p_lo = 2 * k + s
            pick = jnp.concatenate([moves[f] if lo == p_lo else none(16) for f in range(4) for lo in range(8)], 0)
            w32[pl.ds(p_lo, 256, stride=8), :] = jnp.where(lane < 64, part, dot(folded, pick))
    w[...] = w32[...].astype(BF16)


def own_operators(blocks, faces, bounds, w, inverse, coefficients, *scratch):
    coefficients[...] = jnp.concatenate([jnp.broadcast_to(c, (1, 128)) for c in factors(bounds)] + [jnp.zeros((3, 128), F32)], 0)
    chunk = lambda ref: lambda c: ref[:, c * 128 : (c + 1) * 128].astype(F32)
    operators(chunk(blocks), chunk(faces), w, *scratch)
    inverse[...] = 1.0 / diagonals(chunk(blocks))[:, :64]


NOTHING = (8, 128)


def part(ref, start, c, half):
    row = 8 * (c // half)
    lane = start + (c % half) * 128
    return ref[:, lane : lane + 128].astype(F32)[row : row + 8]


def halo_x(low, high, w, *scratch):
    zero = jnp.zeros(NOTHING, F32)

    def block(c):
        near_low = part(low, XA, c - 24, 4) if c >= 24 else zero
        near_high = part(high, XA, c, 4) if c < 8 else zero
        return jnp.concatenate([near_low, zero, near_high, zero], 0)

    def face(c):
        f, ph = c // 8, c % 8
        far_low = part(low, XC, f * 2 + ph - 6, 4) if ph >= 6 else zero
        far_high = part(high, XC, f * 2 + ph, 4) if ph < 2 else zero
        return jnp.concatenate([part(low, XB, c, 16), far_low, part(high, XB, c, 16), far_high], 0)

    operators(block, face, w, *scratch)


def halo_y(even, odd, w, low, high, *scratch):
    first = parity("by") == 0
    for start in range(0, YLEN, 128):
        a = even[:, start : start + 128].astype(F32)
        b = odd[:, start : start + 128].astype(F32)
        low[:, start : start + 128] = jnp.where(first, b, a).astype(BF16)
        high[:, start : start + 128] = jnp.where(first, a, b).astype(BF16)
    zero = jnp.zeros(NOTHING, F32)

    def block(c):
        i, d = c // 8, c % 8
        near_low = part(low, YA, i * 2 + d - 6, 4) if d >= 6 else zero
        near_high = part(high, YA, i * 2 + d, 4) if d < 2 else zero
        return jnp.concatenate([near_low, zero, near_high, zero], 0)

    def face(c):
        f, ph = c // 8, c % 8
        i = ph // 2
        far_low = part(low, YF, f * 4 + i, 8) if ph % 2 == 1 else zero
        far_high = part(high, YF, f * 4 + i, 8) if ph % 2 == 0 else zero
        return jnp.concatenate([part(low, YB, c, 16), far_low, part(high, YB, c, 16), far_high], 0)

    operators(block, face, w, *scratch)


def factors(bounds):
    low, high = bounds[0:1, 0:1], bounds[0:1, 1:2]
    centre = 0.5 * (high + low)
    half_width = 0.5 * (high - low)
    spread = centre / half_width
    first = 1.0 / spread
    second = 1.0 / (2.0 * spread - first)
    third = 1.0 / (2.0 * spread - second)
    return centre, half_width, first, second, third


def beside_own(columns):
    return [((ix + 3) * 16 + iy, 0, ix * 8 + iy) for ix in range(EX) for iy in columns]


def beside_x(k, columns):
    return [((7 + k if s else 2 - k) * 16 + iy, 1, s * 16 + k * 8 + iy) for s in range(2) for iy in columns]


def beside_y(k, rows):
    return [((r + 1) * 16 + (8 + k if s else 15 - k), 2, s * 16 + k * 8 + r) for s in range(2) for r in rows]


INNER, OUTER = range(1, 7), (0, 7)
EARLY = (1, 9, beside_own(INNER) + beside_x(0, INNER) + beside_x(1, INNER))
LATE = (1, 9, beside_own(OUTER) + beside_x(0, OUTER) + beside_x(1, OUTER) + beside_y(0, range(1, 7)) + beside_y(1, range(2, 6)))
SECOND = (2, 8, beside_own(range(EY)) + beside_x(0, range(EY)) + beside_y(0, range(2, 6)))
THIRD = (3, 7, beside_own(range(EY)))


def joined(value):
    return value + pltpu.roll(value, 64, 1)


def apply(plan, values, tables, t_ref, x_ref, a_ref):
    first, last, elements = plan
    lane = iota((16, 128), 1)
    x_ref[SPAN:, :] = jnp.zeros((8 * EXT - SPAN, 128), F32)
    for n in range(NRHS):
        for ri in range(first, last):
            row = n * EXT + ri * 16
            own = t_ref[row : row + 16, :]
            sides = jnp.where(
                lane < 80,
                t_ref[row - 16 : row, :],
                jnp.where(
                    lane < 96,
                    t_ref[row + 16 : row + 32, :],
                    jnp.where(lane < 112, pltpu.roll(own, 1, 0), pltpu.roll(own, 15, 0)),
                ),
            )
            x_ref[row : row + 16, :] = jnp.where(lane < 64, own if values else 0.0, sides)
    for row, table, e in elements:
        hi, lo = split(x_ref[pl.ds(row, 8, stride=EXT), :])
        out = dot(over(hi, lo), tables[table][e * 64 : e * 64 + 64, :], NT)
        a_ref[pl.ds(row, 8, stride=EXT), 0:64] = out[:8] + out[8:]


def start_smoothing(guess, b, inverse, w, wx, x_low, x_high, t_ref, r_ref, i_ref, x_ref, a_ref):
    t_ref[...] = jnp.zeros((SPAN, 128), F32)
    r_ref[...] = jnp.zeros((SPAN, 128), F32)
    i_ref[...] = jnp.ones((EXT, 128), F32)
    a_ref[...] = jnp.zeros((8 * EXT, 128), F32)
    traces = with_traces(guess[...].reshape(NRHS * NE, 64))
    for ix in range(EX):
        row = (ix + 3) * 16
        i_ref[row : row + 8, 0:64] = inverse[ix * 8 : ix * 8 + 8, :]
        for n in range(NRHS):
            source = n * NE + ix * 8
            t_ref[n * EXT + row : n * EXT + row + 8, :] = traces[source : source + 8]
            r_ref[n * EXT + row : n * EXT + row + 8, 0:64] = b[source : source + 8, :]
    for side, message in enumerate((x_low, x_high)):
        at = [(7 + k if side else 2 - k) * 16 for k in range(3)]
        near = message[:, XD : XD + 768].astype(F32)
        far = message[:, XK : XK + 256].astype(F32)
        diagonal = reciprocal(message[:, XE : XE + 128].astype(F32))
        for k in range(2):
            i_ref[at[k] : at[k] + 8, :] = diagonal[8 * k : 8 * k + 8]
        for n in range(NRHS):
            base = n * EXT
            for k in range(2):
                t_ref[base + at[k] : base + at[k] + 8, :] = joined(near[8 * k : 8 * k + 8, n * 128 : n * 128 + 128])
            t_ref[base + at[2] : base + at[2] + 8, :] = joined(unsqueeze(far[:8], n, TRACE_OFFSET[1 - side]))
            r_ref[base + at[0] : base + at[0] + 8, :] = joined(part(message, XH, n, 3))
            r_ref[base + at[1] : base + at[1] + 8, :] = joined(unsqueeze(far[8:], n, VALUE_OFFSET[1 - side]))
    apply(EARLY, False, (w, wx), t_ref, x_ref, a_ref)
    r_ref[...] = r_ref[...] - a_ref[:SPAN, :]


def smooth(guess, w, wx, wy, coefficients, y_low, y_high, t_in, r_in, i_in, smoothed, t_ref, r_ref, i_ref, x_ref, a_ref):
    t_ref[...] = t_in[...]
    r_ref[...] = r_in[...]
    i_ref[...] = i_in[...]
    a_ref[...] = jnp.zeros((8 * EXT, 128), F32)
    for side, message in enumerate((y_low, y_high)):
        column = [16 + (8 + k if side else 15 - k) for k in range(3)]
        diagonal = reciprocal(message[:, YE : YE + 128].astype(F32))
        near = message[:, YD : YD + 768].astype(F32)
        far = message[:, YG : YG + 768].astype(F32)
        for k in range(2):
            i_ref[pl.ds(column[k], 8, stride=16), :] = diagonal[8 * k : 8 * k + 8]
        for n in range(NRHS):
            lanes = slice(n * 128, n * 128 + 128)
            for k, value in enumerate((near[:8, lanes], near[8:, lanes], far[:8, lanes])):
                t_ref[pl.ds(n * EXT + column[k], 8, stride=16), :] = joined(value)
            for k, value in enumerate((far[8:, lanes], part(message, YR, n, 3))):
                r_ref[pl.ds(n * EXT + column[k], 8, stride=16), :] = joined(value)
    tables = (w, wx, wy)
    centre, half_width, first, second, third = [coefficients[i : i + 1, 0:64] for i in range(5)]
    inverse = jnp.concatenate([i_ref[:, 0:64]] * NRHS, 0)
    apply(LATE, False, tables, t_ref, x_ref, a_ref)
    r = r_ref[:, 0:64] - a_ref[:SPAN, 0:64]
    u = inverse * r / centre
    t_ref[...] = with_traces(u)
    apply(SECOND, True, tables, t_ref, x_ref, a_ref)
    r = r - a_ref[:SPAN, 0:64]
    last = second * first * u + (2.0 * second / half_width) * inverse * r
    total = u + last
    t_ref[...] = with_traces(last)
    apply(THIRD, True, tables, t_ref, x_ref, a_ref)
    for n in range(NRHS):
        for ix in range(EX):
            row = n * EXT + (ix + 3) * 16
            own, place = slice(row, row + 8), slice(ix * 8, ix * 8 + 8)
            residue = r[own] - a_ref[row : row + 8, 0:64]
            update = third * second * last[own] + (2.0 * third / half_width) * inverse[own] * residue
            smoothed[n, place, :] = guess[n, place, :] + total[own] + update


def ghost_rows(message, start, out):
    lane = iota((8, 128), 1)
    for j in range(8):
        both = part(message, start, j, 4)
        other = pltpu.roll(both, 64, 1)
        out[pl.ds(2 * j, 8, stride=16), :] = jnp.where(lane < 64, both, other)
        out[pl.ds(2 * j + 1, 8, stride=16), :] = jnp.where(lane < 64, other, both)


def label_masks(masks):
    lane = iota((16, 256), 1)
    for b in range(4):
        masks[b * 16 : b * 16 + 16, :] = onehot(lane // 64 == b)


def masked(masks, piece, label):
    mask = masks[pl.ds(pl.multiple_of(label * 16, 16), 16), :]
    return jnp.concatenate([piece, piece], 1) * jnp.concatenate([mask] * 4, 0)


def face_column(f, rows):
    return jnp.concatenate([none(64 + 16 * f), rows] + ([none(48 - 16 * f)] if f < 3 else []), 0)


def galerkin(half, before_local, labels, t16, plus_y, minus_y, w, local, edge_column, edge_columns, tt, masks, big):
    label_masks(masks)
    lane128 = iota((64, 128), 1)
    for pair in range(8):
        e = 16 * half + 2 * pair
        turned = t16[e * 64 : e * 64 + 128, :].astype(F32).T[:64]
        first, second = labels[e], labels[e + 1]
        for a in range(4):
            keep = jnp.where(
                lane128 < 64,
                jnp.where(first == a, 1.0, 0.0),
                jnp.where(second == a, 1.0, 0.0),
            )
            tt[a * 64 : a * 64 + 64, pair * 128 : pair * 128 + 128] = (turned * keep).astype(BF16)
    edge_column[...] = tt[:, 512 * half : 512 * half + 512]
    for f in range(2):
        for i in range(2):
            start = (4 * i + 3 * f) * 128
            edge_columns[f, :, i * 128 : i * 128 + 128] = tt[:, start : start + 128]

    def row_of_elements(ix, carry):
        for iy in range(EY):
            e = ix * EY + iy
            own = pl.ds(pl.multiple_of(e * 64, 64), 64)
            here = pl.ds(pl.multiple_of((e - 16 * half) * 64, 64), 64)
            before = pl.multiple_of(jnp.maximum(e - 8, 0) * 64, 64)
            after = pl.multiple_of(jnp.minimum(e + 8, 31) * 64, 64)
            rows = [
                t16[pl.ds(before + 48, 16), :],
                t16[pl.ds(after, 16), :],
            ]
            if iy > 0:
                rows.append(plus_y[pl.ds(pl.multiple_of((e - 1) * 16, 16), 16), :])
            else:
                rows.append(none(16))
            if iy < 7:
                rows.append(minus_y[pl.ds(pl.multiple_of((e + 1) * 16, 16), 16), :])
            columns = [jnp.concatenate([t16[own, :], none(64)], 0)]
            columns += [face_column(f, value) for f, value in enumerate(rows)]
            pieces = dot(w[own, :], jnp.concatenate(columns, 1)).astype(BF16)
            piece = lambda s: pieces[:, s * 128 : s * 128 + 128]
            big[0, here, :] = masked(masks, piece(0), labels[e])
            big[1, here, :] = masked(masks, piece(1), labels[jnp.maximum(e - 8, 0)])
            big[2, here, :] = masked(masks, piece(2), labels[jnp.minimum(e + 8, 31)])
            nothing = jnp.zeros((64, 256), BF16)
            big[3, here, :] = masked(masks, piece(3), labels[e - 1]) if iy > 0 else nothing
            big[4, here, :] = masked(masks, piece(4), labels[e + 1]) if iy < 7 else nothing
        return carry

    lax.fori_loop(2 * half, 2 * half + 2, row_of_elements, 0)
    total = dot(tt[...], big[0]) + dot(tt[...], big[3]) + dot(tt[...], big[4])
    if half:
        total = before_local[...] + total + dot(tt[...], big[1]) + dot(tt[:, :512], big[2, :512, :])
    else:
        total = total + dot(tt[:, 512:], big[1, 512:, :]) + dot(tt[...], big[2])
    local[...] = total


def ghost_block(face, message, start, first_row, elements, side_labels, label_start, w, columns, rows, masks, side, result):
    ghost_rows(message, start, rows)
    for i, (e, place) in enumerate(elements):
        near = rows[(i + first_row) * 16 : (i + first_row) * 16 + 16, :].astype(BF16)
        piece = dot(w[e * 64 : e * 64 + 64, :], face_column(face, near)).astype(BF16)
        side[place : place + 64, :] = masked(masks, piece, side_labels[label_start + i])
    width = 512 // len(columns)
    result[...] = sum(dot(c[...], side[i * width : (i + 1) * width, :]) for i, c in enumerate(columns))


def x_wait_kernel(labels, _, blocks, faces, tent, bounds, w, inverse, coefficients, t16, plus_y, minus_y, local, column, columns,
                  stage, fstage, w32, tt, masks, big):
    own_operators(blocks, faces, bounds, w, inverse, coefficients, stage, fstage, w32)
    prolongator(tent, t16, plus_y, minus_y, fstage, w32)
    galerkin(0, None, labels, t16, plus_y, minus_y, w, local, column, columns, tt, masks, big)


def y_wait_kernel(labels, side_labels, t16, plus_y, minus_y, w, before_local, column0, x_low, x_high, guess, b, inverse,
                  local, columns, wx, t_ref, r_ref, i_ref, ghost,
                  stage, fstage, w32, x_ref, a_ref, rows, masks, side, result, sems, column1, tt, big):
    galerkin(1, before_local, labels, t16, plus_y, minus_y, w, local, column1, columns, tt, masks, big)
    copies = []
    for f, (message, column) in enumerate(((x_low, column0), (x_high, column1))):
        elements = [(24 * f + iy, iy * 64) for iy in range(EY)]
        ghost_block(f, message, XT, 0, elements, side_labels, 8 * f, w, (column,), rows, masks, side, result.at[f])
        copies.append(pltpu.make_async_copy(result.at[f], ghost.at[f], sems.at[f]))
        copies[-1].start()
    halo_x(x_low, x_high, wx, stage, fstage, w32)
    start_smoothing(guess, b, inverse, w, wx, x_low, x_high, t_ref, r_ref, i_ref, x_ref, a_ref)
    for copy in copies:
        copy.wait()


def finish_kernel(side_labels, guess, w, wx, coefficients, y_even, y_odd, columns0, columns1, t_in, r_in, i_in, ghost_in,
                  smoothed, ghost, wy, y_low, y_high, stage, fstage, w32, t_ref, r_ref, i_ref, x_ref, a_ref,
                  rows, masks, side, result, sems):
    halo_y(y_even, y_odd, wy, y_low, y_high, stage, fstage, w32)
    label_masks(masks)
    copies = []
    for f, message in enumerate((y_low, y_high)):
        side[...] = jnp.zeros((512, 256), BF16)
        elements = [(8 * ix + 7 * f, ix * 128 + 64 * f) for ix in range(EX)]
        columns = (columns0.at[f], columns1.at[f])
        ghost_block(2 + f, message, YT, 2, elements, side_labels, 16 + 4 * f, w, columns, rows, masks, side, result.at[f])
        copies.append(pltpu.make_async_copy(result.at[f], ghost.at[2 + f], sems.at[f]))
        copies[-1].start()
    smooth(guess, w, wx, wy, coefficients, y_low, y_high, t_in, r_in, i_in, smoothed, t_ref, r_ref, i_ref, x_ref, a_ref)
    for copy in copies:
        copy.wait()


def call(kernel, outs, scratch, operands, flops, moved, in_specs=None, out_specs=None, aliases=None, room=48):
    return pl.pallas_call(
        kernel,
        out_shape=outs,
        in_specs=in_specs or [VMEM] * len(operands),
        out_specs=out_specs or [VMEM] * len(outs),
        scratch_shapes=scratch,
        input_output_aliases=aliases or {},
        cost_estimate=pl.CostEstimate(flops=flops, bytes_accessed=moved, transcendentals=0),
        compiler_params=pltpu.CompilerParams(vmem_limit_bytes=room * 1024 * 1024),
    )(*operands)


def exchange(messages, axis):
    out = []
    for first, message in enumerate(messages):
        pairs = []
        for i in range(first, lax.axis_size(axis) - 1, 2):
            pairs += [(i, i + 1), (i + 1, i)]
        out.append(lax.ppermute(message, axis, pairs))
    return out


def shaped(*shape, dtype=BF16):
    return jax.ShapeDtypeStruct(shape, dtype)


STAGES = [pltpu.VMEM((4, 256, 128), F32), pltpu.VMEM((4, 256, 128), F32), pltpu.VMEM((2048, 128), F32)]


GHOST = [
    pltpu.VMEM((128, 128), F32),
    pltpu.VMEM((64, 256), BF16),
    pltpu.VMEM((512, 256), BF16),
    pltpu.VMEM((2, 256, 256), F32),
    pltpu.SemaphoreType.DMA((2,)),
]


def on_device(blocks, faces, tentative, aggregate, ghost_labels, rhs, guess, bounds):
    wide = lambda *shape: shaped(*shape, dtype=F32)
    rhs = jnp.swapaxes(rhs[0, 0], 1, 2)
    guess = jnp.swapaxes(guess[0, 0], 1, 2)
    labels, side_labels = aggregate.reshape(NE), ghost_labels.reshape(24)
    blocks, faces, tentative = [a.reshape(NE, 4096) for a in (blocks, faces, tentative)]
    even, odd, traces_packed, b_packed, b, diagonal = call(
        pack_x_kernel,
        [shaped(16, XLEN)] * 2 + [shaped(NE, 768)] * 2 + [wide(NRHS * NE, 64), shaped(NE, 128)],
        [pltpu.VMEM((NE, 4096), BF16)] * 3 + [pltpu.VMEM((NRHS, NE, 64), F32)] * 2
        + [STAGES[0], STAGES[2], pltpu.VMEM((2048, 128), BF16)] + [pltpu.VMEM((256, 128), F32)] * 2
        + [pltpu.SemaphoreType.DMA((5,))],
        (blocks, faces, tentative, guess, rhs), 10**6, 2**20, [HBM] * 5, room=62,
    )
    even, odd = exchange((even, odd), "bx")
    half = [wide(256, 256), shaped(256, 512), shaped(2, 256, 256)]
    halves_scratch = [pltpu.VMEM((256, 1024), BF16), GHOST[1], pltpu.VMEM((5, 1024, 256), BF16)]
    w, inverse, coefficients, t16, plus_y, minus_y, local, column0, columns0 = call(
        x_wait_kernel,
        [shaped(2048, 128), wide(NE, 64), wide(8, 128), shaped(2048, 128), shaped(512, 128), shaped(512, 128)] + half,
        STAGES + halves_scratch,
        (labels, side_labels, blocks, faces, tentative, bounds.reshape(1, 2)), 4 * 10**9, 2**22, [SMEM] * 2 + [VMEM] * 4,
    )
    even, odd, x_low, x_high = call(
        pack_y_kernel, [shaped(16, YLEN)] * 2 + [shaped(16, XLEN)] * 2, [],
        (blocks, faces, tentative, traces_packed, b_packed, diagonal, even, odd, column0), 10**8, 2**20,
        [VMEM] * 8 + [ANY],
    )
    even, odd = exchange((even, odd), "by")
    extended = [wide(SPAN, 128)] * 2 + [wide(EXT, 128)]
    fields = [pltpu.VMEM(a.shape, F32) for a in extended]
    pads = [pltpu.VMEM((8 * EXT, 128), F32)] * 2
    local, columns1, wx, traces, residue, inverses, ghost = call(
        y_wait_kernel, [half[0], half[2], shaped(2048, 128)] + extended + [wide(4, 256, 256)],
        STAGES + pads + GHOST + [pltpu.VMEM((256, 512), BF16), halves_scratch[0], halves_scratch[2]],
        (labels, side_labels, t16, plus_y, minus_y, w, local, column0, x_low, x_high, guess, b, inverse), 4 * 10**9, 2**22,
        [SMEM] * 2 + [VMEM] * 11, [VMEM] * 6 + [HBM],
    )
    smoothed, ghost = call(
        finish_kernel, [wide(NRHS, NE, 64), wide(4, 256, 256)],
        [pltpu.VMEM((2048, 128), BF16)] + [pltpu.VMEM((16, YLEN), BF16)] * 2 + STAGES + fields + pads + GHOST,
        (side_labels, guess, w, wx, coefficients, even, odd, columns0, columns1, traces, residue, inverses, ghost),
        10**9, 2**20, [SMEM] + [VMEM] * 11 + [HBM], [VMEM, HBM], {12: 1},
    )
    return jnp.swapaxes(smoothed, 1, 2)[None, None], local[None, None], ghost[None, None]


def solution(mesh):
    b = lambda extra: P("bx", "by", *([None] * extra))
    return jax.shard_map(
        on_device,
        mesh=mesh,
        in_specs=(b(2), b(2), b(2), b(1), b(1), b(3), b(3), P()),
        out_specs=(b(3), b(2), b(3)),
        check_vma=False,
    )
```

```python
import jax
import jax.numpy as jnp
from jax import lax
from jax.experimental import pallas as pl
from jax.experimental.pallas import tpu as pltpu
from jax.sharding import PartitionSpec as P

EX, EY, NE, NRHS = 4, 8, 32, 6
F32, BF16 = jnp.float32, jnp.bfloat16
VMEM = pl.BlockSpec(memory_space=pltpu.VMEM)
SMEM = pl.BlockSpec(memory_space=pltpu.SMEM)
HBM = pl.BlockSpec(memory_space=pltpu.HBM)
ANY = pl.BlockSpec(memory_space=pl.ANY)
NT = (((1,), (1,)), ((), ()))
NN = (((1,), (0,)), ((), ()))

XA = 0
XB = 512
XC = 2560
XD = 3072
XH = 3840
XK = 4224
XT = 4480
XE = 4992
XLEN = 5120
YA, YB = 0, 512
YF = 2560
YD = 3584
YG = 4352
YR = 5120
YT = 5504
YE = 6016
YLEN = 6144

EXT, SPAN = 160, 960


def dot(a, b, dims=NN):
    return lax.dot_general(a, b, dims, preferred_element_type=F32)


def iota(shape, dim):
    return lax.broadcasted_iota(jnp.int32, shape, dim)


def onehot(mask):
    return mask.astype(F32).astype(BF16)


def none(count):
    return jnp.zeros((count, 128), BF16)


def split(x):
    hi = x.astype(BF16)
    return hi, (x - hi.astype(F32)).astype(BF16)


def halves(x):
    lanes = x.shape[1] // 2
    return jnp.concatenate([x[:, :lanes], x[:, lanes:]], 0)


def over(a, b):
    return jnp.concatenate([a, b], 0)


def parity(axis):
    return lax.axis_index(axis) % 2


def with_traces(v):
    q, lane = iota((64, 128), 0), iota((64, 128), 1)
    t = lane % 16
    f = lane // 16 - 4
    along_y = 16 * (t // 4) + t % 4
    source = jnp.where(f == 0, 48 + t, jnp.where(f == 1, t, jnp.where(f == 2, along_y + 12, along_y)))
    pick = onehot(q == jnp.where(f < 0, lane, source))
    hi, lo = split(v)
    return dot(hi, pick) + dot(lo, pick)


def by_element(rows):
    return jnp.concatenate([rows[n * NE : (n + 1) * NE] for n in range(NRHS)], 1)


def pack_lanes(v):
    hi, lo = split(v)
    q, lane = iota((64, 128), 0), iota((64, 128), 1)
    return by_element(dot(hi, onehot(q == lane)) + dot(lo, onehot(q == lane - 64)))


def pack_traces(traces):
    hi, lo = split(traces)
    lane = iota(traces.shape, 1)
    return by_element(jnp.where(lane >= 64, hi.astype(F32), pltpu.roll(lo.astype(F32), 64, 1)))


def squeeze(value, offset):
    lane = iota((8, 128), 1) % 64
    keep = (lane >= offset) & (lane < offset + 16)
    tiles = []
    for first in (0, 4):
        total = jnp.zeros((8, 128), F32)
        for j, n in enumerate(range(first, min(first + 4, NRHS))):
            one = jnp.where(keep, value[:, n * 128 : n * 128 + 128], 0.0)
            total = total + pltpu.roll(one, (16 * j - offset) % 128, 1)
        tiles.append(total)
    return jnp.concatenate(tiles, 1)


def unsqueeze(tiles, n, offset):
    lane = iota((8, 128), 1) % 64
    tile = tiles[:, n // 4 * 128 : n // 4 * 128 + 128]
    moved = pltpu.roll(tile, (offset - 16 * (n % 4)) % 128, 1)
    return jnp.where((lane >= offset) & (lane < offset + 16), moved, 0.0)


TRACE_OFFSET, VALUE_OFFSET = (16, 0), (0, 48)


def pack_x_kernel(blocks_in, faces_in, tent_in, guess_in, rhs_in, odd, even, traces_packed, b_packed, b_out, diagonal,
                  blocks, faces, tent, guess, rhs, stage, w32, w16, x_ref, a_ref, sems):
    copies = [
        pltpu.make_async_copy(source, target, sems.at[i])
        for i, (source, target) in enumerate(
            ((guess_in, guess), (blocks_in, blocks), (rhs_in, rhs), (faces_in, faces), (tent_in, tent))
        )
    ]
    for copy in copies:
        copy.start()
    copies[0].wait()
    v = guess[...].reshape(NRHS * NE, 64)
    traces = with_traces(v)
    t = pack_traces(traces)
    traces_packed[...] = t.astype(BF16)
    x_ref[0:192, :] = traces
    x_ref[192:256, :] = jnp.zeros((64, 128), F32)
    copies[1].wait()
    chunk = lambda c: blocks[:, c * 128 : (c + 1) * 128].astype(F32)
    stage_blocks(chunk, stage)
    diag = diagonals(chunk)
    diagonal[...] = diag.astype(BF16)
    for k in range(4):
        both = stage[k]
        w32[pl.ds(2 * k, 256, stride=8), :] = both
        w32[pl.ds(2 * k + 1, 256, stride=8), :] = pltpu.roll(both, 64, 1)
    w16[...] = w32[...].astype(BF16)
    lane8 = iota((8, 128), 1)
    for e in range(NE):
        hi, lo = split(jnp.where(lane8 < 64, x_ref[pl.ds(e, 8, stride=NE), :], 0.0))
        out = dot(over(hi, lo), w16[e * 64 : e * 64 + 64, :], NT)
        a_ref[pl.ds(e, 8, stride=NE), 0:64] = out[:8] + out[8:]
    for copy in copies[2:]:
        copy.wait()
    b = rhs[...].reshape(NRHS * NE, 64) - a_ref[0:192, 0:64]
    b_out[...] = b
    r = pack_lanes(b)
    b_packed[...] = r.astype(BF16)
    first = parity("bx") == 0

    def put(start, lanes, make):
        low, high = make(0), make(1)
        even[:, start : start + lanes] = jnp.where(first, high, low).astype(BF16)
        odd[:, start : start + lanes] = jnp.where(first, low, high).astype(BF16)

    def rows(k, side):
        return 8 * k if side == 0 else 24 - 8 * k

    def of(ref, k, side, start, lanes):
        row = rows(k, side)
        base = row // 16 * 16
        return ref[base : base + 16, start : start + lanes].astype(F32)[row - base : row - base + 8]

    def packed(value, k, side):
        return value[rows(k, side) : rows(k, side) + 8]

    def face_traces(side):
        return jnp.concatenate([of(faces, 1, side, f * 1024 + 768 * side, 256) for f in range(4)], 1)

    put(XA, 512, lambda s: halves(of(blocks, 0, s, 3072 * s, 1024)))
    for h in range(2):
        put(XB + h * 1024, 1024, lambda s: over(of(faces, 0, s, h * 1024, 1024), of(faces, 0, s, h * 1024 + 2048, 1024)))
    put(XC, 512, lambda s: halves(face_traces(s)))
    put(XD, 768, lambda s: over(packed(t, 0, s), packed(t, 1, s)))
    put(XH, 384, lambda s: halves(packed(r, 0, s)))
    put(XK, 256, lambda s: over(squeeze(packed(t, 2, s), TRACE_OFFSET[s]), squeeze(packed(r, 1, s), VALUE_OFFSET[s])))
    put(XT, 512, lambda s: halves(of(tent, 0, s, 3072 * s, 1024)))
    put(XE, 128, lambda s: over(packed(diag, 0, s), packed(diag, 1, s)))


def pack_y_kernel(blocks, faces, tent, traces_packed, b_packed, diagonal, x_odd, x_even, _, odd, even, low, high):
    first = parity("bx") == 0
    for start in range(0, XLEN, 128):
        a = x_even[:, start : start + 128].astype(F32)
        b = x_odd[:, start : start + 128].astype(F32)
        low[:, start : start + 128] = jnp.where(first, b, a).astype(BF16)
        high[:, start : start + 128] = jnp.where(first, a, b).astype(BF16)
    py = parity("by")
    is_first = py == 0

    def select(k, near=None, far=None, columns=64):
        r, j = iota((16, columns), 0), iota((16, columns), 1)
        high_side = jnp.where(r < 8, py, 1 - py) == 0
        iy = jnp.where(high_side, 7 - k, k)
        row = r % 8 - 2
        source = jnp.where((row >= 0) & (row < 4), row * 8 + iy, -1)
        if near is not None:
            source = jnp.where(row == -1, 32 + near + iy, jnp.where(row == 4, 48 + near + iy, source))
        if far is not None:
            source = jnp.where(row == -2, 32 + far + iy, jnp.where(row == 5, 48 + far + iy, source))
        return onehot(j == source)

    def put(start, value):
        even[:, start : start + value[0].shape[1]] = value[0].astype(BF16)
        odd[:, start : start + value[1].shape[1]] = value[1].astype(BF16)

    def both(make, picked):
        return make(picked[:8]), make(picked[8:])

    cut = []
    for h in range(2):
        source = [faces[:, h * 2048 : h * 2048 + 2048], low[:, XB : XB + 2048], high[:, XB : XB + 2048]]
        cut.append(dot(select(0, 8 * h), jnp.concatenate(source, 0)))
    put(YB, (over(cut[0][:8], cut[1][:8]), over(cut[0][8:], cut[1][8:])))

    def by_side(minus, plus):
        up = jnp.where(is_first, plus[:8], minus[:8])
        down = jnp.where(is_first, minus[8:], plus[8:])
        return halves(up), halves(down)

    own1, own0 = select(1, columns=32), select(0, columns=32)

    def lanes(ref, pieces, width):
        return jnp.concatenate([ref[:, p : p + width] for p in pieces], 1)

    minus, plus = [i * 1024 for i in range(4)], [i * 1024 + 768 for i in range(4)]
    put(YA, by_side(dot(own0, lanes(blocks, minus, 256)), dot(own0, lanes(blocks, plus, 256))))
    put(YT, by_side(dot(own0, lanes(tent, minus, 256)), dot(own0, lanes(tent, plus, 256))))
    minus = [f * 1024 + i * 256 for f in range(4) for i in range(4)]
    plus = [p + 128 for p in minus]
    put(YF, by_side(dot(own1, lanes(faces, minus, 128)), dot(own1, lanes(faces, plus, 128))))
    own = traces_packed[...]
    rows = jnp.concatenate([own, low[:, XD : XD + 768], high[:, XD : XD + 768]], 0)
    g0, g1, g2 = dot(select(0, 0, 8), rows), dot(select(1, 0), rows), dot(select(2, columns=32), own)
    cut = []
    for h in range(2):
        rows = [b_packed[:, h * 384 : h * 384 + 384], low[:, XH : XH + 384], high[:, XH : XH + 384]]
        cut.append(dot(select(0, 8 * h), jnp.concatenate(rows, 0)))
    r0, r1 = jnp.concatenate(cut, 1), dot(own1, b_packed[...])
    put(YD, (over(g0[:8], g1[:8]), over(g0[8:], g1[8:])))
    put(YG, (over(g2[:8], r0[:8]), over(g2[8:], r0[8:])))
    put(YR, both(halves, r1))
    own = diagonal[...]
    d0 = dot(select(0, 0), jnp.concatenate([own, low[:, XE : XE + 128], high[:, XE : XE + 128]], 0))
    d1 = dot(own1, own)
    put(YE, (over(d0[:8], d1[:8]), over(d0[8:], d1[8:])))


def prolongator(tent, t16, plus_y, minus_y, stage, t32):
    lane = iota((256, 128), 1)
    for k in range(4):
        for ph in range(8):
            chunk = tent[:, (ph * 4 + k) * 128 : (ph * 4 + k + 1) * 128].astype(F32)
            stage[k, pl.ds(ph, NE, stride=8), :] = chunk
    for k in range(4):
        both = stage[k]
        other = pltpu.roll(both, 64, 1)
        t32[pl.ds(2 * k, 256, stride=8), :] = jnp.where(lane < 64, both, other)
        t32[pl.ds(2 * k + 1, 256, stride=8), :] = jnp.where(lane < 64, other, both)
    t16[...] = t32[...].astype(BF16)
    sub = iota((8, 128), 0)
    for e in range(NE):
        plus, minus = [], []
        for h in range(2):
            base = e * 64 + 32 * h
            a, b = t32[base + 8 : base + 16, :], t32[base + 24 : base + 32, :]
            plus.append(jnp.where(sub < 4, pltpu.roll(a, 4, 0), b))
            a, b = t32[base : base + 8, :], t32[base + 16 : base + 24, :]
            minus.append(jnp.where(sub < 4, a, pltpu.roll(b, 4, 0)))
        plus_y[e * 16 : e * 16 + 16, :] = jnp.concatenate(plus, 0).astype(BF16)
        minus_y[e * 16 : e * 16 + 16, :] = jnp.concatenate(minus, 0).astype(BF16)


def stage_blocks(block_chunk, stage):
    for k in range(4):
        for ph in range(8):
            stage[k, pl.ds(ph, NE, stride=8), :] = block_chunk(ph * 4 + k)


def diagonals(block_chunk):
    lane = iota((NE, 128), 1)
    diag = jnp.zeros((NE, 128), F32)
    for c in range(32):
        diag = diag + jnp.where((lane == 2 * c) | (lane == 65 + 2 * c), block_chunk(c), 0.0)
    return diag + pltpu.roll(diag, 64, 1)


def reciprocal(diagonal):
    return 1.0 / jnp.where(diagonal == 0.0, 1.0, diagonal)


def operators(block_chunk, face_chunk, w, stage, fstage, w32):
    lane = iota((256, 128), 1)
    stage_blocks(block_chunk, stage)
    for f in range(4):
        for ph in range(8):
            fstage[f, pl.ds(ph, NE, stride=8), :] = face_chunk(f * 8 + ph)
    folded = jnp.concatenate([fstage[f].astype(BF16) for f in range(4)], 1)
    t, lane16 = iota((16, 128), 0), iota((16, 128), 1)
    moves = [onehot(lane16 == 64 + 16 * f + t) for f in range(4)]
    for k in range(4):
        both = stage[k]
        other = pltpu.roll(both, 64, 1)
        for s, part in enumerate((both, other)):
            p_lo = 2 * k + s
            pick = jnp.concatenate([moves[f] if lo == p_lo else none(16) for f in range(4) for lo in range(8)], 0)
            w32[pl.ds(p_lo, 256, stride=8), :] = jnp.where(lane < 64, part, dot(folded, pick))
    w[...] = w32[...].astype(BF16)


def own_operators(blocks, faces, bounds, w, inverse, coefficients, *scratch):
    coefficients[...] = jnp.concatenate([jnp.broadcast_to(c, (1, 128)) for c in factors(bounds)] + [jnp.zeros((3, 128), F32)], 0)
    chunk = lambda ref: lambda c: ref[:, c * 128 : (c + 1) * 128].astype(F32)
    operators(chunk(blocks), chunk(faces), w, *scratch)
    inverse[...] = 1.0 / diagonals(chunk(blocks))[:, :64]


NOTHING = (8, 128)


def part(ref, start, c, half):
    row = 8 * (c // half)
    lane = start + (c % half) * 128
    return ref[:, lane : lane + 128].astype(F32)[row : row + 8]


def halo_x(low, high, w, *scratch):
    zero = jnp.zeros(NOTHING, F32)

    def block(c):
        near_low = part(low, XA, c - 24, 4) if c >= 24 else zero
        near_high = part(high, XA, c, 4) if c < 8 else zero
        return jnp.concatenate([near_low, zero, near_high, zero], 0)

    def face(c):
        f, ph = c // 8, c % 8
        far_low = part(low, XC, f * 2 + ph - 6, 4) if ph >= 6 else zero
        far_high = part(high, XC, f * 2 + ph, 4) if ph < 2 else zero
        return jnp.concatenate([part(low, XB, c, 16), far_low, part(high, XB, c, 16), far_high], 0)

    operators(block, face, w, *scratch)


def halo_y(even, odd, w, low, high, *scratch):
    first = parity("by") == 0
    for start in range(0, YLEN, 128):
        a = even[:, start : start + 128].astype(F32)
        b = odd[:, start : start + 128].astype(F32)
        low[:, start : start + 128] = jnp.where(first, b, a).astype(BF16)
        high[:, start : start + 128] = jnp.where(first, a, b).astype(BF16)
    zero = jnp.zeros(NOTHING, F32)

    def block(c):
        i, d = c // 8, c % 8
        near_low = part(low, YA, i * 2 + d - 6, 4) if d >= 6 else zero
        near_high = part(high, YA, i * 2 + d, 4) if d < 2 else zero
        return jnp.concatenate([near_low, zero, near_high, zero], 0)

    def face(c):
        f, ph = c // 8, c % 8
        i = ph // 2
        far_low = part(low, YF, f * 4 + i, 8) if ph % 2 == 1 else zero
        far_high = part(high, YF, f * 4 + i, 8) if ph % 2 == 0 else zero
        return jnp.concatenate([part(low, YB, c, 16), far_low, part(high, YB, c, 16), far_high], 0)

    operators(block, face, w, *scratch)


def factors(bounds):
    low, high = bounds[0:1, 0:1], bounds[0:1, 1:2]
    centre = 0.5 * (high + low)
    half_width = 0.5 * (high - low)
    spread = centre / half_width
    first = 1.0 / spread
    second = 1.0 / (2.0 * spread - first)
    third = 1.0 / (2.0 * spread - second)
    return centre, half_width, first, second, third


def beside_own(columns):
    return [((ix + 3) * 16 + iy, 0, ix * 8 + iy) for ix in range(EX) for iy in columns]


def beside_x(k, columns):
    return [((7 + k if s else 2 - k) * 16 + iy, 1, s * 16 + k * 8 + iy) for s in range(2) for iy in columns]


def beside_y(k, rows):
    return [((r + 1) * 16 + (8 + k if s else 15 - k), 2, s * 16 + k * 8 + r) for s in range(2) for r in rows]


INNER, OUTER = range(1, 7), (0, 7)
EARLY = (1, 9, beside_own(INNER) + beside_x(0, INNER) + beside_x(1, INNER))
LATE = (1, 9, beside_own(OUTER) + beside_x(0, OUTER) + beside_x(1, OUTER) + beside_y(0, range(1, 7)) + beside_y(1, range(2, 6)))
SECOND = (2, 8, beside_own(range(EY)) + beside_x(0, range(EY)) + beside_y(0, range(2, 6)))
THIRD = (3, 7, beside_own(range(EY)))


def joined(value):
    return value + pltpu.roll(value, 64, 1)


def apply(plan, values, tables, t_ref, x_ref, a_ref):
    first, last, elements = plan
    lane = iota((16, 128), 1)
    x_ref[SPAN:, :] = jnp.zeros((8 * EXT - SPAN, 128), F32)
    for n in range(NRHS):
        for ri in range(first, last):
            row = n * EXT + ri * 16
            own = t_ref[row : row + 16, :]
            sides = jnp.where(
                lane < 80,
                t_ref[row - 16 : row, :],
                jnp.where(
                    lane < 96,
                    t_ref[row + 16 : row + 32, :],
                    jnp.where(lane < 112, pltpu.roll(own, 1, 0), pltpu.roll(own, 15, 0)),
                ),
            )
            x_ref[row : row + 16, :] = jnp.where(lane < 64, own if values else 0.0, sides)
    for row, table, e in elements:
        hi, lo = split(x_ref[pl.ds(row, 8, stride=EXT), :])
        out = dot(over(hi, lo), tables[table][e * 64 : e * 64 + 64, :], NT)
        a_ref[pl.ds(row, 8, stride=EXT), 0:64] = out[:8] + out[8:]


def start_smoothing(guess, b, inverse, w, wx, x_low, x_high, t_ref, r_ref, i_ref, x_ref, a_ref):
    t_ref[...] = jnp.zeros((SPAN, 128), F32)
    r_ref[...] = jnp.zeros((SPAN, 128), F32)
    i_ref[...] = jnp.ones((EXT, 128), F32)
    a_ref[...] = jnp.zeros((8 * EXT, 128), F32)
    traces = with_traces(guess[...].reshape(NRHS * NE, 64))
    for ix in range(EX):
        row = (ix + 3) * 16
        i_ref[row : row + 8, 0:64] = inverse[ix * 8 : ix * 8 + 8, :]
        for n in range(NRHS):
            source = n * NE + ix * 8
            t_ref[n * EXT + row : n * EXT + row + 8, :] = traces[source : source + 8]
            r_ref[n * EXT + row : n * EXT + row + 8, 0:64] = b[source : source + 8, :]
    for side, message in enumerate((x_low, x_high)):
        at = [(7 + k if side else 2 - k) * 16 for k in range(3)]
        near = message[:, XD : XD + 768].astype(F32)
        far = message[:, XK : XK + 256].astype(F32)
        diagonal = reciprocal(message[:, XE : XE + 128].astype(F32))
        for k in range(2):
            i_ref[at[k] : at[k] + 8, :] = diagonal[8 * k : 8 * k + 8]
        for n in range(NRHS):
            base = n * EXT
            for k in range(2):
                t_ref[base + at[k] : base + at[k] + 8, :] = joined(near[8 * k : 8 * k + 8, n * 128 : n * 128 + 128])
            t_ref[base + at[2] : base + at[2] + 8, :] = joined(unsqueeze(far[:8], n, TRACE_OFFSET[1 - side]))
            r_ref[base + at[0] : base + at[0] + 8, :] = joined(part(message, XH, n, 3))
            r_ref[base + at[1] : base + at[1] + 8, :] = joined(unsqueeze(far[8:], n, VALUE_OFFSET[1 - side]))
    apply(EARLY, False, (w, wx), t_ref, x_ref, a_ref)
    r_ref[...] = r_ref[...] - a_ref[:SPAN, :]


def smooth(guess, w, wx, wy, coefficients, y_low, y_high, t_in, r_in, i_in, smoothed, t_ref, r_ref, i_ref, x_ref, a_ref):
    t_ref[...] = t_in[...]
    r_ref[...] = r_in[...]
    i_ref[...] = i_in[...]
    a_ref[:SPAN, :] = jnp.zeros((SPAN, 128), F32)
    for side, message in enumerate((y_low, y_high)):
        column = [16 + (8 + k if side else 15 - k) for k in range(3)]
        diagonal = reciprocal(message[:, YE : YE + 128].astype(F32))
        near = message[:, YD : YD + 768].astype(F32)
        far = message[:, YG : YG + 768].astype(F32)
        for k in range(2):
            i_ref[pl.ds(column[k], 8, stride=16), :] = diagonal[8 * k : 8 * k + 8]
        for n in range(NRHS):
            lanes = slice(n * 128, n * 128 + 128)
            for k, value in enumerate((near[:8, lanes], near[8:, lanes], far[:8, lanes])):
                t_ref[pl.ds(n * EXT + column[k], 8, stride=16), :] = joined(value)
            for k, value in enumerate((far[8:, lanes], part(message, YR, n, 3))):
                r_ref[pl.ds(n * EXT + column[k], 8, stride=16), :] = joined(value)
    tables = (w, wx, wy)
    centre, half_width, first, second, third = [coefficients[i : i + 1, 0:64] for i in range(5)]

    def put_traces(parts, start):
        rows = parts[0].shape[0]
        traces = with_traces(jnp.concatenate(parts, 0))
        for n in range(NRHS):
            t_ref[n * EXT + start : n * EXT + start + rows, :] = traces[n * rows : n * rows + rows]

    apply(LATE, False, tables, t_ref, x_ref, a_ref)
    inverse = i_ref[16:144, 0:64]
    residues, updates = [], []
    for n in range(NRHS):
        rows = slice(n * EXT + 16, n * EXT + 144)
        r = r_ref[rows, 0:64] - a_ref[rows, 0:64]
        residues.append(r[16:112])
        updates.append(inverse * r / centre)
    put_traces(updates, 16)
    apply(SECOND, True, tables, t_ref, x_ref, a_ref)
    inverse = i_ref[32:128, 0:64]
    lasts = []
    for n in range(NRHS):
        residues[n] = residues[n] - a_ref[n * EXT + 32 : n * EXT + 128, 0:64]
        updates[n] = updates[n][16:112]
        lasts.append(second * first * updates[n] + (2.0 * second / half_width) * inverse * residues[n])
    put_traces(lasts, 32)
    apply(THIRD, True, tables, t_ref, x_ref, a_ref)
    for n in range(NRHS):
        for ix in range(EX):
            row, place = n * EXT + (ix + 3) * 16, slice(ix * 8, ix * 8 + 8)
            own = slice(ix * 16 + 16, ix * 16 + 24)
            residue = residues[n][own] - a_ref[row : row + 8, 0:64]
            update = third * second * lasts[n][own] + (2.0 * third / half_width) * inverse[own] * residue
            smoothed[n, place, :] = guess[n, place, :] + updates[n][own] + lasts[n][own] + update


def ghost_rows(message, start, out):
    lane = iota((8, 128), 1)
    for j in range(8):
        both = part(message, start, j, 4)
        other = pltpu.roll(both, 64, 1)
        out[pl.ds(2 * j, 8, stride=16), :] = jnp.where(lane < 64, both, other)
        out[pl.ds(2 * j + 1, 8, stride=16), :] = jnp.where(lane < 64, other, both)


def label_masks(masks):
    lane = iota((16, 256), 1)
    for b in range(4):
        masks[b * 16 : b * 16 + 16, :] = onehot(lane // 64 == b)


def mask_of(masks, label):
    return masks[pl.ds(pl.multiple_of(label * 16, 16), 16), :]


def times(piece, mask):
    return jnp.concatenate([piece, piece], 1) * jnp.concatenate([mask] * 4, 0)


def masked(masks, piece, label):
    return times(piece, mask_of(masks, label))


def face_column(f, rows):
    return jnp.concatenate([none(64 + 16 * f), rows] + ([none(48 - 16 * f)] if f < 3 else []), 0)


def galerkin(half, before_local, labels, t16, plus_y, minus_y, w, local, edge_column, edge_columns, tt, masks, big):
    label_masks(masks)
    lane128 = iota((64, 128), 1)
    for pair in range(8):
        e = 16 * half + 2 * pair
        turned = t16[e * 64 : e * 64 + 128, :].astype(F32).T[:64]
        first, second = labels[e], labels[e + 1]
        for a in range(4):
            keep = jnp.where(
                lane128 < 64,
                jnp.where(first == a, 1.0, 0.0),
                jnp.where(second == a, 1.0, 0.0),
            )
            tt[a * 64 : a * 64 + 64, pair * 128 : pair * 128 + 128] = (turned * keep).astype(BF16)
    edge_column[...] = tt[:, 512 * half : 512 * half + 512]
    for f in range(2):
        for i in range(2):
            start = (4 * i + 3 * f) * 128
            edge_columns[f, :, i * 128 : i * 128 + 128] = tt[:, start : start + 128]

    def row_of_elements(ix, carry):
        for iy in range(EY):
            e = ix * EY + iy
            own = pl.ds(pl.multiple_of(e * 64, 64), 64)
            here = pl.ds(pl.multiple_of((e - 16 * half) * 64, 64), 64)
            before = pl.multiple_of(jnp.maximum(e - 8, 0) * 64, 64)
            after = pl.multiple_of(jnp.minimum(e + 8, 31) * 64, 64)
            rows = [
                t16[pl.ds(before + 48, 16), :],
                t16[pl.ds(after, 16), :],
            ]
            if iy > 0:
                rows.append(plus_y[pl.ds(pl.multiple_of((e - 1) * 16, 16), 16), :])
            else:
                rows.append(none(16))
            if iy < 7:
                rows.append(minus_y[pl.ds(pl.multiple_of((e + 1) * 16, 16), 16), :])
            columns = [jnp.concatenate([t16[own, :], none(64)], 0)]
            columns += [face_column(f, value) for f, value in enumerate(rows)]
            pieces = dot(w[own, :], jnp.concatenate(columns, 1)).astype(BF16)
            piece = lambda s: pieces[:, s * 128 : s * 128 + 128]
            big[0, here, :] = masked(masks, piece(0), labels[e])
            big[1, here, :] = masked(masks, piece(1), labels[jnp.maximum(e - 8, 0)])
            big[2, here, :] = masked(masks, piece(2), labels[jnp.minimum(e + 8, 31)])
            nothing = jnp.zeros((64, 256), BF16)
            big[3, here, :] = masked(masks, piece(3), labels[e - 1]) if iy > 0 else nothing
            big[4, here, :] = masked(masks, piece(4), labels[e + 1]) if iy < 7 else nothing
        return carry

    lax.fori_loop(2 * half, 2 * half + 2, row_of_elements, 0)
    total = dot(tt[...], big[0]) + dot(tt[...], big[3]) + dot(tt[...], big[4])
    if half:
        total = before_local[...] + total + dot(tt[...], big[1]) + dot(tt[:, :512], big[2, :512, :])
    else:
        total = total + dot(tt[:, 512:], big[1, 512:, :]) + dot(tt[...], big[2])
    local[...] = total


def ghost_block(face, message, start, first_row, elements, mask, w, columns, rows, side, result):
    ghost_rows(message, start, rows)
    for i, (e, place) in enumerate(elements):
        near = rows[(i + first_row) * 16 : (i + first_row) * 16 + 16, :].astype(BF16)
        piece = dot(w[e * 64 : e * 64 + 64, :], face_column(face, near)).astype(BF16)
        side[place : place + 64, :] = times(piece, mask(i))
    width = 512 // len(columns)
    result[...] = sum(dot(c[...], side[i * width : (i + 1) * width, :]) for i, c in enumerate(columns))


def x_wait_kernel(labels, _, blocks, faces, tent, bounds, w, inverse, coefficients, t16, plus_y, minus_y, local, column, columns,
                  stage, fstage, w32, tt, masks, big):
    own_operators(blocks, faces, bounds, w, inverse, coefficients, stage, fstage, w32)
    prolongator(tent, t16, plus_y, minus_y, fstage, w32)
    galerkin(0, None, labels, t16, plus_y, minus_y, w, local, column, columns, tt, masks, big)


def y_wait_kernel(labels, side_labels, t16, plus_y, minus_y, w, before_local, column0, x_low, x_high, guess, b, inverse,
                  local, columns, wx, mask_rows, t_ref, r_ref, i_ref, ghost,
                  stage, fstage, w32, x_ref, a_ref, rows, masks, side, result, sems, column1, tt, big):
    galerkin(1, before_local, labels, t16, plus_y, minus_y, w, local, column1, columns, tt, masks, big)
    copies = []
    for f, (message, column) in enumerate(((x_low, column0), (x_high, column1))):
        elements = [(24 * f + iy, iy * 64) for iy in range(EY)]
        mask = lambda i: mask_of(masks, side_labels[8 * f + i])
        ghost_block(f, message, XT, 0, elements, mask, w, (column,), rows, side, result.at[f])
        copies.append(pltpu.make_async_copy(result.at[f], ghost.at[f], sems.at[f]))
        copies[-1].start()
    for i in range(8):
        mask_rows[i * 16 : i * 16 + 16, :] = mask_of(masks, side_labels[16 + i])
    halo_x(x_low, x_high, wx, stage, fstage, w32)
    start_smoothing(guess, b, inverse, w, wx, x_low, x_high, t_ref, r_ref, i_ref, x_ref, a_ref)
    for copy in copies:
        copy.wait()


def finish_kernel(mask_rows, guess, w, wx, coefficients, y_odd, y_even, columns0, columns1, t_in, r_in, i_in, ghost_in,
                  smoothed, ghost, wy, y_low, y_high, stage, fstage, w32, t_ref, r_ref, i_ref, x_ref, a_ref,
                  rows, side, result, sems):
    halo_y(y_even, y_odd, wy, y_low, y_high, stage, fstage, w32)
    copies = []
    for f, message in enumerate((y_low, y_high)):
        side[...] = jnp.zeros((512, 256), BF16)
        elements = [(8 * ix + 7 * f, ix * 128 + 64 * f) for ix in range(EX)]
        columns = (columns0.at[f], columns1.at[f])
        mask = lambda i: mask_rows[(4 * f + i) * 16 : (4 * f + i) * 16 + 16, :]
        ghost_block(2 + f, message, YT, 2, elements, mask, w, columns, rows, side, result.at[f])
        copies.append(pltpu.make_async_copy(result.at[f], ghost.at[2 + f], sems.at[f]))
        copies[-1].start()
    smooth(guess, w, wx, wy, coefficients, y_low, y_high, t_in, r_in, i_in, smoothed, t_ref, r_ref, i_ref, x_ref, a_ref)
    for copy in copies:
        copy.wait()


def call(kernel, outs, scratch, operands, flops, moved, in_specs=None, out_specs=None, aliases=None, room=48):
    return pl.pallas_call(
        kernel,
        out_shape=outs,
        in_specs=in_specs or [VMEM] * len(operands),
        out_specs=out_specs or [VMEM] * len(outs),
        scratch_shapes=scratch,
        input_output_aliases=aliases or {},
        cost_estimate=pl.CostEstimate(flops=flops, bytes_accessed=moved, transcendentals=0),
        compiler_params=pltpu.CompilerParams(vmem_limit_bytes=room * 1024 * 1024),
    )(*operands)


def exchange(messages, axis):
    out = []
    for first, message in zip((1, 0), messages):
        pairs = []
        for i in range(first, lax.axis_size(axis) - 1, 2):
            pairs += [(i, i + 1), (i + 1, i)]
        out.append(lax.ppermute(message, axis, pairs))
    return out


def shaped(*shape, dtype=BF16):
    return jax.ShapeDtypeStruct(shape, dtype)


STAGES = [pltpu.VMEM((4, 256, 128), F32), pltpu.VMEM((4, 256, 128), F32), pltpu.VMEM((2048, 128), F32)]


GHOST = [
    pltpu.VMEM((128, 128), F32),
    pltpu.VMEM((64, 256), BF16),
    pltpu.VMEM((512, 256), BF16),
    pltpu.VMEM((2, 256, 256), F32),
    pltpu.SemaphoreType.DMA((2,)),
]


def on_device(blocks, faces, tentative, aggregate, ghost_labels, rhs, guess, bounds):
    wide = lambda *shape: shaped(*shape, dtype=F32)
    rhs = jnp.swapaxes(rhs[0, 0], 1, 2)
    guess = jnp.swapaxes(guess[0, 0], 1, 2)
    labels, side_labels = aggregate.reshape(NE), ghost_labels.reshape(24)
    blocks, faces, tentative = [a.reshape(NE, 4096) for a in (blocks, faces, tentative)]
    odd, even, traces_packed, b_packed, b, diagonal = call(
        pack_x_kernel,
        [shaped(16, XLEN)] * 2 + [shaped(NE, 768)] * 2 + [wide(NRHS * NE, 64), shaped(NE, 128)],
        [pltpu.VMEM((NE, 4096), BF16)] * 3 + [pltpu.VMEM((NRHS, NE, 64), F32)] * 2
        + [STAGES[0], STAGES[2], pltpu.VMEM((2048, 128), BF16)] + [pltpu.VMEM((256, 128), F32)] * 2
        + [pltpu.SemaphoreType.DMA((5,))],
        (blocks, faces, tentative, guess, rhs), 10**6, 2**20, [HBM] * 5, room=62,
    )
    odd, even = exchange((odd, even), "bx")
    half = [wide(256, 256), shaped(256, 512), shaped(2, 256, 256)]
    halves_scratch = [pltpu.VMEM((256, 1024), BF16), GHOST[1], pltpu.VMEM((5, 1024, 256), BF16)]
    w, inverse, coefficients, t16, plus_y, minus_y, local, column0, columns0 = call(
        x_wait_kernel,
        [shaped(2048, 128), wide(NE, 64), wide(8, 128), shaped(2048, 128), shaped(512, 128), shaped(512, 128)] + half,
        STAGES + halves_scratch,
        (labels, side_labels, blocks, faces, tentative, bounds.reshape(1, 2)), 4 * 10**9, 2**22, [SMEM] * 2 + [VMEM] * 4,
    )
    odd, even, x_low, x_high = call(
        pack_y_kernel, [shaped(16, YLEN)] * 2 + [shaped(16, XLEN)] * 2, [],
        (blocks, faces, tentative, traces_packed, b_packed, diagonal, odd, even, column0), 10**8, 2**20,
        [VMEM] * 8 + [ANY],
    )
    odd, even = exchange((odd, even), "by")
    extended = [wide(SPAN, 128)] * 2 + [wide(EXT, 128)]
    fields = [pltpu.VMEM(a.shape, F32) for a in extended]
    pads = [pltpu.VMEM((8 * EXT, 128), F32)] * 2
    local, columns1, wx, mask_rows, traces, residue, inverses, ghost = call(
        y_wait_kernel, [half[0], half[2], shaped(2048, 128), shaped(128, 256)] + extended + [wide(4, 256, 256)],
        STAGES + pads + GHOST + [pltpu.VMEM((256, 512), BF16), halves_scratch[0], halves_scratch[2]],
        (labels, side_labels, t16, plus_y, minus_y, w, local, column0, x_low, x_high, guess, b, inverse), 4 * 10**9, 2**22,
        [SMEM] * 2 + [VMEM] * 11, [VMEM] * 7 + [HBM],
    )
    smoothed, ghost = call(
        finish_kernel, [wide(NRHS, NE, 64), wide(4, 256, 256)],
        [pltpu.VMEM((2048, 128), BF16)] + [pltpu.VMEM((16, YLEN), BF16)] * 2 + STAGES + fields + pads + GHOST[:1] + GHOST[2:],
        (mask_rows, guess, w, wx, coefficients, odd, even, columns0, columns1, traces, residue, inverses, ghost),
        10**9, 2**20, [VMEM] * 12 + [HBM], [VMEM, HBM], {12: 1},
    )
    return jnp.swapaxes(smoothed, 1, 2)[None, None], local[None, None], ghost[None, None]


def solution(mesh):
    b = lambda extra: P("bx", "by", *([None] * extra))
    return jax.shard_map(
        on_device,
        mesh=mesh,
        in_specs=(b(2), b(2), b(2), b(1), b(1), b(3), b(3), P()),
        out_specs=(b(3), b(2), b(3)),
        check_vma=False,
    )
```

```python
import jax
import jax.numpy as jnp
from jax import lax
from jax.experimental import pallas as pl
from jax.experimental.pallas import tpu as pltpu
from jax.sharding import PartitionSpec as P

EX, EY, NE, NRHS = 4, 8, 32, 6
F32, BF16 = jnp.float32, jnp.bfloat16
VMEM = pl.BlockSpec(memory_space=pltpu.VMEM)
SMEM = pl.BlockSpec(memory_space=pltpu.SMEM)
HBM = pl.BlockSpec(memory_space=pltpu.HBM)
ANY = pl.BlockSpec(memory_space=pl.ANY)
NT = (((1,), (1,)), ((), ()))
NN = (((1,), (0,)), ((), ()))

XA = 0
XB = 512
XC = 2560
XD = 3072
XH = 3840
XK = 4224
XT = 4480
XE = 4992
XLEN = 5120
YA, YB = 0, 512
YF = 2560
YD = 3584
YG = 4352
YR = 5120
YT = 5504
YE = 6016
YLEN = 6144

EXT, SPAN = 160, 960


def dot(a, b, dims=NN):
    return lax.dot_general(a, b, dims, preferred_element_type=F32)


def iota(shape, dim):
    return lax.broadcasted_iota(jnp.int32, shape, dim)


def onehot(mask):
    return mask.astype(F32).astype(BF16)


def none(count):
    return jnp.zeros((count, 128), BF16)


def split(x):
    hi = x.astype(BF16)
    return hi, (x - hi.astype(F32)).astype(BF16)


def halves(x):
    lanes = x.shape[1] // 2
    return jnp.concatenate([x[:, :lanes], x[:, lanes:]], 0)


def over(a, b):
    return jnp.concatenate([a, b], 0)


def parity(axis):
    return lax.axis_index(axis) % 2


def with_traces(v):
    q, lane = iota((64, 128), 0), iota((64, 128), 1)
    t = lane % 16
    f = lane // 16 - 4
    along_y = 16 * (t // 4) + t % 4
    source = jnp.where(f == 0, 48 + t, jnp.where(f == 1, t, jnp.where(f == 2, along_y + 12, along_y)))
    pick = onehot(q == jnp.where(f < 0, lane, source))
    hi, lo = split(v)
    return dot(hi, pick) + dot(lo, pick)


def by_element(rows):
    return jnp.concatenate([rows[n * NE : (n + 1) * NE] for n in range(NRHS)], 1)


def pack_lanes(v):
    hi, lo = split(v)
    q, lane = iota((64, 128), 0), iota((64, 128), 1)
    return by_element(dot(hi, onehot(q == lane)) + dot(lo, onehot(q == lane - 64)))


def pack_traces(traces):
    hi, lo = split(traces)
    lane = iota(traces.shape, 1)
    return by_element(jnp.where(lane >= 64, hi.astype(F32), pltpu.roll(lo.astype(F32), 64, 1)))


def squeeze(value, offset):
    lane = iota((8, 128), 1) % 64
    keep = (lane >= offset) & (lane < offset + 16)
    tiles = []
    for first in (0, 4):
        total = jnp.zeros((8, 128), F32)
        for j, n in enumerate(range(first, min(first + 4, NRHS))):
            one = jnp.where(keep, value[:, n * 128 : n * 128 + 128], 0.0)
            total = total + pltpu.roll(one, (16 * j - offset) % 128, 1)
        tiles.append(total)
    return jnp.concatenate(tiles, 1)


def unsqueeze(tiles, n, offset):
    lane = iota((8, 128), 1) % 64
    tile = tiles[:, n // 4 * 128 : n // 4 * 128 + 128]
    moved = pltpu.roll(tile, (offset - 16 * (n % 4)) % 128, 1)
    return jnp.where((lane >= offset) & (lane < offset + 16), moved, 0.0)


TRACE_OFFSET, VALUE_OFFSET = (16, 0), (0, 48)


def pack_x_kernel(blocks_in, faces_in, tent_in, guess_in, rhs_in, even, odd, traces_packed, b_packed, b_out, diagonal,
                  blocks, faces, tent, guess, rhs, stage, w32, w16, x_ref, a_ref, sems):
    copies = [
        pltpu.make_async_copy(source, target, sems.at[i])
        for i, (source, target) in enumerate(
            ((guess_in, guess), (blocks_in, blocks), (rhs_in, rhs), (faces_in, faces), (tent_in, tent))
        )
    ]
    for copy in copies:
        copy.start()
    copies[0].wait()
    v = guess[...].reshape(NRHS * NE, 64)
    traces = with_traces(v)
    t = pack_traces(traces)
    traces_packed[...] = t.astype(BF16)
    x_ref[0:192, :] = traces
    x_ref[192:256, :] = jnp.zeros((64, 128), F32)
    copies[1].wait()
    chunk = lambda c: blocks[:, c * 128 : (c + 1) * 128].astype(F32)
    stage_blocks(chunk, stage)
    diag = diagonals(chunk)
    diagonal[...] = diag.astype(BF16)
    for k in range(4):
        both = stage[k]
        w32[pl.ds(2 * k, 256, stride=8), :] = both
        w32[pl.ds(2 * k + 1, 256, stride=8), :] = pltpu.roll(both, 64, 1)
    w16[...] = w32[...].astype(BF16)
    lane8 = iota((8, 128), 1)
    for e in range(NE):
        hi, lo = split(jnp.where(lane8 < 64, x_ref[pl.ds(e, 8, stride=NE), :], 0.0))
        out = dot(over(hi, lo), w16[e * 64 : e * 64 + 64, :], NT)
        a_ref[pl.ds(e, 8, stride=NE), 0:64] = out[:8] + out[8:]
    for copy in copies[2:]:
        copy.wait()
    b = rhs[...].reshape(NRHS * NE, 64) - a_ref[0:192, 0:64]
    b_out[...] = b
    r = pack_lanes(b)
    b_packed[...] = r.astype(BF16)
    first = parity("bx") == 0

    def put(start, lanes, make):
        low, high = make(0), make(1)
        even[:, start : start + lanes] = jnp.where(first, high, low).astype(BF16)
        odd[:, start : start + lanes] = jnp.where(first, low, high).astype(BF16)

    def rows(k, side):
        return 8 * k if side == 0 else 24 - 8 * k

    def of(ref, k, side, start, lanes):
        row = rows(k, side)
        base = row // 16 * 16
        return ref[base : base + 16, start : start + lanes].astype(F32)[row - base : row - base + 8]

    def packed(value, k, side):
        return value[rows(k, side) : rows(k, side) + 8]

    def face_traces(side):
        return jnp.concatenate([of(faces, 1, side, f * 1024 + 768 * side, 256) for f in range(4)], 1)

    put(XA, 512, lambda s: halves(of(blocks, 0, s, 3072 * s, 1024)))
    for h in range(2):
        put(XB + h * 1024, 1024, lambda s: over(of(faces, 0, s, h * 1024, 1024), of(faces, 0, s, h * 1024 + 2048, 1024)))
    put(XC, 512, lambda s: halves(face_traces(s)))
    put(XD, 768, lambda s: over(packed(t, 0, s), packed(t, 1, s)))
    put(XH, 384, lambda s: halves(packed(r, 0, s)))
    put(XK, 256, lambda s: over(squeeze(packed(t, 2, s), TRACE_OFFSET[s]), squeeze(packed(r, 1, s), VALUE_OFFSET[s])))
    put(XT, 512, lambda s: halves(of(tent, 0, s, 3072 * s, 1024)))
    put(XE, 128, lambda s: over(packed(diag, 0, s), packed(diag, 1, s)))


def pack_y_kernel(blocks, faces, tent, traces_packed, b_packed, diagonal, x_even, x_odd, _, odd, even, low, high):
    first = parity("bx") == 0
    for start in range(0, XLEN, 128):
        a = x_even[:, start : start + 128].astype(F32)
        b = x_odd[:, start : start + 128].astype(F32)
        low[:, start : start + 128] = jnp.where(first, b, a).astype(BF16)
        high[:, start : start + 128] = jnp.where(first, a, b).astype(BF16)
    py = parity("by")
    is_first = py == 0

    def select(k, near=None, far=None, columns=64):
        r, j = iota((16, columns), 0), iota((16, columns), 1)
        high_side = jnp.where(r < 8, py, 1 - py) == 0
        iy = jnp.where(high_side, 7 - k, k)
        row = r % 8 - 2
        source = jnp.where((row >= 0) & (row < 4), row * 8 + iy, -1)
        if near is not None:
            source = jnp.where(row == -1, 32 + near + iy, jnp.where(row == 4, 48 + near + iy, source))
        if far is not None:
            source = jnp.where(row == -2, 32 + far + iy, jnp.where(row == 5, 48 + far + iy, source))
        return onehot(j == source)

    def put(start, value):
        even[:, start : start + value[0].shape[1]] = value[0].astype(BF16)
        odd[:, start : start + value[1].shape[1]] = value[1].astype(BF16)

    def both(make, picked):
        return make(picked[:8]), make(picked[8:])

    cut = []
    for h in range(2):
        source = [faces[:, h * 2048 : h * 2048 + 2048], low[:, XB : XB + 2048], high[:, XB : XB + 2048]]
        cut.append(dot(select(0, 8 * h), jnp.concatenate(source, 0)))
    put(YB, (over(cut[0][:8], cut[1][:8]), over(cut[0][8:], cut[1][8:])))

    def by_side(minus, plus):
        up = jnp.where(is_first, plus[:8], minus[:8])
        down = jnp.where(is_first, minus[8:], plus[8:])
        return halves(up), halves(down)

    own1, own0 = select(1, columns=32), select(0, columns=32)

    def lanes(ref, pieces, width):
        return jnp.concatenate([ref[:, p : p + width] for p in pieces], 1)

    minus, plus = [i * 1024 for i in range(4)], [i * 1024 + 768 for i in range(4)]
    put(YA, by_side(dot(own0, lanes(blocks, minus, 256)), dot(own0, lanes(blocks, plus, 256))))
    put(YT, by_side(dot(own0, lanes(tent, minus, 256)), dot(own0, lanes(tent, plus, 256))))
    minus = [f * 1024 + i * 256 for f in range(4) for i in range(4)]
    plus = [p + 128 for p in minus]
    put(YF, by_side(dot(own1, lanes(faces, minus, 128)), dot(own1, lanes(faces, plus, 128))))
    own = traces_packed[...]
    rows = jnp.concatenate([own, low[:, XD : XD + 768], high[:, XD : XD + 768]], 0)
    g0, g1, g2 = dot(select(0, 0, 8), rows), dot(select(1, 0), rows), dot(select(2, columns=32), own)
    cut = []
    for h in range(2):
        rows = [b_packed[:, h * 384 : h * 384 + 384], low[:, XH : XH + 384], high[:, XH : XH + 384]]
        cut.append(dot(select(0, 8 * h), jnp.concatenate(rows, 0)))
    r0, r1 = jnp.concatenate(cut, 1), dot(own1, b_packed[...])
    put(YD, (over(g0[:8], g1[:8]), over(g0[8:], g1[8:])))
    put(YG, (over(g2[:8], r0[:8]), over(g2[8:], r0[8:])))
    put(YR, both(halves, r1))
    own = diagonal[...]
    d0 = dot(select(0, 0), jnp.concatenate([own, low[:, XE : XE + 128], high[:, XE : XE + 128]], 0))
    d1 = dot(own1, own)
    put(YE, (over(d0[:8], d1[:8]), over(d0[8:], d1[8:])))


def prolongator(tent, t16, plus_y, minus_y, stage, t32):
    lane = iota((256, 128), 1)
    for k in range(4):
        for ph in range(8):
            chunk = tent[:, (ph * 4 + k) * 128 : (ph * 4 + k + 1) * 128].astype(F32)
            stage[k, pl.ds(ph, NE, stride=8), :] = chunk
    for k in range(4):
        both = stage[k]
        other = pltpu.roll(both, 64, 1)
        t32[pl.ds(2 * k, 256, stride=8), :] = jnp.where(lane < 64, both, other)
        t32[pl.ds(2 * k + 1, 256, stride=8), :] = jnp.where(lane < 64, other, both)
    t16[...] = t32[...].astype(BF16)
    sub = iota((8, 128), 0)
    for e in range(NE):
        plus, minus = [], []
        for h in range(2):
            base = e * 64 + 32 * h
            a, b = t32[base + 8 : base + 16, :], t32[base + 24 : base + 32, :]
            plus.append(jnp.where(sub < 4, pltpu.roll(a, 4, 0), b))
            a, b = t32[base : base + 8, :], t32[base + 16 : base + 24, :]
            minus.append(jnp.where(sub < 4, a, pltpu.roll(b, 4, 0)))
        plus_y[e * 16 : e * 16 + 16, :] = jnp.concatenate(plus, 0).astype(BF16)
        minus_y[e * 16 : e * 16 + 16, :] = jnp.concatenate(minus, 0).astype(BF16)


def stage_blocks(block_chunk, stage):
    for k in range(4):
        for ph in range(8):
            stage[k, pl.ds(ph, NE, stride=8), :] = block_chunk(ph * 4 + k)


def diagonals(block_chunk):
    lane = iota((NE, 128), 1)
    diag = jnp.zeros((NE, 128), F32)
    for c in range(32):
        diag = diag + jnp.where((lane == 2 * c) | (lane == 65 + 2 * c), block_chunk(c), 0.0)
    return diag + pltpu.roll(diag, 64, 1)


def reciprocal(diagonal):
    return 1.0 / jnp.where(diagonal == 0.0, 1.0, diagonal)


def operators(block_chunk, face_chunk, w, stage, fstage, w32):
    lane = iota((256, 128), 1)
    stage_blocks(block_chunk, stage)
    for f in range(4):
        for ph in range(8):
            fstage[f, pl.ds(ph, NE, stride=8), :] = face_chunk(f * 8 + ph)
    folded = jnp.concatenate([fstage[f].astype(BF16) for f in range(4)], 1)
    t, lane16 = iota((16, 128), 0), iota((16, 128), 1)
    moves = [onehot(lane16 == 64 + 16 * f + t) for f in range(4)]
    for k in range(4):
        both = stage[k]
        other = pltpu.roll(both, 64, 1)
        for s, part in enumerate((both, other)):
            p_lo = 2 * k + s
            pick = jnp.concatenate([moves[f] if lo == p_lo else none(16) for f in range(4) for lo in range(8)], 0)
            w32[pl.ds(p_lo, 256, stride=8), :] = jnp.where(lane < 64, part, dot(folded, pick))
    w[...] = w32[...].astype(BF16)


def own_operators(blocks, faces, bounds, w, inverse, coefficients, *scratch):
    coefficients[...] = jnp.concatenate([jnp.broadcast_to(c, (1, 128)) for c in factors(bounds)] + [jnp.zeros((3, 128), F32)], 0)
    chunk = lambda ref: lambda c: ref[:, c * 128 : (c + 1) * 128].astype(F32)
    operators(chunk(blocks), chunk(faces), w, *scratch)
    inverse[...] = 1.0 / diagonals(chunk(blocks))[:, :64]


NOTHING = (8, 128)


def part(ref, start, c, half):
    row = 8 * (c // half)
    lane = start + (c % half) * 128
    return ref[:, lane : lane + 128].astype(F32)[row : row + 8]


def halo_x(low, high, w, *scratch):
    zero = jnp.zeros(NOTHING, F32)

    def block(c):
        near_low = part(low, XA, c - 24, 4) if c >= 24 else zero
        near_high = part(high, XA, c, 4) if c < 8 else zero
        return jnp.concatenate([near_low, zero, near_high, zero], 0)

    def face(c):
        f, ph = c // 8, c % 8
        far_low = part(low, XC, f * 2 + ph - 6, 4) if ph >= 6 else zero
        far_high = part(high, XC, f * 2 + ph, 4) if ph < 2 else zero
        return jnp.concatenate([part(low, XB, c, 16), far_low, part(high, XB, c, 16), far_high], 0)

    operators(block, face, w, *scratch)


def halo_y(even, odd, w, low, high, *scratch):
    first = parity("by") == 0
    for start in range(0, YLEN, 128):
        a = even[:, start : start + 128].astype(F32)
        b = odd[:, start : start + 128].astype(F32)
        low[:, start : start + 128] = jnp.where(first, b, a).astype(BF16)
        high[:, start : start + 128] = jnp.where(first, a, b).astype(BF16)
    zero = jnp.zeros(NOTHING, F32)

    def block(c):
        i, d = c // 8, c % 8
        near_low = part(low, YA, i * 2 + d - 6, 4) if d >= 6 else zero
        near_high = part(high, YA, i * 2 + d, 4) if d < 2 else zero
        return jnp.concatenate([near_low, zero, near_high, zero], 0)

    def face(c):
        f, ph = c // 8, c % 8
        i = ph // 2
        far_low = part(low, YF, f * 4 + i, 8) if ph % 2 == 1 else zero
        far_high = part(high, YF, f * 4 + i, 8) if ph % 2 == 0 else zero
        return jnp.concatenate([part(low, YB, c, 16), far_low, part(high, YB, c, 16), far_high], 0)

    operators(block, face, w, *scratch)


def factors(bounds):
    low, high = bounds[0:1, 0:1], bounds[0:1, 1:2]
    centre = 0.5 * (high + low)
    half_width = 0.5 * (high - low)
    spread = centre / half_width
    first = 1.0 / spread
    second = 1.0 / (2.0 * spread - first)
    third = 1.0 / (2.0 * spread - second)
    return centre, half_width, first, second, third


def beside_own(columns):
    return [((ix + 3) * 16 + iy, 0, ix * 8 + iy) for ix in range(EX) for iy in columns]


def beside_x(k, columns):
    return [((7 + k if s else 2 - k) * 16 + iy, 1, s * 16 + k * 8 + iy) for s in range(2) for iy in columns]


def beside_y(k, rows):
    return [((r + 1) * 16 + (8 + k if s else 15 - k), 2, s * 16 + k * 8 + r) for s in range(2) for r in rows]


INNER, OUTER = range(1, 7), (0, 7)
EARLY = (1, 9, beside_own(INNER) + beside_x(0, INNER) + beside_x(1, INNER))
LATE = (1, 9, beside_own(OUTER) + beside_x(0, OUTER) + beside_x(1, OUTER) + beside_y(0, range(1, 7)) + beside_y(1, range(2, 6)))
SECOND = (2, 8, beside_own(range(EY)) + beside_x(0, range(EY)) + beside_y(0, range(2, 6)))
THIRD = (3, 7, beside_own(range(EY)))


def joined(value):
    return value + pltpu.roll(value, 64, 1)


def apply(plan, values, tables, t_ref, x_ref, a_ref):
    first, last, elements = plan
    lane = iota((16, 128), 1)
    x_ref[SPAN:, :] = jnp.zeros((8 * EXT - SPAN, 128), F32)
    for n in range(NRHS):
        for ri in range(first, last):
            row = n * EXT + ri * 16
            own = t_ref[row : row + 16, :]
            sides = jnp.where(
                lane < 80,
                t_ref[row - 16 : row, :],
                jnp.where(
                    lane < 96,
                    t_ref[row + 16 : row + 32, :],
                    jnp.where(lane < 112, pltpu.roll(own, 1, 0), pltpu.roll(own, 15, 0)),
                ),
            )
            x_ref[row : row + 16, :] = jnp.where(lane < 64, own if values else 0.0, sides)
    for row, table, e in elements:
        hi, lo = split(x_ref[pl.ds(row, 8, stride=EXT), :])
        out = dot(over(hi, lo), tables[table][e * 64 : e * 64 + 64, :], NT)
        a_ref[pl.ds(row, 8, stride=EXT), 0:64] = out[:8] + out[8:]


def start_smoothing(guess, b, inverse, w, wx, x_low, x_high, t_ref, r_ref, i_ref, x_ref, a_ref):
    t_ref[...] = jnp.zeros((SPAN, 128), F32)
    r_ref[...] = jnp.zeros((SPAN, 128), F32)
    i_ref[...] = jnp.ones((EXT, 128), F32)
    a_ref[...] = jnp.zeros((8 * EXT, 128), F32)
    traces = with_traces(guess[...].reshape(NRHS * NE, 64))
    for ix in range(EX):
        row = (ix + 3) * 16
        i_ref[row : row + 8, 0:64] = inverse[ix * 8 : ix * 8 + 8, :]
        for n in range(NRHS):
            source = n * NE + ix * 8
            t_ref[n * EXT + row : n * EXT + row + 8, :] = traces[source : source + 8]
            r_ref[n * EXT + row : n * EXT + row + 8, 0:64] = b[source : source + 8, :]
    for side, message in enumerate((x_low, x_high)):
        at = [(7 + k if side else 2 - k) * 16 for k in range(3)]
        near = message[:, XD : XD + 768].astype(F32)
        far = message[:, XK : XK + 256].astype(F32)
        diagonal = reciprocal(message[:, XE : XE + 128].astype(F32))
        for k in range(2):
            i_ref[at[k] : at[k] + 8, :] = diagonal[8 * k : 8 * k + 8]
        for n in range(NRHS):
            base = n * EXT
            for k in range(2):
                t_ref[base + at[k] : base + at[k] + 8, :] = joined(near[8 * k : 8 * k + 8, n * 128 : n * 128 + 128])
            t_ref[base + at[2] : base + at[2] + 8, :] = joined(unsqueeze(far[:8], n, TRACE_OFFSET[1 - side]))
            r_ref[base + at[0] : base + at[0] + 8, :] = joined(part(message, XH, n, 3))
            r_ref[base + at[1] : base + at[1] + 8, :] = joined(unsqueeze(far[8:], n, VALUE_OFFSET[1 - side]))
    apply(EARLY, False, (w, wx), t_ref, x_ref, a_ref)
    r_ref[...] = r_ref[...] - a_ref[:SPAN, :]


def smooth(guess, w, wx, wy, coefficients, y_low, y_high, t_in, r_in, i_in, smoothed, t_ref, r_ref, i_ref, x_ref, a_ref):
    t_ref[...] = t_in[...]
    r_ref[...] = r_in[...]
    i_ref[...] = i_in[...]
    a_ref[:SPAN, :] = jnp.zeros((SPAN, 128), F32)
    for side, message in enumerate((y_low, y_high)):
        column = [16 + (8 + k if side else 15 - k) for k in range(3)]
        diagonal = reciprocal(message[:, YE : YE + 128].astype(F32))
        near = message[:, YD : YD + 768].astype(F32)
        far = message[:, YG : YG + 768].astype(F32)
        for k in range(2):
            i_ref[pl.ds(column[k], 8, stride=16), :] = diagonal[8 * k : 8 * k + 8]
        for n in range(NRHS):
            lanes = slice(n * 128, n * 128 + 128)
            for k, value in enumerate((near[:8, lanes], near[8:, lanes], far[:8, lanes])):
                t_ref[pl.ds(n * EXT + column[k], 8, stride=16), :] = joined(value)
            for k, value in enumerate((far[8:, lanes], part(message, YR, n, 3))):
                r_ref[pl.ds(n * EXT + column[k], 8, stride=16), :] = joined(value)
    tables = (w, wx, wy)
    centre, half_width, first, second, third = [coefficients[i : i + 1, 0:64] for i in range(5)]

    def put_traces(parts, start):
        rows = parts[0].shape[0]
        traces = with_traces(jnp.concatenate(parts, 0))
        for n in range(NRHS):
            t_ref[n * EXT + start : n * EXT + start + rows, :] = traces[n * rows : n * rows + rows]

    apply(LATE, False, tables, t_ref, x_ref, a_ref)
    inverse = i_ref[16:144, 0:64]
    residues, updates = [], []
    for n in range(NRHS):
        rows = slice(n * EXT + 16, n * EXT + 144)
        r = r_ref[rows, 0:64] - a_ref[rows, 0:64]
        residues.append(r[16:112])
        updates.append(inverse * r / centre)
    put_traces(updates, 16)
    apply(SECOND, True, tables, t_ref, x_ref, a_ref)
    inverse = i_ref[32:128, 0:64]
    lasts = []
    for n in range(NRHS):
        residues[n] = residues[n] - a_ref[n * EXT + 32 : n * EXT + 128, 0:64]
        updates[n] = updates[n][16:112]
        lasts.append(second * first * updates[n] + (2.0 * second / half_width) * inverse * residues[n])
    put_traces(lasts, 32)
    apply(THIRD, True, tables, t_ref, x_ref, a_ref)
    for n in range(NRHS):
        for ix in range(EX):
            row, place = n * EXT + (ix + 3) * 16, slice(ix * 8, ix * 8 + 8)
            own = slice(ix * 16 + 16, ix * 16 + 24)
            residue = residues[n][own] - a_ref[row : row + 8, 0:64]
            update = third * second * lasts[n][own] + (2.0 * third / half_width) * inverse[own] * residue
            smoothed[n, place, :] = guess[n, place, :] + updates[n][own] + lasts[n][own] + update


def ghost_rows(message, start, out):
    lane = iota((8, 128), 1)
    for j in range(8):
        both = part(message, start, j, 4)
        other = pltpu.roll(both, 64, 1)
        out[pl.ds(2 * j, 8, stride=16), :] = jnp.where(lane < 64, both, other)
        out[pl.ds(2 * j + 1, 8, stride=16), :] = jnp.where(lane < 64, other, both)


def label_masks(masks):
    lane = iota((16, 256), 1)
    for b in range(4):
        masks[b * 16 : b * 16 + 16, :] = onehot(lane // 64 == b)


def mask_of(masks, label):
    return masks[pl.ds(pl.multiple_of(label * 16, 16), 16), :]


def times(piece, mask):
    return jnp.concatenate([piece, piece], 1) * jnp.concatenate([mask] * 4, 0)


def masked(masks, piece, label):
    return times(piece, mask_of(masks, label))


def face_column(f, rows):
    return jnp.concatenate([none(64 + 16 * f), rows] + ([none(48 - 16 * f)] if f < 3 else []), 0)


ROWS_EARLY = 3


def galerkin(late, before_local, labels, t16, plus_y, minus_y, w, local, edge_column, edge_columns, tt, masks, big):
    first_row, last_row = (ROWS_EARLY, EX) if late else (0, ROWS_EARLY)
    rows = last_row - first_row
    label_masks(masks)
    lane128 = iota((64, 128), 1)
    for pair in range(4 * rows):
        e = 8 * first_row + 2 * pair
        turned = t16[e * 64 : e * 64 + 128, :].astype(F32).T[:64]
        first, second = labels[e], labels[e + 1]
        for a in range(4):
            keep = jnp.where(
                lane128 < 64,
                jnp.where(first == a, 1.0, 0.0),
                jnp.where(second == a, 1.0, 0.0),
            )
            tt[a * 64 : a * 64 + 64, pair * 128 : pair * 128 + 128] = (turned * keep).astype(BF16)
    edge_column[...] = tt[:, 512 * rows - 512 :] if late else tt[:, :512]
    for f in range(2):
        for i in range(rows):
            start = (4 * i + 3 * f) * 128
            edge_columns[f, :, i * 128 : i * 128 + 128] = tt[:, start : start + 128]

    def row_of_elements(ix, carry):
        for iy in range(EY):
            e = ix * EY + iy
            own = pl.ds(pl.multiple_of(e * 64, 64), 64)
            here = pl.ds(pl.multiple_of((e - 8 * first_row) * 64, 64), 64)
            before = pl.multiple_of(jnp.maximum(e - 8, 0) * 64, 64)
            after = pl.multiple_of(jnp.minimum(e + 8, 31) * 64, 64)
            rows = [
                t16[pl.ds(before + 48, 16), :],
                t16[pl.ds(after, 16), :],
            ]
            if iy > 0:
                rows.append(plus_y[pl.ds(pl.multiple_of((e - 1) * 16, 16), 16), :])
            else:
                rows.append(none(16))
            if iy < 7:
                rows.append(minus_y[pl.ds(pl.multiple_of((e + 1) * 16, 16), 16), :])
            columns = [jnp.concatenate([t16[own, :], none(64)], 0)]
            columns += [face_column(f, value) for f, value in enumerate(rows)]
            pieces = dot(w[own, :], jnp.concatenate(columns, 1)).astype(BF16)
            piece = lambda s: pieces[:, s * 128 : s * 128 + 128]
            big[0, here, :] = masked(masks, piece(0), labels[e])
            big[1, here, :] = masked(masks, piece(1), labels[jnp.maximum(e - 8, 0)])
            big[2, here, :] = masked(masks, piece(2), labels[jnp.minimum(e + 8, 31)])
            nothing = jnp.zeros((64, 256), BF16)
            big[3, here, :] = masked(masks, piece(3), labels[e - 1]) if iy > 0 else nothing
            big[4, here, :] = masked(masks, piece(4), labels[e + 1]) if iy < 7 else nothing
        return carry

    lax.fori_loop(first_row, last_row, row_of_elements, 0)
    total = dot(tt[...], big[0]) + dot(tt[...], big[3]) + dot(tt[...], big[4])
    if late:
        total = before_local[...] + total + dot(tt[...], big[1])
        if rows > 1:
            total = total + dot(tt[:, : 512 * rows - 512], big[2, : 512 * rows - 512, :])
    else:
        total = total + dot(tt[...], big[2])
        if rows > 1:
            total = total + dot(tt[:, 512:], big[1, 512:, :])
    local[...] = total


def ghost_block(face, message, start, first_row, elements, mask, w, columns, rows, side, result):
    ghost_rows(message, start, rows)
    for i, (e, place) in enumerate(elements):
        near = rows[(i + first_row) * 16 : (i + first_row) * 16 + 16, :].astype(BF16)
        piece = dot(w[e * 64 : e * 64 + 64, :], face_column(face, near)).astype(BF16)
        side[place : place + 64, :] = times(piece, mask(i))
    total, start = 0.0, 0
    for c in columns:
        width = c.shape[-1]
        total = total + dot(c[...], side[start : start + width, :])
        start += width
    result[...] = total


def x_wait_kernel(labels, _, blocks, faces, tent, bounds, w, inverse, coefficients, t16, plus_y, minus_y, local, column, columns,
                  stage, fstage, w32, tt, masks, big):
    own_operators(blocks, faces, bounds, w, inverse, coefficients, stage, fstage, w32)
    prolongator(tent, t16, plus_y, minus_y, fstage, w32)
    galerkin(0, None, labels, t16, plus_y, minus_y, w, local, column, columns, tt, masks, big)


def y_wait_kernel(labels, side_labels, t16, plus_y, minus_y, w, before_local, column0, x_low, x_high, guess, b, inverse,
                  local, columns, wx, mask_rows, t_ref, r_ref, i_ref, ghost,
                  stage, fstage, w32, x_ref, a_ref, rows, masks, side, result, sems, column1, tt, big):
    galerkin(1, before_local, labels, t16, plus_y, minus_y, w, local, column1, columns, tt, masks, big)
    copies = []
    for f, (message, column) in enumerate(((x_low, column0), (x_high, column1))):
        elements = [(24 * f + iy, iy * 64) for iy in range(EY)]
        mask = lambda i: mask_of(masks, side_labels[8 * f + i])
        ghost_block(f, message, XT, 0, elements, mask, w, (column,), rows, side, result.at[f])
        copies.append(pltpu.make_async_copy(result.at[f], ghost.at[f], sems.at[f]))
        copies[-1].start()
    for i in range(8):
        mask_rows[i * 16 : i * 16 + 16, :] = mask_of(masks, side_labels[16 + i])
    halo_x(x_low, x_high, wx, stage, fstage, w32)
    start_smoothing(guess, b, inverse, w, wx, x_low, x_high, t_ref, r_ref, i_ref, x_ref, a_ref)
    for copy in copies:
        copy.wait()


def finish_kernel(mask_rows, guess, w, wx, coefficients, y_odd, y_even, columns0, columns1, t_in, r_in, i_in, ghost_in,
                  smoothed, ghost, wy, y_low, y_high, stage, fstage, w32, t_ref, r_ref, i_ref, x_ref, a_ref,
                  rows, side, result, sems):
    halo_y(y_even, y_odd, wy, y_low, y_high, stage, fstage, w32)
    copies = []
    for f, message in enumerate((y_low, y_high)):
        side[...] = jnp.zeros((512, 256), BF16)
        elements = [(8 * ix + 7 * f, ix * 128 + 64 * f) for ix in range(EX)]
        columns = (columns0.at[f], columns1.at[f])
        mask = lambda i: mask_rows[(4 * f + i) * 16 : (4 * f + i) * 16 + 16, :]
        ghost_block(2 + f, message, YT, 2, elements, mask, w, columns, rows, side, result.at[f])
        copies.append(pltpu.make_async_copy(result.at[f], ghost.at[2 + f], sems.at[f]))
        copies[-1].start()
    smooth(guess, w, wx, wy, coefficients, y_low, y_high, t_in, r_in, i_in, smoothed, t_ref, r_ref, i_ref, x_ref, a_ref)
    for copy in copies:
        copy.wait()


def call(kernel, outs, scratch, operands, flops, moved, in_specs=None, out_specs=None, aliases=None, room=48):
    return pl.pallas_call(
        kernel,
        out_shape=outs,
        in_specs=in_specs or [VMEM] * len(operands),
        out_specs=out_specs or [VMEM] * len(outs),
        scratch_shapes=scratch,
        input_output_aliases=aliases or {},
        cost_estimate=pl.CostEstimate(flops=flops, bytes_accessed=moved, transcendentals=0),
        compiler_params=pltpu.CompilerParams(vmem_limit_bytes=room * 1024 * 1024),
    )(*operands)


def exchange(messages, axis, firsts):
    out = []
    for first, message in zip(firsts, messages):
        pairs = []
        for i in range(first, lax.axis_size(axis) - 1, 2):
            pairs += [(i, i + 1), (i + 1, i)]
        out.append(lax.ppermute(message, axis, pairs))
    return out


def shaped(*shape, dtype=BF16):
    return jax.ShapeDtypeStruct(shape, dtype)


STAGES = [pltpu.VMEM((4, 256, 128), F32), pltpu.VMEM((4, 256, 128), F32), pltpu.VMEM((2048, 128), F32)]


GHOST = [
    pltpu.VMEM((128, 128), F32),
    pltpu.VMEM((64, 256), BF16),
    pltpu.VMEM((512, 256), BF16),
    pltpu.VMEM((2, 256, 256), F32),
    pltpu.SemaphoreType.DMA((2,)),
]


def on_device(blocks, faces, tentative, aggregate, ghost_labels, rhs, guess, bounds):
    wide = lambda *shape: shaped(*shape, dtype=F32)
    rhs = jnp.swapaxes(rhs[0, 0], 1, 2)
    guess = jnp.swapaxes(guess[0, 0], 1, 2)
    labels, side_labels = aggregate.reshape(NE), ghost_labels.reshape(24)
    blocks, faces, tentative = [a.reshape(NE, 4096) for a in (blocks, faces, tentative)]
    even, odd, traces_packed, b_packed, b, diagonal = call(
        pack_x_kernel,
        [shaped(16, XLEN)] * 2 + [shaped(NE, 768)] * 2 + [wide(NRHS * NE, 64), shaped(NE, 128)],
        [pltpu.VMEM((NE, 4096), BF16)] * 3 + [pltpu.VMEM((NRHS, NE, 64), F32)] * 2
        + [STAGES[0], STAGES[2], pltpu.VMEM((2048, 128), BF16)] + [pltpu.VMEM((256, 128), F32)] * 2
        + [pltpu.SemaphoreType.DMA((5,))],
        (blocks, faces, tentative, guess, rhs), 10**6, 2**20, [HBM] * 5, room=62,
    )
    even, odd = exchange((even, odd), "bx", (0, 1))
    def part_of(rows):
        outs = [wide(256, 256), shaped(256, 512), shaped(2, 256, 128 * rows)]
        return outs, [pltpu.VMEM((256, 512 * rows), BF16), GHOST[1], pltpu.VMEM((5, 512 * rows, 256), BF16)]

    early, early_scratch = part_of(ROWS_EARLY)
    late, late_scratch = part_of(EX - ROWS_EARLY)
    w, inverse, coefficients, t16, plus_y, minus_y, local, column0, columns0 = call(
        x_wait_kernel,
        [shaped(2048, 128), wide(NE, 64), wide(8, 128), shaped(2048, 128), shaped(512, 128), shaped(512, 128)] + early,
        STAGES + early_scratch,
        (labels, side_labels, blocks, faces, tentative, bounds.reshape(1, 2)), 4 * 10**9, 2**22, [SMEM] * 2 + [VMEM] * 4,
    )
    odd, even, x_low, x_high = call(
        pack_y_kernel, [shaped(16, YLEN)] * 2 + [shaped(16, XLEN)] * 2, [],
        (blocks, faces, tentative, traces_packed, b_packed, diagonal, even, odd, column0), 10**8, 2**20,
        [VMEM] * 8 + [ANY],
    )
    odd, even = exchange((odd, even), "by", (1, 0))
    extended = [wide(SPAN, 128)] * 2 + [wide(EXT, 128)]
    fields = [pltpu.VMEM(a.shape, F32) for a in extended]
    pads = [pltpu.VMEM((8 * EXT, 128), F32)] * 2
    local, columns1, wx, mask_rows, traces, residue, inverses, ghost = call(
        y_wait_kernel, [late[0], late[2], shaped(2048, 128), shaped(128, 256)] + extended + [wide(4, 256, 256)],
        STAGES + pads + GHOST + [pltpu.VMEM((256, 512), BF16), late_scratch[0], late_scratch[2]],
        (labels, side_labels, t16, plus_y, minus_y, w, local, column0, x_low, x_high, guess, b, inverse), 4 * 10**9, 2**22,
        [SMEM] * 2 + [VMEM] * 11, [VMEM] * 7 + [HBM],
    )
    smoothed, ghost = call(
        finish_kernel, [wide(NRHS, NE, 64), wide(4, 256, 256)],
        [pltpu.VMEM((2048, 128), BF16)] + [pltpu.VMEM((16, YLEN), BF16)] * 2 + STAGES + fields + pads + GHOST[:1] + GHOST[2:],
        (mask_rows, guess, w, wx, coefficients, odd, even, columns0, columns1, traces, residue, inverses, ghost),
        10**9, 2**20, [VMEM] * 12 + [HBM], [VMEM, HBM], {12: 1},
    )
    return jnp.swapaxes(smoothed, 1, 2)[None, None], local[None, None], ghost[None, None]


def solution(mesh):
    b = lambda extra: P("bx", "by", *([None] * extra))
    return jax.shard_map(
        on_device,
        mesh=mesh,
        in_specs=(b(2), b(2), b(2), b(1), b(1), b(3), b(3), P()),
        out_specs=(b(3), b(2), b(3)),
        check_vma=False,
    )
```

```python
import jax
import jax.numpy as jnp
from jax import lax
from jax.experimental import pallas as pl
from jax.experimental.pallas import tpu as pltpu
from jax.sharding import PartitionSpec as P

EX, EY, NE, NRHS = 4, 8, 32, 6
F32, BF16 = jnp.float32, jnp.bfloat16
VMEM = pl.BlockSpec(memory_space=pltpu.VMEM)
SMEM = pl.BlockSpec(memory_space=pltpu.SMEM)
HBM = pl.BlockSpec(memory_space=pltpu.HBM)
ANY = pl.BlockSpec(memory_space=pl.ANY)
NT = (((1,), (1,)), ((), ()))
NN = (((1,), (0,)), ((), ()))

XA = 0
XB = 512
XC = 2560
XD = 3072
XH = 3840
XK = 4224
XT = 4480
XE = 4992
XLEN = 5120
YA, YB = 0, 512
YF = 2560
YD = 3584
YG = 4352
YR = 5120
YT = 5504
YE = 6016
YLEN = 6144

EXT, SPAN = 160, 960


def dot(a, b, dims=NN):
    return lax.dot_general(a, b, dims, preferred_element_type=F32)


def iota(shape, dim):
    return lax.broadcasted_iota(jnp.int32, shape, dim)


def onehot(mask):
    return mask.astype(F32).astype(BF16)


def none(count):
    return jnp.zeros((count, 128), BF16)


def split(x):
    hi = x.astype(BF16)
    return hi, (x - hi.astype(F32)).astype(BF16)


def halves(x):
    lanes = x.shape[1] // 2
    return jnp.concatenate([x[:, :lanes], x[:, lanes:]], 0)


def over(a, b):
    return jnp.concatenate([a, b], 0)


def parity(axis):
    return lax.axis_index(axis) % 2


def with_traces(v):
    q, lane = iota((64, 128), 0), iota((64, 128), 1)
    t = lane % 16
    f = lane // 16 - 4
    along_y = 16 * (t // 4) + t % 4
    source = jnp.where(f == 0, 48 + t, jnp.where(f == 1, t, jnp.where(f == 2, along_y + 12, along_y)))
    pick = onehot(q == jnp.where(f < 0, lane, source))
    hi, lo = split(v)
    return dot(hi, pick) + dot(lo, pick)


def by_element(rows):
    return jnp.concatenate([rows[n * NE : (n + 1) * NE] for n in range(NRHS)], 1)


def pack_lanes(v):
    hi, lo = split(v)
    q, lane = iota((64, 128), 0), iota((64, 128), 1)
    return by_element(dot(hi, onehot(q == lane)) + dot(lo, onehot(q == lane - 64)))


def pack_traces(traces):
    hi, lo = split(traces)
    lane = iota(traces.shape, 1)
    return by_element(jnp.where(lane >= 64, hi.astype(F32), pltpu.roll(lo.astype(F32), 64, 1)))


def squeeze(value, offset):
    lane = iota((8, 128), 1) % 64
    keep = (lane >= offset) & (lane < offset + 16)
    tiles = []
    for first in (0, 4):
        total = jnp.zeros((8, 128), F32)
        for j, n in enumerate(range(first, min(first + 4, NRHS))):
            one = jnp.where(keep, value[:, n * 128 : n * 128 + 128], 0.0)
            total = total + pltpu.roll(one, (16 * j - offset) % 128, 1)
        tiles.append(total)
    return jnp.concatenate(tiles, 1)


def unsqueeze(tiles, n, offset):
    lane = iota((8, 128), 1) % 64
    tile = tiles[:, n // 4 * 128 : n // 4 * 128 + 128]
    moved = pltpu.roll(tile, (offset - 16 * (n % 4)) % 128, 1)
    return jnp.where((lane >= offset) & (lane < offset + 16), moved, 0.0)


TRACE_OFFSET, VALUE_OFFSET = (16, 0), (0, 48)


def pack_x_kernel(blocks_in, faces_in, tent_in, guess_in, rhs_in, bounds_in, labels_in, sides_in,
                  even, odd, traces_packed, b_packed, b_out, diagonal, labels_out,
                  blocks, faces, tent, guess, rhs, bounds, labels, sides, stage, w32, w16, x_ref, a_ref, sems):
    copies = [
        pltpu.make_async_copy(source, target, sems.at[i])
        for i, (source, target) in enumerate(
            ((guess_in, guess), (blocks_in, blocks), (rhs_in, rhs), (faces_in, faces), (tent_in, tent),
             (bounds_in, bounds), (labels_in, labels), (sides_in, sides))
        )
    ]
    for copy in copies:
        copy.start()
    copies[0].wait()
    v = guess[...].reshape(NRHS * NE, 64)
    traces = with_traces(v)
    t = pack_traces(traces)
    traces_packed[...] = t.astype(BF16)
    x_ref[0:192, :] = traces
    x_ref[192:256, :] = jnp.zeros((64, 128), F32)
    copies[1].wait()
    chunk = lambda c: blocks[:, c * 128 : (c + 1) * 128].astype(F32)
    stage_blocks(chunk, stage)
    diag = diagonals(chunk)
    diagonal[...] = diag.astype(BF16)
    for k in range(4):
        both = stage[k]
        w32[pl.ds(2 * k, 256, stride=8), :] = both
        w32[pl.ds(2 * k + 1, 256, stride=8), :] = pltpu.roll(both, 64, 1)
    w16[...] = w32[...].astype(BF16)
    lane8 = iota((8, 128), 1)
    for e in range(NE):
        hi, lo = split(jnp.where(lane8 < 64, x_ref[pl.ds(e, 8, stride=NE), :], 0.0))
        out = dot(over(hi, lo), w16[e * 64 : e * 64 + 64, :], NT)
        a_ref[pl.ds(e, 8, stride=NE), 0:64] = out[:8] + out[8:]
    for copy in copies[2:]:
        copy.wait()
    b = rhs[...].reshape(NRHS * NE, 64) - a_ref[0:192, 0:64]
    b_out[0:192, :] = b
    b_out[192:200, :] = jnp.concatenate(
        [jnp.broadcast_to(c, (1, 64)) for c in factors(bounds)] + [jnp.zeros((3, 64), F32)], 0
    )
    labels_out[...] = jnp.zeros((8, 128), jnp.int32)
    labels_out[0:1, 0:NE] = labels[...]
    labels_out[1:2, 0:24] = sides[...]
    r = pack_lanes(b)
    b_packed[...] = r.astype(BF16)
    first = parity("bx") == 0

    def put(start, lanes, make):
        low, high = make(0), make(1)
        even[:, start : start + lanes] = jnp.where(first, high, low).astype(BF16)
        odd[:, start : start + lanes] = jnp.where(first, low, high).astype(BF16)

    def rows(k, side):
        return 8 * k if side == 0 else 24 - 8 * k

    def of(ref, k, side, start, lanes):
        row = rows(k, side)
        base = row // 16 * 16
        return ref[base : base + 16, start : start + lanes].astype(F32)[row - base : row - base + 8]

    def packed(value, k, side):
        return value[rows(k, side) : rows(k, side) + 8]

    def face_traces(side):
        return jnp.concatenate([of(faces, 1, side, f * 1024 + 768 * side, 256) for f in range(4)], 1)

    put(XA, 512, lambda s: halves(of(blocks, 0, s, 3072 * s, 1024)))
    for h in range(2):
        put(XB + h * 1024, 1024, lambda s: over(of(faces, 0, s, h * 1024, 1024), of(faces, 0, s, h * 1024 + 2048, 1024)))
    put(XC, 512, lambda s: halves(face_traces(s)))
    put(XD, 768, lambda s: over(packed(t, 0, s), packed(t, 1, s)))
    put(XH, 384, lambda s: halves(packed(r, 0, s)))
    put(XK, 256, lambda s: over(squeeze(packed(t, 2, s), TRACE_OFFSET[s]), squeeze(packed(r, 1, s), VALUE_OFFSET[s])))
    put(XT, 512, lambda s: halves(of(tent, 0, s, 3072 * s, 1024)))
    put(XE, 128, lambda s: over(packed(diag, 0, s), packed(diag, 1, s)))


def pack_y_kernel(blocks, faces, tent, traces_packed, b_packed, diagonal, x_even, x_odd, _, odd, even, low, high):
    first = parity("bx") == 0
    for start in range(0, XLEN, 128):
        a = x_even[:, start : start + 128].astype(F32)
        b = x_odd[:, start : start + 128].astype(F32)
        low[:, start : start + 128] = jnp.where(first, b, a).astype(BF16)
        high[:, start : start + 128] = jnp.where(first, a, b).astype(BF16)
    py = parity("by")
    is_first = py == 0

    def select(k, near=None, far=None, columns=64):
        r, j = iota((16, columns), 0), iota((16, columns), 1)
        high_side = jnp.where(r < 8, py, 1 - py) == 0
        iy = jnp.where(high_side, 7 - k, k)
        row = r % 8 - 2
        source = jnp.where((row >= 0) & (row < 4), row * 8 + iy, -1)
        if near is not None:
            source = jnp.where(row == -1, 32 + near + iy, jnp.where(row == 4, 48 + near + iy, source))
        if far is not None:
            source = jnp.where(row == -2, 32 + far + iy, jnp.where(row == 5, 48 + far + iy, source))
        return onehot(j == source)

    def put(start, value):
        even[:, start : start + value[0].shape[1]] = value[0].astype(BF16)
        odd[:, start : start + value[1].shape[1]] = value[1].astype(BF16)

    def both(make, picked):
        return make(picked[:8]), make(picked[8:])

    cut = []
    for h in range(2):
        source = [faces[:, h * 2048 : h * 2048 + 2048], low[:, XB : XB + 2048], high[:, XB : XB + 2048]]
        cut.append(dot(select(0, 8 * h), jnp.concatenate(source, 0)))
    put(YB, (over(cut[0][:8], cut[1][:8]), over(cut[0][8:], cut[1][8:])))

    def by_side(minus, plus):
        up = jnp.where(is_first, plus[:8], minus[:8])
        down = jnp.where(is_first, minus[8:], plus[8:])
        return halves(up), halves(down)

    own1, own0 = select(1, columns=32), select(0, columns=32)

    def lanes(ref, pieces, width):
        return jnp.concatenate([ref[:, p : p + width] for p in pieces], 1)

    minus, plus = [i * 1024 for i in range(4)], [i * 1024 + 768 for i in range(4)]
    put(YA, by_side(dot(own0, lanes(blocks, minus, 256)), dot(own0, lanes(blocks, plus, 256))))
    put(YT, by_side(dot(own0, lanes(tent, minus, 256)), dot(own0, lanes(tent, plus, 256))))
    minus = [f * 1024 + i * 256 for f in range(4) for i in range(4)]
    plus = [p + 128 for p in minus]
    put(YF, by_side(dot(own1, lanes(faces, minus, 128)), dot(own1, lanes(faces, plus, 128))))
    own = traces_packed[...]
    rows = jnp.concatenate([own, low[:, XD : XD + 768], high[:, XD : XD + 768]], 0)
    g0, g1, g2 = dot(select(0, 0, 8), rows), dot(select(1, 0), rows), dot(select(2, columns=32), own)
    cut = []
    for h in range(2):
        rows = [b_packed[:, h * 384 : h * 384 + 384], low[:, XH : XH + 384], high[:, XH : XH + 384]]
        cut.append(dot(select(0, 8 * h), jnp.concatenate(rows, 0)))
    r0, r1 = jnp.concatenate(cut, 1), dot(own1, b_packed[...])
    put(YD, (over(g0[:8], g1[:8]), over(g0[8:], g1[8:])))
    put(YG, (over(g2[:8], r0[:8]), over(g2[8:], r0[8:])))
    put(YR, both(halves, r1))
    own = diagonal[...]
    d0 = dot(select(0, 0), jnp.concatenate([own, low[:, XE : XE + 128], high[:, XE : XE + 128]], 0))
    d1 = dot(own1, own)
    put(YE, (over(d0[:8], d1[:8]), over(d0[8:], d1[8:])))


def prolongator(tent, t16, plus_y, minus_y, stage, t32):
    lane = iota((256, 128), 1)
    for k in range(4):
        for ph in range(8):
            chunk = tent[:, (ph * 4 + k) * 128 : (ph * 4 + k + 1) * 128].astype(F32)
            stage[k, pl.ds(ph, NE, stride=8), :] = chunk
    for k in range(4):
        both = stage[k]
        other = pltpu.roll(both, 64, 1)
        t32[pl.ds(2 * k, 256, stride=8), :] = jnp.where(lane < 64, both, other)
        t32[pl.ds(2 * k + 1, 256, stride=8), :] = jnp.where(lane < 64, other, both)
    t16[...] = t32[...].astype(BF16)
    sub = iota((8, 128), 0)
    for e in range(NE):
        plus, minus = [], []
        for h in range(2):
            base = e * 64 + 32 * h
            a, b = t32[base + 8 : base + 16, :], t32[base + 24 : base + 32, :]
            plus.append(jnp.where(sub < 4, pltpu.roll(a, 4, 0), b))
            a, b = t32[base : base + 8, :], t32[base + 16 : base + 24, :]
            minus.append(jnp.where(sub < 4, a, pltpu.roll(b, 4, 0)))
        plus_y[e * 16 : e * 16 + 16, :] = jnp.concatenate(plus, 0).astype(BF16)
        minus_y[e * 16 : e * 16 + 16, :] = jnp.concatenate(minus, 0).astype(BF16)


def stage_blocks(block_chunk, stage):
    for k in range(4):
        for ph in range(8):
            stage[k, pl.ds(ph, NE, stride=8), :] = block_chunk(ph * 4 + k)


def diagonals(block_chunk):
    lane = iota((NE, 128), 1)
    diag = jnp.zeros((NE, 128), F32)
    for c in range(32):
        diag = diag + jnp.where((lane == 2 * c) | (lane == 65 + 2 * c), block_chunk(c), 0.0)
    return diag + pltpu.roll(diag, 64, 1)


def reciprocal(diagonal):
    return 1.0 / jnp.where(diagonal == 0.0, 1.0, diagonal)


def operators(block_chunk, face_chunk, w, stage, fstage, w32):
    lane = iota((256, 128), 1)
    stage_blocks(block_chunk, stage)
    for f in range(4):
        for ph in range(8):
            fstage[f, pl.ds(ph, NE, stride=8), :] = face_chunk(f * 8 + ph)
    folded = jnp.concatenate([fstage[f].astype(BF16) for f in range(4)], 1)
    t, lane16 = iota((16, 128), 0), iota((16, 128), 1)
    moves = [onehot(lane16 == 64 + 16 * f + t) for f in range(4)]
    for k in range(4):
        both = stage[k]
        other = pltpu.roll(both, 64, 1)
        for s, part in enumerate((both, other)):
            p_lo = 2 * k + s
            pick = jnp.concatenate([moves[f] if lo == p_lo else none(16) for f in range(4) for lo in range(8)], 0)
            w32[pl.ds(p_lo, 256, stride=8), :] = jnp.where(lane < 64, part, dot(folded, pick))
    w[...] = w32[...].astype(BF16)


def own_operators(blocks, faces, w, *scratch):
    chunk = lambda ref: lambda c: ref[:, c * 128 : (c + 1) * 128].astype(F32)
    operators(chunk(blocks), chunk(faces), w, *scratch)


NOTHING = (8, 128)


def part(ref, start, c, half):
    row = 8 * (c // half)
    lane = start + (c % half) * 128
    return ref[:, lane : lane + 128].astype(F32)[row : row + 8]


def halo_x(low, high, w, *scratch):
    zero = jnp.zeros(NOTHING, F32)

    def block(c):
        near_low = part(low, XA, c - 24, 4) if c >= 24 else zero
        near_high = part(high, XA, c, 4) if c < 8 else zero
        return jnp.concatenate([near_low, zero, near_high, zero], 0)

    def face(c):
        f, ph = c // 8, c % 8
        far_low = part(low, XC, f * 2 + ph - 6, 4) if ph >= 6 else zero
        far_high = part(high, XC, f * 2 + ph, 4) if ph < 2 else zero
        return jnp.concatenate([part(low, XB, c, 16), far_low, part(high, XB, c, 16), far_high], 0)

    operators(block, face, w, *scratch)


def halo_y(even, odd, w, low, high, *scratch):
    first = parity("by") == 0
    for start in range(0, YLEN, 128):
        a = even[:, start : start + 128].astype(F32)
        b = odd[:, start : start + 128].astype(F32)
        low[:, start : start + 128] = jnp.where(first, b, a).astype(BF16)
        high[:, start : start + 128] = jnp.where(first, a, b).astype(BF16)
    zero = jnp.zeros(NOTHING, F32)

    def block(c):
        i, d = c // 8, c % 8
        near_low = part(low, YA, i * 2 + d - 6, 4) if d >= 6 else zero
        near_high = part(high, YA, i * 2 + d, 4) if d < 2 else zero
        return jnp.concatenate([near_low, zero, near_high, zero], 0)

    def face(c):
        f, ph = c // 8, c % 8
        i = ph // 2
        far_low = part(low, YF, f * 4 + i, 8) if ph % 2 == 1 else zero
        far_high = part(high, YF, f * 4 + i, 8) if ph % 2 == 0 else zero
        return jnp.concatenate([part(low, YB, c, 16), far_low, part(high, YB, c, 16), far_high], 0)

    operators(block, face, w, *scratch)


def factors(bounds):
    low, high = bounds[0:1, 0:1], bounds[0:1, 1:2]
    centre = 0.5 * (high + low)
    half_width = 0.5 * (high - low)
    spread = centre / half_width
    first = 1.0 / spread
    second = 1.0 / (2.0 * spread - first)
    third = 1.0 / (2.0 * spread - second)
    return centre, half_width, first, second, third


def beside_own(columns):
    return [((ix + 3) * 16 + iy, 0, ix * 8 + iy) for ix in range(EX) for iy in columns]


def beside_x(k, columns):
    return [((7 + k if s else 2 - k) * 16 + iy, 1, s * 16 + k * 8 + iy) for s in range(2) for iy in columns]


def beside_y(k, rows):
    return [((r + 1) * 16 + (8 + k if s else 15 - k), 2, s * 16 + k * 8 + r) for s in range(2) for r in rows]


INNER, OUTER = range(1, 7), (0, 7)
EARLY = (1, 9, beside_own(INNER) + beside_x(0, INNER) + beside_x(1, INNER))
LATE = (1, 9, beside_own(OUTER) + beside_x(0, OUTER) + beside_x(1, OUTER) + beside_y(0, range(1, 7)) + beside_y(1, range(2, 6)))
SECOND = (2, 8, beside_own(range(EY)) + beside_x(0, range(EY)) + beside_y(0, range(2, 6)))
THIRD = (3, 7, beside_own(range(EY)))


def joined(value):
    return value + pltpu.roll(value, 64, 1)


def apply(plan, values, tables, t_ref, x_ref, a_ref):
    first, last, elements = plan
    lane = iota((16, 128), 1)
    x_ref[SPAN:, :] = jnp.zeros((8 * EXT - SPAN, 128), F32)
    for n in range(NRHS):
        for ri in range(first, last):
            row = n * EXT + ri * 16
            own = t_ref[row : row + 16, :]
            sides = jnp.where(
                lane < 80,
                t_ref[row - 16 : row, :],
                jnp.where(
                    lane < 96,
                    t_ref[row + 16 : row + 32, :],
                    jnp.where(lane < 112, pltpu.roll(own, 1, 0), pltpu.roll(own, 15, 0)),
                ),
            )
            x_ref[row : row + 16, :] = jnp.where(lane < 64, own if values else 0.0, sides)
    for row, table, e in elements:
        hi, lo = split(x_ref[pl.ds(row, 8, stride=EXT), :])
        out = dot(over(hi, lo), tables[table][e * 64 : e * 64 + 64, :], NT)
        a_ref[pl.ds(row, 8, stride=EXT), 0:64] = out[:8] + out[8:]


def start_smoothing(guess, b, diagonal, w, wx, x_low, x_high, t_ref, r_ref, i_ref, x_ref, a_ref):
    t_ref[...] = jnp.zeros((SPAN, 128), F32)
    r_ref[...] = jnp.zeros((SPAN, 128), F32)
    i_ref[...] = jnp.ones((EXT, 128), F32)
    a_ref[...] = jnp.zeros((8 * EXT, 128), F32)
    traces = with_traces(guess[...].reshape(NRHS * NE, 64))
    inverse = 1.0 / diagonal[...].astype(F32)
    for ix in range(EX):
        row = (ix + 3) * 16
        i_ref[row : row + 8, :] = inverse[ix * 8 : ix * 8 + 8]
        for n in range(NRHS):
            source = n * NE + ix * 8
            t_ref[n * EXT + row : n * EXT + row + 8, :] = traces[source : source + 8]
            r_ref[n * EXT + row : n * EXT + row + 8, 0:64] = b[source : source + 8, :]
    for side, message in enumerate((x_low, x_high)):
        at = [(7 + k if side else 2 - k) * 16 for k in range(3)]
        near = message[:, XD : XD + 768].astype(F32)
        far = message[:, XK : XK + 256].astype(F32)
        diagonal = reciprocal(message[:, XE : XE + 128].astype(F32))
        for k in range(2):
            i_ref[at[k] : at[k] + 8, :] = diagonal[8 * k : 8 * k + 8]
        for n in range(NRHS):
            base = n * EXT
            for k in range(2):
                t_ref[base + at[k] : base + at[k] + 8, :] = joined(near[8 * k : 8 * k + 8, n * 128 : n * 128 + 128])
            t_ref[base + at[2] : base + at[2] + 8, :] = joined(unsqueeze(far[:8], n, TRACE_OFFSET[1 - side]))
            r_ref[base + at[0] : base + at[0] + 8, :] = joined(part(message, XH, n, 3))
            r_ref[base + at[1] : base + at[1] + 8, :] = joined(unsqueeze(far[8:], n, VALUE_OFFSET[1 - side]))
    apply(EARLY, False, (w, wx), t_ref, x_ref, a_ref)
    r_ref[...] = r_ref[...] - a_ref[:SPAN, :]


def smooth(guess, w, wx, wy, coefficients, y_low, y_high, t_in, r_in, i_in, smoothed, t_ref, r_ref, i_ref, x_ref, a_ref):
    t_ref[...] = t_in[...]
    r_ref[...] = r_in[...]
    i_ref[...] = i_in[...]
    a_ref[:SPAN, :] = jnp.zeros((SPAN, 128), F32)
    for side, message in enumerate((y_low, y_high)):
        column = [16 + (8 + k if side else 15 - k) for k in range(3)]
        diagonal = reciprocal(message[:, YE : YE + 128].astype(F32))
        near = message[:, YD : YD + 768].astype(F32)
        far = message[:, YG : YG + 768].astype(F32)
        for k in range(2):
            i_ref[pl.ds(column[k], 8, stride=16), :] = diagonal[8 * k : 8 * k + 8]
        for n in range(NRHS):
            lanes = slice(n * 128, n * 128 + 128)
            for k, value in enumerate((near[:8, lanes], near[8:, lanes], far[:8, lanes])):
                t_ref[pl.ds(n * EXT + column[k], 8, stride=16), :] = joined(value)
            for k, value in enumerate((far[8:, lanes], part(message, YR, n, 3))):
                r_ref[pl.ds(n * EXT + column[k], 8, stride=16), :] = joined(value)
    tables = (w, wx, wy)
    centre, half_width, first, second, third = [coefficients[i : i + 1, 0:64] for i in range(5)]

    def put_traces(parts, start):
        rows = parts[0].shape[0]
        traces = with_traces(jnp.concatenate(parts, 0))
        for n in range(NRHS):
            t_ref[n * EXT + start : n * EXT + start + rows, :] = traces[n * rows : n * rows + rows]

    apply(LATE, False, tables, t_ref, x_ref, a_ref)
    inverse = i_ref[16:144, 0:64]
    residues, updates = [], []
    for n in range(NRHS):
        rows = slice(n * EXT + 16, n * EXT + 144)
        r = r_ref[rows, 0:64] - a_ref[rows, 0:64]
        residues.append(r[16:112])
        updates.append(inverse * r / centre)
    put_traces(updates, 16)
    apply(SECOND, True, tables, t_ref, x_ref, a_ref)
    inverse = i_ref[32:128, 0:64]
    lasts = []
    for n in range(NRHS):
        residues[n] = residues[n] - a_ref[n * EXT + 32 : n * EXT + 128, 0:64]
        updates[n] = updates[n][16:112]
        lasts.append(second * first * updates[n] + (2.0 * second / half_width) * inverse * residues[n])
    put_traces(lasts, 32)
    apply(THIRD, True, tables, t_ref, x_ref, a_ref)
    for n in range(NRHS):
        for ix in range(EX):
            row, place = n * EXT + (ix + 3) * 16, slice(ix * 8, ix * 8 + 8)
            own = slice(ix * 16 + 16, ix * 16 + 24)
            residue = residues[n][own] - a_ref[row : row + 8, 0:64]
            update = third * second * lasts[n][own] + (2.0 * third / half_width) * inverse[own] * residue
            smoothed[n, place, :] = guess[n, place, :] + updates[n][own] + lasts[n][own] + update


def ghost_rows(message, start, out):
    lane = iota((8, 128), 1)
    for j in range(8):
        both = part(message, start, j, 4)
        other = pltpu.roll(both, 64, 1)
        out[pl.ds(2 * j, 8, stride=16), :] = jnp.where(lane < 64, both, other)
        out[pl.ds(2 * j + 1, 8, stride=16), :] = jnp.where(lane < 64, other, both)


def label_masks(masks):
    lane = iota((16, 256), 1)
    for b in range(4):
        masks[b * 16 : b * 16 + 16, :] = onehot(lane // 64 == b)


def mask_of(masks, label):
    return masks[pl.ds(pl.multiple_of(label * 16, 16), 16), :]


def times(piece, mask):
    return jnp.concatenate([piece, piece], 1) * jnp.concatenate([mask] * 4, 0)


def masked(masks, piece, label):
    return times(piece, mask_of(masks, label))


def face_column(f, rows):
    return jnp.concatenate([none(64 + 16 * f), rows] + ([none(48 - 16 * f)] if f < 3 else []), 0)


ROWS_EARLY = 3


def galerkin(late, before_local, labels, t16, plus_y, minus_y, w, local, edge_column, edge_columns, tt, masks, big):
    first_row, last_row = (ROWS_EARLY, EX) if late else (0, ROWS_EARLY)
    rows = last_row - first_row
    label_masks(masks)
    lane128 = iota((64, 128), 1)
    for pair in range(4 * rows):
        e = 8 * first_row + 2 * pair
        turned = t16[e * 64 : e * 64 + 128, :].astype(F32).T[:64]
        first, second = labels[0, e], labels[0, e + 1]
        for a in range(4):
            keep = jnp.where(
                lane128 < 64,
                jnp.where(first == a, 1.0, 0.0),
                jnp.where(second == a, 1.0, 0.0),
            )
            tt[a * 64 : a * 64 + 64, pair * 128 : pair * 128 + 128] = (turned * keep).astype(BF16)
    edge_column[...] = tt[:, 512 * rows - 512 :] if late else tt[:, :512]
    for f in range(2):
        for i in range(rows):
            start = (4 * i + 3 * f) * 128
            edge_columns[f, :, i * 128 : i * 128 + 128] = tt[:, start : start + 128]

    def row_of_elements(ix, carry):
        for iy in range(EY):
            e = ix * EY + iy
            own = pl.ds(pl.multiple_of(e * 64, 64), 64)
            here = pl.ds(pl.multiple_of((e - 8 * first_row) * 64, 64), 64)
            before = pl.multiple_of(jnp.maximum(e - 8, 0) * 64, 64)
            after = pl.multiple_of(jnp.minimum(e + 8, 31) * 64, 64)
            rows = [
                t16[pl.ds(before + 48, 16), :],
                t16[pl.ds(after, 16), :],
            ]
            if iy > 0:
                rows.append(plus_y[pl.ds(pl.multiple_of((e - 1) * 16, 16), 16), :])
            else:
                rows.append(none(16))
            if iy < 7:
                rows.append(minus_y[pl.ds(pl.multiple_of((e + 1) * 16, 16), 16), :])
            columns = [jnp.concatenate([t16[own, :], none(64)], 0)]
            columns += [face_column(f, value) for f, value in enumerate(rows)]
            pieces = dot(w[own, :], jnp.concatenate(columns, 1)).astype(BF16)
            piece = lambda s: pieces[:, s * 128 : s * 128 + 128]
            big[0, here, :] = masked(masks, piece(0), labels[0, e])
            big[1, here, :] = masked(masks, piece(1), labels[0, jnp.maximum(e - 8, 0)])
            big[2, here, :] = masked(masks, piece(2), labels[0, jnp.minimum(e + 8, 31)])
            nothing = jnp.zeros((64, 256), BF16)
            big[3, here, :] = masked(masks, piece(3), labels[0, e - 1]) if iy > 0 else nothing
            big[4, here, :] = masked(masks, piece(4), labels[0, e + 1]) if iy < 7 else nothing
        return carry

    lax.fori_loop(first_row, last_row, row_of_elements, 0)
    total = dot(tt[...], big[0]) + dot(tt[...], big[3]) + dot(tt[...], big[4])
    if late:
        total = before_local[...] + total + dot(tt[...], big[1])
        if rows > 1:
            total = total + dot(tt[:, : 512 * rows - 512], big[2, : 512 * rows - 512, :])
    else:
        total = total + dot(tt[...], big[2])
        if rows > 1:
            total = total + dot(tt[:, 512:], big[1, 512:, :])
    local[...] = total


def ghost_block(face, message, start, first_row, elements, mask, w, columns, rows, side, result):
    ghost_rows(message, start, rows)
    for i, (e, place) in enumerate(elements):
        near = rows[(i + first_row) * 16 : (i + first_row) * 16 + 16, :].astype(BF16)
        piece = dot(w[e * 64 : e * 64 + 64, :], face_column(face, near)).astype(BF16)
        side[place : place + 64, :] = times(piece, mask(i))
    total, start = 0.0, 0
    for c in columns:
        width = c.shape[-1]
        total = total + dot(c[...], side[start : start + width, :])
        start += width
    result[...] = total


def x_wait_kernel(labels_in, blocks, faces, tent, w, t16, plus_y, minus_y, local, column, columns, _,
                  stage, fstage, w32, tt, masks, big, labels, label_sem):
    fetch = pltpu.make_async_copy(labels_in, labels, label_sem.at[0])
    fetch.start()
    own_operators(blocks, faces, w, stage, fstage, w32)
    prolongator(tent, t16, plus_y, minus_y, fstage, w32)
    fetch.wait()
    galerkin(0, None, labels, t16, plus_y, minus_y, w, local, column, columns, tt, masks, big)


def y_wait_kernel(labels_in, t16, plus_y, minus_y, w, before_local, column0, x_low, x_high, guess, b, diagonal,
                  local, columns, wx, mask_rows, t_ref, r_ref, i_ref, coefficients, ghost, _,
                  stage, fstage, w32, x_ref, a_ref, rows, masks, side, result, sems, column1, tt, big, labels, label_sem):
    fetch = pltpu.make_async_copy(labels_in, labels, label_sem.at[0])
    fetch.start()
    coefficients[...] = b[192:200, :]
    halo_x(x_low, x_high, wx, stage, fstage, w32)
    start_smoothing(guess, b, diagonal, w, wx, x_low, x_high, t_ref, r_ref, i_ref, x_ref, a_ref)
    fetch.wait()
    galerkin(1, before_local, labels, t16, plus_y, minus_y, w, local, column1, columns, tt, masks, big)
    copies = []
    for f, (message, column) in enumerate(((x_low, column0), (x_high, column1))):
        elements = [(24 * f + iy, iy * 64) for iy in range(EY)]
        mask = lambda i: mask_of(masks, labels[1, 8 * f + i])
        ghost_block(f, message, XT, 0, elements, mask, w, (column,), rows, side, result.at[f])
        copies.append(pltpu.make_async_copy(result.at[f], ghost.at[f], sems.at[f]))
        copies[-1].start()
    for i in range(8):
        mask_rows[i * 16 : i * 16 + 16, :] = mask_of(masks, labels[1, 16 + i])
    for copy in copies:
        copy.wait()


def finish_kernel(mask_rows, guess, w, wx, coefficients, y_odd, y_even, columns0, columns1, t_in, r_in, i_in, ghost_in,
                  smoothed, ghost, wy, y_low, y_high, stage, fstage, w32, t_ref, r_ref, i_ref, x_ref, a_ref,
                  rows, side, result, sems):
    halo_y(y_even, y_odd, wy, y_low, y_high, stage, fstage, w32)
    copies = []
    for f, message in enumerate((y_low, y_high)):
        side[...] = jnp.zeros((512, 256), BF16)
        elements = [(8 * ix + 7 * f, ix * 128 + 64 * f) for ix in range(EX)]
        columns = (columns0.at[f], columns1.at[f])
        mask = lambda i: mask_rows[(4 * f + i) * 16 : (4 * f + i) * 16 + 16, :]
        ghost_block(2 + f, message, YT, 2, elements, mask, w, columns, rows, side, result.at[f])
        copies.append(pltpu.make_async_copy(result.at[f], ghost.at[2 + f], sems.at[f]))
        copies[-1].start()
    smooth(guess, w, wx, wy, coefficients, y_low, y_high, t_in, r_in, i_in, smoothed, t_ref, r_ref, i_ref, x_ref, a_ref)
    for copy in copies:
        copy.wait()


def call(kernel, outs, scratch, operands, flops, moved, in_specs=None, out_specs=None, aliases=None, room=48):
    return pl.pallas_call(
        kernel,
        out_shape=outs,
        in_specs=in_specs or [VMEM] * len(operands),
        out_specs=out_specs or [VMEM] * len(outs),
        scratch_shapes=scratch,
        input_output_aliases=aliases or {},
        cost_estimate=pl.CostEstimate(flops=flops, bytes_accessed=moved, transcendentals=0),
        compiler_params=pltpu.CompilerParams(vmem_limit_bytes=room * 1024 * 1024),
    )(*operands)


def exchange(messages, axis, firsts):
    out = []
    for first, message in zip(firsts, messages):
        pairs = []
        for i in range(first, lax.axis_size(axis) - 1, 2):
            pairs += [(i, i + 1), (i + 1, i)]
        out.append(lax.ppermute(message, axis, pairs))
    return out


def shaped(*shape, dtype=BF16):
    return jax.ShapeDtypeStruct(shape, dtype)


STAGES = [pltpu.VMEM((4, 256, 128), F32), pltpu.VMEM((4, 256, 128), F32), pltpu.VMEM((2048, 128), F32)]


GHOST = [
    pltpu.VMEM((128, 128), F32),
    pltpu.VMEM((64, 256), BF16),
    pltpu.VMEM((512, 256), BF16),
    pltpu.VMEM((2, 256, 256), F32),
    pltpu.SemaphoreType.DMA((2,)),
]


def on_device(blocks, faces, tentative, aggregate, ghost_labels, rhs, guess, bounds):
    wide = lambda *shape: shaped(*shape, dtype=F32)
    rhs = jnp.swapaxes(rhs[0, 0], 1, 2)
    guess = jnp.swapaxes(guess[0, 0], 1, 2)
    blocks, faces, tentative = [a.reshape(NE, 4096) for a in (blocks, faces, tentative)]
    even, odd, traces_packed, b_packed, b, diagonal, labels = call(
        pack_x_kernel,
        [shaped(16, XLEN)] * 2 + [shaped(NE, 768)] * 2 + [wide(NRHS * NE + 8, 64), shaped(NE, 128), shaped(8, 128, dtype=jnp.int32)],
        [pltpu.VMEM((NE, 4096), BF16)] * 3 + [pltpu.VMEM((NRHS, NE, 64), F32)] * 2
        + [pltpu.VMEM((1, 2), F32), pltpu.VMEM((1, NE), jnp.int32), pltpu.VMEM((1, 24), jnp.int32)]
        + [STAGES[0], STAGES[2], pltpu.VMEM((2048, 128), BF16)] + [pltpu.VMEM((256, 128), F32)] * 2
        + [pltpu.SemaphoreType.DMA((8,))],
        (blocks, faces, tentative, guess, rhs, bounds.reshape(1, 2), aggregate.reshape(1, NE), ghost_labels.reshape(1, 24)),
        10**6, 2**20, [HBM] * 8, room=62,
    )
    even, odd = exchange((even, odd), "bx", (0, 1))
    def part_of(rows):
        outs = [wide(256, 256), shaped(256, 512), shaped(2, 256, 128 * rows)]
        return outs, [pltpu.VMEM((256, 512 * rows), BF16), GHOST[1], pltpu.VMEM((5, 512 * rows, 256), BF16)]

    early, early_scratch = part_of(ROWS_EARLY)
    late, late_scratch = part_of(EX - ROWS_EARLY)
    scalars = [pltpu.SMEM((8, 128), jnp.int32), pltpu.SemaphoreType.DMA((1,))]
    passed = shaped(8, 128, dtype=jnp.int32)
    w, t16, plus_y, minus_y, local, column0, columns0, labels = call(
        x_wait_kernel,
        [shaped(2048, 128), shaped(2048, 128), shaped(512, 128), shaped(512, 128)] + early + [passed],
        STAGES + early_scratch + scalars,
        (labels, blocks, faces, tentative), 4 * 10**9, 2**22, [HBM] + [VMEM] * 3, [VMEM] * 7 + [HBM], {0: 7},
    )
    odd, even, x_low, x_high = call(
        pack_y_kernel, [shaped(16, YLEN)] * 2 + [shaped(16, XLEN)] * 2, [],
        (blocks, faces, tentative, traces_packed, b_packed, diagonal, even, odd, column0), 10**8, 2**20,
        [VMEM] * 8 + [ANY],
    )
    odd, even = exchange((odd, even), "by", (1, 0))
    extended = [wide(SPAN, 128)] * 2 + [wide(EXT, 128)]
    fields = [pltpu.VMEM(a.shape, F32) for a in extended]
    pads = [pltpu.VMEM((8 * EXT, 128), F32)] * 2
    local, columns1, wx, mask_rows, traces, residue, inverses, coefficients, ghost, _ = call(
        y_wait_kernel,
        [late[0], late[2], shaped(2048, 128), shaped(128, 256)] + extended + [wide(8, 64), wide(4, 256, 256), passed],
        STAGES + pads + GHOST + [pltpu.VMEM((256, 512), BF16), late_scratch[0], late_scratch[2]] + scalars,
        (labels, t16, plus_y, minus_y, w, local, column0, x_low, x_high, guess, b, diagonal), 4 * 10**9, 2**22,
        [HBM] + [VMEM] * 11, [VMEM] * 8 + [HBM] * 2, {0: 9},
    )
    smoothed, ghost = call(
        finish_kernel, [wide(NRHS, NE, 64), wide(4, 256, 256)],
        [pltpu.VMEM((2048, 128), BF16)] + [pltpu.VMEM((16, YLEN), BF16)] * 2 + STAGES + fields + pads + GHOST[:1] + GHOST[2:],
        (mask_rows, guess, w, wx, coefficients, odd, even, columns0, columns1, traces, residue, inverses, ghost),
        10**9, 2**20, [VMEM] * 12 + [HBM], [VMEM, HBM], {12: 1},
    )
    return jnp.swapaxes(smoothed, 1, 2)[None, None], local[None, None], ghost[None, None]


def solution(mesh):
    b = lambda extra: P("bx", "by", *([None] * extra))
    return jax.shard_map(
        on_device,
        mesh=mesh,
        in_specs=(b(2), b(2), b(2), b(1), b(1), b(3), b(3), P()),
        out_specs=(b(3), b(2), b(3)),
        check_vma=False,
    )
```

```python
import jax
import jax.numpy as jnp
from jax import lax
from jax.experimental import pallas as pl
from jax.experimental.pallas import tpu as pltpu
from jax.sharding import PartitionSpec as P

EX, EY, NE, NRHS = 4, 8, 32, 6
F32, BF16 = jnp.float32, jnp.bfloat16
VMEM = pl.BlockSpec(memory_space=pltpu.VMEM)
SMEM = pl.BlockSpec(memory_space=pltpu.SMEM)
HBM = pl.BlockSpec(memory_space=pltpu.HBM)
ANY = pl.BlockSpec(memory_space=pl.ANY)
NT = (((1,), (1,)), ((), ()))
NN = (((1,), (0,)), ((), ()))

XA = 0
XB = 512
XC = 2560
XD = 3072
XH = 3840
XK = 4224
XT = 4480
XE = 4992
XLEN = 5120
YA, YB = 0, 512
YF = 2560
YD = 3584
YG = 4352
YR = 5120
YT = 5504
YE = 6016
YLEN = 6144

EXT, SPAN = 160, 960


def dot(a, b, dims=NN):
    return lax.dot_general(a, b, dims, preferred_element_type=F32)


def iota(shape, dim):
    return lax.broadcasted_iota(jnp.int32, shape, dim)


def onehot(mask):
    return mask.astype(F32).astype(BF16)


def none(count):
    return jnp.zeros((count, 128), BF16)


def split(x):
    hi = x.astype(BF16)
    return hi, (x - hi.astype(F32)).astype(BF16)


def halves(x):
    lanes = x.shape[1] // 2
    return jnp.concatenate([x[:, :lanes], x[:, lanes:]], 0)


def over(a, b):
    return jnp.concatenate([a, b], 0)


def parity(axis):
    return lax.axis_index(axis) % 2


def with_traces(v):
    q, lane = iota((64, 128), 0), iota((64, 128), 1)
    t = lane % 16
    f = lane // 16 - 4
    along_y = 16 * (t // 4) + t % 4
    source = jnp.where(f == 0, 48 + t, jnp.where(f == 1, t, jnp.where(f == 2, along_y + 12, along_y)))
    pick = onehot(q == jnp.where(f < 0, lane, source))
    hi, lo = split(v)
    return dot(hi, pick) + dot(lo, pick)


def by_element(rows):
    return jnp.concatenate([rows[n * NE : (n + 1) * NE] for n in range(NRHS)], 1)


def pack_lanes(v):
    hi, lo = split(v)
    q, lane = iota((64, 128), 0), iota((64, 128), 1)
    return by_element(dot(hi, onehot(q == lane)) + dot(lo, onehot(q == lane - 64)))


def pack_traces(traces):
    hi, lo = split(traces)
    lane = iota(traces.shape, 1)
    return by_element(jnp.where(lane >= 64, hi.astype(F32), pltpu.roll(lo.astype(F32), 64, 1)))


def squeeze(value, offset):
    lane = iota((8, 128), 1) % 64
    keep = (lane >= offset) & (lane < offset + 16)
    tiles = []
    for first in (0, 4):
        total = jnp.zeros((8, 128), F32)
        for j, n in enumerate(range(first, min(first + 4, NRHS))):
            one = jnp.where(keep, value[:, n * 128 : n * 128 + 128], 0.0)
            total = total + pltpu.roll(one, (16 * j - offset) % 128, 1)
        tiles.append(total)
    return jnp.concatenate(tiles, 1)


def unsqueeze(tiles, n, offset):
    lane = iota((8, 128), 1) % 64
    tile = tiles[:, n // 4 * 128 : n // 4 * 128 + 128]
    moved = pltpu.roll(tile, (offset - 16 * (n % 4)) % 128, 1)
    return jnp.where((lane >= offset) & (lane < offset + 16), moved, 0.0)


TRACE_OFFSET, VALUE_OFFSET = (16, 0), (0, 48)


def pack_x_kernel(blocks_in, faces_in, tent_in, guess_in, rhs_in, bounds_in, labels_in, sides_in,
                  even, odd, traces_packed, b_packed, b_out, diagonal, labels_out,
                  blocks, faces, tent, guess, rhs, bounds, labels, sides, stage, w32, w16, x_ref, a_ref, sems):
    copies = [
        pltpu.make_async_copy(source, target, sems.at[i])
        for i, (source, target) in enumerate(
            ((guess_in, guess), (blocks_in, blocks), (rhs_in, rhs), (faces_in, faces), (tent_in, tent),
             (bounds_in, bounds), (labels_in, labels), (sides_in, sides))
        )
    ]
    for copy in copies:
        copy.start()
    copies[0].wait()
    v = guess[...].reshape(NRHS * NE, 64)
    traces = with_traces(v)
    t = pack_traces(traces)
    traces_packed[...] = t.astype(BF16)
    x_ref[0:192, :] = traces
    x_ref[192:256, :] = jnp.zeros((64, 128), F32)
    copies[1].wait()
    chunk = lambda c: blocks[:, c * 128 : (c + 1) * 128].astype(F32)
    stage_blocks(chunk, stage)
    diag = diagonals(chunk)
    diagonal[...] = diag.astype(BF16)
    for k in range(4):
        both = stage[k]
        w32[pl.ds(2 * k, 256, stride=8), :] = both
        w32[pl.ds(2 * k + 1, 256, stride=8), :] = pltpu.roll(both, 64, 1)
    w16[...] = w32[...].astype(BF16)
    lane8 = iota((8, 128), 1)
    for e in range(NE):
        hi, lo = split(jnp.where(lane8 < 64, x_ref[pl.ds(e, 8, stride=NE), :], 0.0))
        out = dot(over(hi, lo), w16[e * 64 : e * 64 + 64, :], NT)
        a_ref[pl.ds(e, 8, stride=NE), 0:64] = out[:8] + out[8:]
    for copy in copies[2:]:
        copy.wait()
    b = rhs[...].reshape(NRHS * NE, 64) - a_ref[0:192, 0:64]
    b_out[0:192, :] = b
    b_out[192:200, :] = jnp.concatenate(
        [jnp.broadcast_to(c, (1, 64)) for c in factors(bounds)] + [jnp.zeros((3, 64), F32)], 0
    )
    labels_out[...] = jnp.zeros((8, 128), jnp.int32)
    labels_out[0:1, 0:NE] = labels[...]
    labels_out[1:2, 0:24] = sides[...]
    r = pack_lanes(b)
    b_packed[...] = r.astype(BF16)
    first = parity("bx") == 0

    def put(start, lanes, make):
        low, high = make(0), make(1)
        even[:, start : start + lanes] = jnp.where(first, high, low).astype(BF16)
        odd[:, start : start + lanes] = jnp.where(first, low, high).astype(BF16)

    def rows(k, side):
        return 8 * k if side == 0 else 24 - 8 * k

    def of(ref, k, side, start, lanes):
        row = rows(k, side)
        base = row // 16 * 16
        return ref[base : base + 16, start : start + lanes].astype(F32)[row - base : row - base + 8]

    def packed(value, k, side):
        return value[rows(k, side) : rows(k, side) + 8]

    def face_traces(side):
        return jnp.concatenate([of(faces, 1, side, f * 1024 + 768 * side, 256) for f in range(4)], 1)

    put(XA, 512, lambda s: halves(of(blocks, 0, s, 3072 * s, 1024)))
    for h in range(2):
        put(XB + h * 1024, 1024, lambda s: over(of(faces, 0, s, h * 1024, 1024), of(faces, 0, s, h * 1024 + 2048, 1024)))
    put(XC, 512, lambda s: halves(face_traces(s)))
    put(XD, 768, lambda s: over(packed(t, 0, s), packed(t, 1, s)))
    put(XH, 384, lambda s: halves(packed(r, 0, s)))
    put(XK, 256, lambda s: over(squeeze(packed(t, 2, s), TRACE_OFFSET[s]), squeeze(packed(r, 1, s), VALUE_OFFSET[s])))
    put(XT, 512, lambda s: halves(of(tent, 0, s, 3072 * s, 1024)))
    put(XE, 128, lambda s: over(packed(diag, 0, s), packed(diag, 1, s)))


def pack_y_kernel(blocks, faces, tent, traces_packed, b_packed, diagonal, x_even, x_odd, _, odd, even, low, high):
    first = parity("bx") == 0
    for start in range(0, XLEN, 128):
        a = x_even[:, start : start + 128].astype(F32)
        b = x_odd[:, start : start + 128].astype(F32)
        low[:, start : start + 128] = jnp.where(first, b, a).astype(BF16)
        high[:, start : start + 128] = jnp.where(first, a, b).astype(BF16)
    py = parity("by")
    is_first = py == 0

    def select(k, near=None, far=None, columns=64):
        r, j = iota((16, columns), 0), iota((16, columns), 1)
        high_side = jnp.where(r < 8, py, 1 - py) == 0
        iy = jnp.where(high_side, 7 - k, k)
        row = r % 8 - 2
        source = jnp.where((row >= 0) & (row < 4), row * 8 + iy, -1)
        if near is not None:
            source = jnp.where(row == -1, 32 + near + iy, jnp.where(row == 4, 48 + near + iy, source))
        if far is not None:
            source = jnp.where(row == -2, 32 + far + iy, jnp.where(row == 5, 48 + far + iy, source))
        return onehot(j == source)

    def put(start, value):
        even[:, start : start + value[0].shape[1]] = value[0].astype(BF16)
        odd[:, start : start + value[1].shape[1]] = value[1].astype(BF16)

    def both(make, picked):
        return make(picked[:8]), make(picked[8:])

    cut = []
    for h in range(2):
        source = [faces[:, h * 2048 : h * 2048 + 2048], low[:, XB : XB + 2048], high[:, XB : XB + 2048]]
        cut.append(dot(select(0, 8 * h), jnp.concatenate(source, 0)))
    put(YB, (over(cut[0][:8], cut[1][:8]), over(cut[0][8:], cut[1][8:])))

    def by_side(minus, plus):
        up = jnp.where(is_first, plus[:8], minus[:8])
        down = jnp.where(is_first, minus[8:], plus[8:])
        return halves(up), halves(down)

    own1, own0 = select(1, columns=32), select(0, columns=32)

    def lanes(ref, pieces, width):
        return jnp.concatenate([ref[:, p : p + width] for p in pieces], 1)

    minus, plus = [i * 1024 for i in range(4)], [i * 1024 + 768 for i in range(4)]
    put(YA, by_side(dot(own0, lanes(blocks, minus, 256)), dot(own0, lanes(blocks, plus, 256))))
    put(YT, by_side(dot(own0, lanes(tent, minus, 256)), dot(own0, lanes(tent, plus, 256))))
    minus = [f * 1024 + i * 256 for f in range(4) for i in range(4)]
    plus = [p + 128 for p in minus]
    put(YF, by_side(dot(own1, lanes(faces, minus, 128)), dot(own1, lanes(faces, plus, 128))))
    own = traces_packed[...]
    rows = jnp.concatenate([own, low[:, XD : XD + 768], high[:, XD : XD + 768]], 0)
    g0, g1, g2 = dot(select(0, 0, 8), rows), dot(select(1, 0), rows), dot(select(2, columns=32), own)
    cut = []
    for h in range(2):
        rows = [b_packed[:, h * 384 : h * 384 + 384], low[:, XH : XH + 384], high[:, XH : XH + 384]]
        cut.append(dot(select(0, 8 * h), jnp.concatenate(rows, 0)))
    r0, r1 = jnp.concatenate(cut, 1), dot(own1, b_packed[...])
    put(YD, (over(g0[:8], g1[:8]), over(g0[8:], g1[8:])))
    put(YG, (over(g2[:8], r0[:8]), over(g2[8:], r0[8:])))
    put(YR, both(halves, r1))
    own = diagonal[...]
    d0 = dot(select(0, 0), jnp.concatenate([own, low[:, XE : XE + 128], high[:, XE : XE + 128]], 0))
    d1 = dot(own1, own)
    put(YE, (over(d0[:8], d1[:8]), over(d0[8:], d1[8:])))


def prolongator(tent, t16, plus_y, minus_y, stage, t32):
    lane = iota((256, 128), 1)
    for k in range(4):
        for ph in range(8):
            chunk = tent[:, (ph * 4 + k) * 128 : (ph * 4 + k + 1) * 128].astype(F32)
            stage[k, pl.ds(ph, NE, stride=8), :] = chunk
    for k in range(4):
        both = stage[k]
        other = pltpu.roll(both, 64, 1)
        t32[pl.ds(2 * k, 256, stride=8), :] = jnp.where(lane < 64, both, other)
        t32[pl.ds(2 * k + 1, 256, stride=8), :] = jnp.where(lane < 64, other, both)
    t16[...] = t32[...].astype(BF16)
    sub = iota((8, 128), 0)
    for e in range(NE):
        plus, minus = [], []
        for h in range(2):
            base = e * 64 + 32 * h
            a, b = t32[base + 8 : base + 16, :], t32[base + 24 : base + 32, :]
            plus.append(jnp.where(sub < 4, pltpu.roll(a, 4, 0), b))
            a, b = t32[base : base + 8, :], t32[base + 16 : base + 24, :]
            minus.append(jnp.where(sub < 4, a, pltpu.roll(b, 4, 0)))
        plus_y[e * 16 : e * 16 + 16, :] = jnp.concatenate(plus, 0).astype(BF16)
        minus_y[e * 16 : e * 16 + 16, :] = jnp.concatenate(minus, 0).astype(BF16)


def stage_blocks(block_chunk, stage):
    for k in range(4):
        for ph in range(8):
            stage[k, pl.ds(ph, NE, stride=8), :] = block_chunk(ph * 4 + k)


def diagonals(block_chunk):
    lane = iota((NE, 128), 1)
    diag = jnp.zeros((NE, 128), F32)
    for c in range(32):
        diag = diag + jnp.where((lane == 2 * c) | (lane == 65 + 2 * c), block_chunk(c), 0.0)
    return diag + pltpu.roll(diag, 64, 1)


def reciprocal(diagonal):
    return 1.0 / jnp.where(diagonal == 0.0, 1.0, diagonal)


def operators(block_chunk, face_chunk, w, stage, fstage, w32):
    lane = iota((256, 128), 1)
    stage_blocks(block_chunk, stage)
    for f in range(4):
        for ph in range(8):
            fstage[f, pl.ds(ph, NE, stride=8), :] = face_chunk(f * 8 + ph)
    folded = jnp.concatenate([fstage[f].astype(BF16) for f in range(4)], 1)
    t, lane16 = iota((16, 128), 0), iota((16, 128), 1)
    moves = [onehot(lane16 == 64 + 16 * f + t) for f in range(4)]
    for k in range(4):
        both = stage[k]
        other = pltpu.roll(both, 64, 1)
        for s, part in enumerate((both, other)):
            p_lo = 2 * k + s
            pick = jnp.concatenate([moves[f] if lo == p_lo else none(16) for f in range(4) for lo in range(8)], 0)
            w32[pl.ds(p_lo, 256, stride=8), :] = jnp.where(lane < 64, part, dot(folded, pick))
    w[...] = w32[...].astype(BF16)


def own_operators(blocks, faces, w, *scratch):
    chunk = lambda ref: lambda c: ref[:, c * 128 : (c + 1) * 128].astype(F32)
    operators(chunk(blocks), chunk(faces), w, *scratch)


NOTHING = (8, 128)


def part(ref, start, c, half):
    row = 8 * (c // half)
    lane = start + (c % half) * 128
    return ref[:, lane : lane + 128].astype(F32)[row : row + 8]


def halo_x(low, high, w, *scratch):
    zero = jnp.zeros(NOTHING, F32)

    def block(c):
        near_low = part(low, XA, c - 24, 4) if c >= 24 else zero
        near_high = part(high, XA, c, 4) if c < 8 else zero
        return jnp.concatenate([near_low, zero, near_high, zero], 0)

    def face(c):
        f, ph = c // 8, c % 8
        far_low = part(low, XC, f * 2 + ph - 6, 4) if ph >= 6 else zero
        far_high = part(high, XC, f * 2 + ph, 4) if ph < 2 else zero
        return jnp.concatenate([part(low, XB, c, 16), far_low, part(high, XB, c, 16), far_high], 0)

    operators(block, face, w, *scratch)


def halo_y(even, odd, w, low, high, *scratch):
    first = parity("by") == 0
    for start in range(0, YLEN, 128):
        a = even[:, start : start + 128].astype(F32)
        b = odd[:, start : start + 128].astype(F32)
        low[:, start : start + 128] = jnp.where(first, b, a).astype(BF16)
        high[:, start : start + 128] = jnp.where(first, a, b).astype(BF16)
    zero = jnp.zeros(NOTHING, F32)

    def block(c):
        i, d = c // 8, c % 8
        near_low = part(low, YA, i * 2 + d - 6, 4) if d >= 6 else zero
        near_high = part(high, YA, i * 2 + d, 4) if d < 2 else zero
        return jnp.concatenate([near_low, zero, near_high, zero], 0)

    def face(c):
        f, ph = c // 8, c % 8
        i = ph // 2
        far_low = part(low, YF, f * 4 + i, 8) if ph % 2 == 1 else zero
        far_high = part(high, YF, f * 4 + i, 8) if ph % 2 == 0 else zero
        return jnp.concatenate([part(low, YB, c, 16), far_low, part(high, YB, c, 16), far_high], 0)

    operators(block, face, w, *scratch)


def factors(bounds):
    low, high = bounds[0:1, 0:1], bounds[0:1, 1:2]
    centre = 0.5 * (high + low)
    half_width = 0.5 * (high - low)
    spread = centre / half_width
    first = 1.0 / spread
    second = 1.0 / (2.0 * spread - first)
    third = 1.0 / (2.0 * spread - second)
    return centre, half_width, first, second, third


def beside_own(columns):
    return [((ix + 3) * 16 + iy, 0, ix * 8 + iy) for ix in range(EX) for iy in columns]


def beside_x(k, columns):
    return [((7 + k if s else 2 - k) * 16 + iy, 1, s * 16 + k * 8 + iy) for s in range(2) for iy in columns]


def beside_y(k, rows):
    return [((r + 1) * 16 + (8 + k if s else 15 - k), 2, s * 16 + k * 8 + r) for s in range(2) for r in rows]


INNER, OUTER = range(1, 7), (0, 7)
EARLY = (1, 9, beside_own(INNER) + beside_x(0, INNER) + beside_x(1, INNER))
LATE = (1, 9, beside_own(OUTER) + beside_x(0, OUTER) + beside_x(1, OUTER) + beside_y(0, range(1, 7)) + beside_y(1, range(2, 6)))
SECOND = (2, 8, beside_own(range(EY)) + beside_x(0, range(EY)) + beside_y(0, range(2, 6)))
THIRD = (3, 7, beside_own(range(EY)))


def joined(value):
    return value + pltpu.roll(value, 64, 1)


def apply(plan, values, tables, t_ref, x_ref, a_ref):
    first, last, elements = plan
    lane = iota((16, 128), 1)
    x_ref[SPAN:, :] = jnp.zeros((8 * EXT - SPAN, 128), F32)
    for n in range(NRHS):
        for ri in range(first, last):
            row = n * EXT + ri * 16
            own = t_ref[row : row + 16, :]
            sides = jnp.where(
                lane < 80,
                t_ref[row - 16 : row, :],
                jnp.where(
                    lane < 96,
                    t_ref[row + 16 : row + 32, :],
                    jnp.where(lane < 112, pltpu.roll(own, 1, 0), pltpu.roll(own, 15, 0)),
                ),
            )
            x_ref[row : row + 16, :] = jnp.where(lane < 64, own if values else 0.0, sides)
    for row, table, e in elements:
        hi, lo = split(x_ref[pl.ds(row, 8, stride=EXT), :])
        out = dot(over(hi, lo), tables[table][e * 64 : e * 64 + 64, :], NT)
        a_ref[pl.ds(row, 8, stride=EXT), 0:64] = out[:8] + out[8:]


def start_smoothing(guess, b, diagonal, w, wx, x_low, x_high, t_ref, r_ref, i_ref, x_ref, a_ref):
    t_ref[...] = jnp.zeros((SPAN, 128), F32)
    r_ref[...] = jnp.zeros((SPAN, 128), F32)
    i_ref[...] = jnp.ones((EXT, 128), F32)
    a_ref[...] = jnp.zeros((8 * EXT, 128), F32)
    traces = with_traces(guess[...].reshape(NRHS * NE, 64))
    inverse = 1.0 / diagonal[...].astype(F32)
    for ix in range(EX):
        row = (ix + 3) * 16
        i_ref[row : row + 8, :] = inverse[ix * 8 : ix * 8 + 8]
        for n in range(NRHS):
            source = n * NE + ix * 8
            t_ref[n * EXT + row : n * EXT + row + 8, :] = traces[source : source + 8]
            r_ref[n * EXT + row : n * EXT + row + 8, 0:64] = b[source : source + 8, :]
    for side, message in enumerate((x_low, x_high)):
        at = [(7 + k if side else 2 - k) * 16 for k in range(3)]
        near = message[:, XD : XD + 768].astype(F32)
        far = message[:, XK : XK + 256].astype(F32)
        diagonal = reciprocal(message[:, XE : XE + 128].astype(F32))
        for k in range(2):
            i_ref[at[k] : at[k] + 8, :] = diagonal[8 * k : 8 * k + 8]
        for n in range(NRHS):
            base = n * EXT
            for k in range(2):
                t_ref[base + at[k] : base + at[k] + 8, :] = joined(near[8 * k : 8 * k + 8, n * 128 : n * 128 + 128])
            t_ref[base + at[2] : base + at[2] + 8, :] = joined(unsqueeze(far[:8], n, TRACE_OFFSET[1 - side]))
            r_ref[base + at[0] : base + at[0] + 8, :] = joined(part(message, XH, n, 3))
            r_ref[base + at[1] : base + at[1] + 8, :] = joined(unsqueeze(far[8:], n, VALUE_OFFSET[1 - side]))
    apply(EARLY, False, (w, wx), t_ref, x_ref, a_ref)
    r_ref[...] = r_ref[...] - a_ref[:SPAN, :]


def smooth(guess, w, wx, wy, coefficients, y_low, y_high, t_in, r_in, i_in, smoothed, t_ref, r_ref, i_ref, x_ref, a_ref):
    t_ref[...] = t_in[...]
    r_ref[...] = r_in[...]
    i_ref[...] = i_in[...]
    a_ref[:SPAN, :] = jnp.zeros((SPAN, 128), F32)
    for side, message in enumerate((y_low, y_high)):
        column = [16 + (8 + k if side else 15 - k) for k in range(3)]
        diagonal = reciprocal(message[:, YE : YE + 128].astype(F32))
        near = message[:, YD : YD + 768].astype(F32)
        far = message[:, YG : YG + 768].astype(F32)
        for k in range(2):
            i_ref[pl.ds(column[k], 8, stride=16), :] = diagonal[8 * k : 8 * k + 8]
        for n in range(NRHS):
            lanes = slice(n * 128, n * 128 + 128)
            for k, value in enumerate((near[:8, lanes], near[8:, lanes], far[:8, lanes])):
                t_ref[pl.ds(n * EXT + column[k], 8, stride=16), :] = joined(value)
            for k, value in enumerate((far[8:, lanes], part(message, YR, n, 3))):
                r_ref[pl.ds(n * EXT + column[k], 8, stride=16), :] = joined(value)
    tables = (w, wx, wy)
    centre, half_width, first, second, third = [coefficients[i : i + 1, 0:64] for i in range(5)]

    def put_traces(parts, start):
        rows = parts[0].shape[0]
        traces = with_traces(jnp.concatenate(parts, 0))
        for n in range(NRHS):
            t_ref[n * EXT + start : n * EXT + start + rows, :] = traces[n * rows : n * rows + rows]

    apply(LATE, False, tables, t_ref, x_ref, a_ref)
    inverse = i_ref[16:144, 0:64]
    residues, updates = [], []
    for n in range(NRHS):
        rows = slice(n * EXT + 16, n * EXT + 144)
        r = r_ref[rows, 0:64] - a_ref[rows, 0:64]
        residues.append(r[16:112])
        updates.append(inverse * r / centre)
    put_traces(updates, 16)
    apply(SECOND, True, tables, t_ref, x_ref, a_ref)
    inverse = i_ref[32:128, 0:64]
    lasts = []
    for n in range(NRHS):
        residues[n] = residues[n] - a_ref[n * EXT + 32 : n * EXT + 128, 0:64]
        updates[n] = updates[n][16:112]
        lasts.append(second * first * updates[n] + (2.0 * second / half_width) * inverse * residues[n])
    put_traces(lasts, 32)
    apply(THIRD, True, tables, t_ref, x_ref, a_ref)
    for n in range(NRHS):
        for ix in range(EX):
            row, place = n * EXT + (ix + 3) * 16, slice(ix * 8, ix * 8 + 8)
            own = slice(ix * 16 + 16, ix * 16 + 24)
            residue = residues[n][own] - a_ref[row : row + 8, 0:64]
            update = third * second * lasts[n][own] + (2.0 * third / half_width) * inverse[own] * residue
            smoothed[n, place, :] = guess[n, place, :] + updates[n][own] + lasts[n][own] + update


def ghost_rows(message, start, out):
    lane = iota((8, 128), 1)
    for j in range(8):
        both = part(message, start, j, 4)
        other = pltpu.roll(both, 64, 1)
        out[pl.ds(2 * j, 8, stride=16), :] = jnp.where(lane < 64, both, other)
        out[pl.ds(2 * j + 1, 8, stride=16), :] = jnp.where(lane < 64, other, both)


def label_masks(masks):
    lane = iota((16, 256), 1)
    for b in range(4):
        masks[b * 16 : b * 16 + 16, :] = onehot(lane // 64 == b)


def mask_of(masks, label):
    return masks[pl.ds(pl.multiple_of(label * 16, 16), 16), :]


def times(piece, mask):
    return jnp.concatenate([piece, piece], 1) * jnp.concatenate([mask] * 4, 0)


def masked(masks, piece, label):
    return times(piece, mask_of(masks, label))


def face_column(f, rows):
    return jnp.concatenate([none(64 + 16 * f), rows] + ([none(48 - 16 * f)] if f < 3 else []), 0)


ROWS_EARLY = 3


def galerkin(late, before_local, labels, t16, plus_y, minus_y, w, local, edge_column, edge_columns, tt, masks, big):
    first_row, last_row = (ROWS_EARLY, EX) if late else (0, ROWS_EARLY)
    rows = last_row - first_row
    label_masks(masks)
    lane128 = iota((64, 128), 1)
    for pair in range(4 * rows):
        e = 8 * first_row + 2 * pair
        turned = t16[e * 64 : e * 64 + 128, :].astype(F32).T[:64]
        first, second = labels[0, e], labels[0, e + 1]
        for a in range(4):
            keep = jnp.where(
                lane128 < 64,
                jnp.where(first == a, 1.0, 0.0),
                jnp.where(second == a, 1.0, 0.0),
            )
            tt[a * 64 : a * 64 + 64, pair * 128 : pair * 128 + 128] = (turned * keep).astype(BF16)
    edge_column[...] = tt[:, 512 * rows - 512 :] if late else tt[:, :512]
    for f in range(2):
        for i in range(rows):
            start = (4 * i + 3 * f) * 128
            edge_columns[f, :, i * 128 : i * 128 + 128] = tt[:, start : start + 128]

    def row_of_elements(ix, carry):
        for iy in range(EY):
            e = ix * EY + iy
            own = pl.ds(pl.multiple_of(e * 64, 64), 64)
            here = pl.ds(pl.multiple_of((e - 8 * first_row) * 64, 64), 64)
            before = pl.multiple_of(jnp.maximum(e - 8, 0) * 64, 64)
            after = pl.multiple_of(jnp.minimum(e + 8, 31) * 64, 64)
            rows = [
                t16[pl.ds(before + 48, 16), :],
                t16[pl.ds(after, 16), :],
            ]
            if iy > 0:
                rows.append(plus_y[pl.ds(pl.multiple_of((e - 1) * 16, 16), 16), :])
            else:
                rows.append(none(16))
            if iy < 7:
                rows.append(minus_y[pl.ds(pl.multiple_of((e + 1) * 16, 16), 16), :])
            columns = [jnp.concatenate([t16[own, :], none(64)], 0)]
            columns += [face_column(f, value) for f, value in enumerate(rows)]
            pieces = dot(w[own, :], jnp.concatenate(columns, 1)).astype(BF16)
            piece = lambda s: pieces[:, s * 128 : s * 128 + 128]
            big[0, here, :] = masked(masks, piece(0), labels[0, e])
            big[1, here, :] = masked(masks, piece(1), labels[0, jnp.maximum(e - 8, 0)])
            big[2, here, :] = masked(masks, piece(2), labels[0, jnp.minimum(e + 8, 31)])
            nothing = jnp.zeros((64, 256), BF16)
            big[3, here, :] = masked(masks, piece(3), labels[0, e - 1]) if iy > 0 else nothing
            big[4, here, :] = masked(masks, piece(4), labels[0, e + 1]) if iy < 7 else nothing
        return carry

    lax.fori_loop(first_row, last_row, row_of_elements, 0)
    total = dot(tt[...], big[0]) + dot(tt[...], big[3]) + dot(tt[...], big[4])
    if late:
        total = before_local[...] + total + dot(tt[...], big[1])
        if rows > 1:
            total = total + dot(tt[:, : 512 * rows - 512], big[2, : 512 * rows - 512, :])
    else:
        total = total + dot(tt[...], big[2])
        if rows > 1:
            total = total + dot(tt[:, 512:], big[1, 512:, :])
    local[...] = total


def ghost_block(face, message, start, first_row, elements, mask, w, columns, rows, side, result):
    ghost_rows(message, start, rows)
    for i, (e, place) in enumerate(elements):
        near = rows[(i + first_row) * 16 : (i + first_row) * 16 + 16, :].astype(BF16)
        piece = dot(w[e * 64 : e * 64 + 64, :], face_column(face, near)).astype(BF16)
        side[place : place + 64, :] = times(piece, mask(i))
    total, start = 0.0, 0
    for c in columns:
        width = c.shape[-1]
        total = total + dot(c[...], side[start : start + width, :])
        start += width
    result[...] = total


def x_wait_kernel(labels_in, blocks, faces, tent, w, t16, plus_y, minus_y, local, column, columns, _,
                  stage, fstage, w32, tt, masks, big, labels, label_sem):
    fetch = pltpu.make_async_copy(labels_in, labels, label_sem.at[0])
    fetch.start()
    own_operators(blocks, faces, w, stage, fstage, w32)
    prolongator(tent, t16, plus_y, minus_y, fstage, w32)
    fetch.wait()
    galerkin(0, None, labels, t16, plus_y, minus_y, w, local, column, columns, tt, masks, big)


def y_wait_kernel(labels_in, t16, plus_y, minus_y, w, before_local, column0, x_low, x_high, guess, b, diagonal,
                  local, columns, wx, mask_rows, t_ref, r_ref, i_ref, coefficients, ghost, _,
                  stage, fstage, w32, x_ref, a_ref, rows, masks, side, result, sems, column1, tt, big, labels, label_sem):
    fetch = pltpu.make_async_copy(labels_in, labels, label_sem.at[0])
    fetch.start()
    coefficients[...] = b[192:200, :]
    halo_x(x_low, x_high, wx, stage, fstage, w32)
    fetch.wait()
    galerkin(1, before_local, labels, t16, plus_y, minus_y, w, local, column1, columns, tt, masks, big)
    copies = []
    for f, (message, column) in enumerate(((x_low, column0), (x_high, column1))):
        elements = [(24 * f + iy, iy * 64) for iy in range(EY)]
        mask = lambda i: mask_of(masks, labels[1, 8 * f + i])
        ghost_block(f, message, XT, 0, elements, mask, w, (column,), rows, side, result.at[f])
        copies.append(pltpu.make_async_copy(result.at[f], ghost.at[f], sems.at[f]))
        copies[-1].start()
    for i in range(8):
        mask_rows[i * 16 : i * 16 + 16, :] = mask_of(masks, labels[1, 16 + i])
    start_smoothing(guess, b, diagonal, w, wx, x_low, x_high, t_ref, r_ref, i_ref, x_ref, a_ref)
    for copy in copies:
        copy.wait()


def finish_kernel(mask_rows, guess, w, wx, coefficients, y_odd, y_even, columns0, columns1, t_in, r_in, i_in, ghost_in,
                  smoothed, ghost, wy, y_low, y_high, stage, fstage, w32, t_ref, r_ref, i_ref, x_ref, a_ref,
                  rows, side, result, sems):
    halo_y(y_even, y_odd, wy, y_low, y_high, stage, fstage, w32)
    copies = []
    for f, message in enumerate((y_low, y_high)):
        side[...] = jnp.zeros((512, 256), BF16)
        elements = [(8 * ix + 7 * f, ix * 128 + 64 * f) for ix in range(EX)]
        columns = (columns0.at[f], columns1.at[f])
        mask = lambda i: mask_rows[(4 * f + i) * 16 : (4 * f + i) * 16 + 16, :]
        ghost_block(2 + f, message, YT, 2, elements, mask, w, columns, rows, side, result.at[f])
        copies.append(pltpu.make_async_copy(result.at[f], ghost.at[2 + f], sems.at[f]))
        copies[-1].start()
    smooth(guess, w, wx, wy, coefficients, y_low, y_high, t_in, r_in, i_in, smoothed, t_ref, r_ref, i_ref, x_ref, a_ref)
    for copy in copies:
        copy.wait()


def call(kernel, outs, scratch, operands, flops, moved, in_specs=None, out_specs=None, aliases=None, room=48):
    return pl.pallas_call(
        kernel,
        out_shape=outs,
        in_specs=in_specs or [VMEM] * len(operands),
        out_specs=out_specs or [VMEM] * len(outs),
        scratch_shapes=scratch,
        input_output_aliases=aliases or {},
        cost_estimate=pl.CostEstimate(flops=flops, bytes_accessed=moved, transcendentals=0),
        compiler_params=pltpu.CompilerParams(vmem_limit_bytes=room * 1024 * 1024),
    )(*operands)


def exchange(messages, axis, firsts):
    out = []
    for first, message in zip(firsts, messages):
        pairs = []
        for i in range(first, lax.axis_size(axis) - 1, 2):
            pairs += [(i, i + 1), (i + 1, i)]
        out.append(lax.ppermute(message, axis, pairs))
    return out


def shaped(*shape, dtype=BF16):
    return jax.ShapeDtypeStruct(shape, dtype)


STAGES = [pltpu.VMEM((4, 256, 128), F32), pltpu.VMEM((4, 256, 128), F32), pltpu.VMEM((2048, 128), F32)]


GHOST = [
    pltpu.VMEM((128, 128), F32),
    pltpu.VMEM((64, 256), BF16),
    pltpu.VMEM((512, 256), BF16),
    pltpu.VMEM((2, 256, 256), F32),
    pltpu.SemaphoreType.DMA((2,)),
]


def on_device(blocks, faces, tentative, aggregate, ghost_labels, rhs, guess, bounds):
    wide = lambda *shape: shaped(*shape, dtype=F32)
    rhs = jnp.swapaxes(rhs[0, 0], 1, 2)
    guess = jnp.swapaxes(guess[0, 0], 1, 2)
    blocks, faces, tentative = [a.reshape(NE, 4096) for a in (blocks, faces, tentative)]
    even, odd, traces_packed, b_packed, b, diagonal, labels = call(
        pack_x_kernel,
        [shaped(16, XLEN)] * 2 + [shaped(NE, 768)] * 2 + [wide(NRHS * NE + 8, 64), shaped(NE, 128), shaped(8, 128, dtype=jnp.int32)],
        [pltpu.VMEM((NE, 4096), BF16)] * 3 + [pltpu.VMEM((NRHS, NE, 64), F32)] * 2
        + [pltpu.VMEM((1, 2), F32), pltpu.VMEM((1, NE), jnp.int32), pltpu.VMEM((1, 24), jnp.int32)]
        + [STAGES[0], STAGES[2], pltpu.VMEM((2048, 128), BF16)] + [pltpu.VMEM((256, 128), F32)] * 2
        + [pltpu.SemaphoreType.DMA((8,))],
        (blocks, faces, tentative, guess, rhs, bounds.reshape(1, 2), aggregate.reshape(1, NE), ghost_labels.reshape(1, 24)),
        10**6, 2**20, [HBM] * 8, room=62,
    )
    even, odd = exchange((even, odd), "bx", (0, 1))
    def part_of(rows):
        outs = [wide(256, 256), shaped(256, 512), shaped(2, 256, 128 * rows)]
        return outs, [pltpu.VMEM((256, 512 * rows), BF16), GHOST[1], pltpu.VMEM((5, 512 * rows, 256), BF16)]

    early, early_scratch = part_of(ROWS_EARLY)
    late, late_scratch = part_of(EX - ROWS_EARLY)
    scalars = [pltpu.SMEM((8, 128), jnp.int32), pltpu.SemaphoreType.DMA((1,))]
    passed = shaped(8, 128, dtype=jnp.int32)
    w, t16, plus_y, minus_y, local, column0, columns0, labels = call(
        x_wait_kernel,
        [shaped(2048, 128), shaped(2048, 128), shaped(512, 128), shaped(512, 128)] + early + [passed],
        STAGES + early_scratch + scalars,
        (labels, blocks, faces, tentative), 4 * 10**9, 2**22, [HBM] + [VMEM] * 3, [VMEM] * 7 + [HBM], {0: 7},
    )
    odd, even, x_low, x_high = call(
        pack_y_kernel, [shaped(16, YLEN)] * 2 + [shaped(16, XLEN)] * 2, [],
        (blocks, faces, tentative, traces_packed, b_packed, diagonal, even, odd, column0), 10**8, 2**20,
        [VMEM] * 8 + [ANY],
    )
    odd, even = exchange((odd, even), "by", (1, 0))
    extended = [wide(SPAN, 128)] * 2 + [wide(EXT, 128)]
    fields = [pltpu.VMEM(a.shape, F32) for a in extended]
    pads = [pltpu.VMEM((8 * EXT, 128), F32)] * 2
    local, columns1, wx, mask_rows, traces, residue, inverses, coefficients, ghost, _ = call(
        y_wait_kernel,
        [late[0], late[2], shaped(2048, 128), shaped(128, 256)] + extended + [wide(8, 64), wide(4, 256, 256), passed],
        STAGES + pads + GHOST + [pltpu.VMEM((256, 512), BF16), late_scratch[0], late_scratch[2]] + scalars,
        (labels, t16, plus_y, minus_y, w, local, column0, x_low, x_high, guess, b, diagonal), 4 * 10**9, 2**22,
        [HBM] + [VMEM] * 11, [VMEM] * 8 + [HBM] * 2, {0: 9},
    )
    smoothed, ghost = call(
        finish_kernel, [wide(NRHS, NE, 64), wide(4, 256, 256)],
        [pltpu.VMEM((2048, 128), BF16)] + [pltpu.VMEM((16, YLEN), BF16)] * 2 + STAGES + fields + pads + GHOST[:1] + GHOST[2:],
        (mask_rows, guess, w, wx, coefficients, odd, even, columns0, columns1, traces, residue, inverses, ghost),
        10**9, 2**20, [VMEM] * 12 + [HBM], [VMEM, HBM], {12: 1},
    )
    return jnp.swapaxes(smoothed, 1, 2)[None, None], local[None, None], ghost[None, None]


def solution(mesh):
    b = lambda extra: P("bx", "by", *([None] * extra))
    return jax.shard_map(
        on_device,
        mesh=mesh,
        in_specs=(b(2), b(2), b(2), b(1), b(1), b(3), b(3), P()),
        out_specs=(b(3), b(2), b(3)),
        check_vma=False,
    )
```
